32 devices in a mesh: lon: 8 (over z, y), ch: 4 (over x, core).
Axes of the slice: x: 2, y: 2, z: 4, core: 2. Of those that a mesh axis runs over, the one named last changes fastest.
Arguments:
- features: bfloat16 [1024, 1, 144, 128], P('ch', None, 'lon'), may hold values from -6 to 6
- cotangent: bfloat16 [3, 256, 1, 144, 128], P(None, 'ch', None, 'lon'), may hold values from -6 to 6
- weights: bfloat16 [3, 3, 3, 256, 1024], P(None, None, None, 'ch'), may hold values from -0.0625 to 0.0625
Outputs:
- input_grad: bfloat16 [1024, 1, 144, 128], P('ch', None, 'lon')
- kernel_grad: float32 [3, 3, 3, 256, 1024], P(None, None, None, 'ch')
The draws below stay inside these ranges and needn't reach their ends.
All inputs are finite; a program needn't handle non-finite values.
Results may differ from the reference program's by a relative error of at most 0.001.
Values may be sent and summed in bfloat16 or wider, within the bound.
No kernel may reach another device: no remote copies, remote signals or barrier semaphores. Data moves between devices by JAX's collectives and lax.ppermute only.
A program may use at most 256 MiB of HBM per device.

```python
import jax
import jax.numpy as jnp

IN_CH = 1024
OUT_CH = 256
BATCH = 1
ROWS = 128
LON = 144


def block_levels(own_key, dims, shards, least, largest):
    def one(axis_at, shards_of):
        draws = jax.random.uniform(jax.random.fold_in(jax.random.fold_in(own_key, 6), axis_at), (shards_of,), jnp.float32, least / len(shards), largest / len(shards))
        return jnp.repeat(jnp.exp(draws), dims[axis_at] // shards_of).reshape((-1,) + (1,) * (len(dims) - axis_at - 1))

    level = one(*shards[0])
    for cut in shards[1:]:
        level = level * one(*cut)
    return level


def normal_values(own_key, extent, width, bound, cuts=(), held_as=jnp.bfloat16):
    values = width * jax.random.normal(own_key, extent, jnp.float32)
    if cuts:
        values = values * block_levels(own_key, extent, cuts, -0.22, 0.18)
    return jnp.clip(values, -bound, bound).astype(held_as)


def setup_inputs(seed: int = 0) -> dict:
    key_of = jax.random.split(jax.random.key(seed), 4)
    return {
        "features": normal_values(key_of[0], (IN_CH, BATCH, LON, ROWS), 1.0, 6.0, ((0, 4), (2, 8))),
        "cotangent": normal_values(key_of[1], (3, OUT_CH, BATCH, LON, ROWS), 1.0, 6.0, ((1, 4), (3, 8))),
        "weights": normal_values(key_of[2], (3, 3, 3, OUT_CH, IN_CH), (9 * IN_CH) ** -0.5, 0.0625, ((3, 4),)),
    }


DILATIONS = (6, 12, 18)

def reference(features, cotangent, weights):
    feat = features.astype(jnp.float32)
    grads = cotangent.astype(jnp.float32)
    kernels = weights.astype(jnp.float32)
    cells = BATCH * LON * ROWS
    input_sum = jnp.zeros((IN_CH, cells), jnp.float32)
    kernel_list = []
    for branch in range(3):
        dilation = DILATIONS[branch]
        grad_here = grads[branch]
        grad_pad = jnp.pad(grad_here, ((0, 0), (0, 0), (0, 0), (dilation, dilation)))
        feat_pad = jnp.pad(feat, ((0, 0), (0, 0), (0, 0), (dilation, dilation)))
        flat_grad = grad_here.reshape(OUT_CH, cells)
        for lat_tap in range(3):
            for lon_tap in range(3):
                lat_off = dilation * (lat_tap - 1)
                lon_off = dilation * (lon_tap - 1)
                shifted = jnp.roll(feat_pad, -lon_off, axis=2)[:, :, :, dilation + lat_off:dilation + lat_off + ROWS]
                kernel_list.append(jnp.dot(flat_grad, shifted.reshape(IN_CH, cells).T, preferred_element_type=jnp.float32))
                moved = jnp.roll(grad_pad, lon_off, axis=2)[:, :, :, dilation - lat_off:dilation - lat_off + ROWS]
                input_sum = input_sum + jnp.dot(kernels[branch, lat_tap, lon_tap].T, moved.reshape(OUT_CH, cells), preferred_element_type=jnp.float32)
    kernel_grad = jnp.stack(kernel_list).reshape(3, 3, 3, OUT_CH, IN_CH) / jnp.sqrt(jnp.float32(cells))
    input_grad = input_sum.reshape(IN_CH, BATCH, LON, ROWS).astype(jnp.bfloat16)
    return (input_grad, kernel_grad)
```

```python
import functools

import jax
import jax.numpy as jnp
from jax import lax
from jax.experimental import pallas as pl
from jax.experimental.pallas import tpu as pltpu
from jax.sharding import PartitionSpec as P

DILATIONS = (6, 12, 18)
TAPS = 9
GROUP = 8
VMEM = 40 * 1024 * 1024


def ring_order(count):
    return list(range(0, count, 2)) + list(range(count - 1, 0, -2))


def ring_position(index, count):
    return jnp.where(index % 2 == 0, index // 2, count - 1 - index // 2)


def encode(value, scale):
    power = value * scale
    power = power * power
    power = power * power
    power = power * power
    return jnp.where(value < 0, -power, power).astype(jnp.bfloat16)


def decode(code, unit):
    wide = code.astype(jnp.float32)
    root = jnp.exp2(0.125 * jnp.log2(jnp.abs(wide))) * unit
    return jnp.where(wide < 0, -root, root)


def spread_kernel(cot_ref, left_ref, right_ref, out_ref):
    branch_at = pl.program_id(0)
    cols, chans, rows = cot_ref.shape[1:]
    lane = lax.broadcasted_iota(jnp.int32, (chans, rows), 1)
    start = 0
    for branch in range(3):
        dilation = DILATIONS[branch]

        @pl.when(branch_at == branch)
        def _(dilation=dilation, start=start):
            for place in range(-dilation, cols + dilation):
                if place < 0:
                    column = left_ref[start + place + dilation]
                elif place >= cols:
                    column = right_ref[start + place - cols]
                else:
                    column = cot_ref[0, place]
                wide = column.astype(jnp.float32)
                for lat_tap in range(3):
                    shift = dilation * (lat_tap - 1)
                    if shift == 0:
                        moved = column
                    else:
                        keep = lane >= shift if shift > 0 else lane < rows + shift
                        moved = jnp.where(keep, pltpu.roll(wide, shift % rows, 1), 0.0)
                        moved = moved.astype(jnp.bfloat16)
                    for lon_tap in range(3):
                        target = place + dilation * (lon_tap - 1)
                        if 0 <= target < cols:
                            tap = 3 * lat_tap + lon_tap
                            out_ref[
                                tap * chans : (tap + 1) * chans, target * rows : (target + 1) * rows
                            ] = moved

        start += dilation


def spread(cot, left, right):
    branches, cols, chans, rows = cot.shape
    return pl.pallas_call(
        spread_kernel,
        grid=(branches,),
        in_specs=[
            pl.BlockSpec((1, cols, chans, rows), lambda k: (k, 0, 0, 0)),
            pl.BlockSpec(left.shape, lambda k: (0, 0, 0)),
            pl.BlockSpec(right.shape, lambda k: (0, 0, 0)),
        ],
        out_specs=pl.BlockSpec((TAPS * chans, cols * rows), lambda k: (k, 0)),
        out_shape=jax.ShapeDtypeStruct((branches * TAPS * chans, cols * rows), jnp.bfloat16),
        compiler_params=pltpu.CompilerParams(vmem_limit_bytes=VMEM),
        cost_estimate=pl.CostEstimate(flops=0, bytes_accessed=20_000_000, transcendentals=0),
        name="spread",
    )(cot, left, right)


def kernel_terms_kernel(count, place_ref, grid_ref, first_ref, second_ref, out_ref, flat_ref):
    cols, block, rows = first_ref.shape
    chans = grid_ref.shape[0] // TAPS
    parts = count // GROUP
    height = chans // GROUP
    width = 2 * block // parts

    @pl.when(pl.program_id(0) == 0)
    def _():
        for ref, core in ((first_ref, place_ref[1]), (second_ref, 1 - place_ref[1])):
            at = pl.ds(pl.multiple_of(core * block, block), block)
            for col in range(cols):
                flat_ref[at, col * rows : (col + 1) * rows] = ref[col]

    sums = lax.dot_general(
        grid_ref[...], flat_ref[...], (((1,), (1,)), ((), ())), preferred_element_type=jnp.float32
    )
    for owner in range(count):
        at = lax.rem(owner - place_ref[0] + count, count)
        top = (owner % GROUP) * height
        side = (owner // GROUP) * width
        for tap in range(TAPS):
            low = tap * chans + top
            out_ref[at, tap] = sums[low : low + height, side : side + width]


def kernel_terms(place, grid, first, second, count):
    cols, block, rows = first.shape
    taps = 3 * TAPS
    chans = grid.shape[0] // taps
    parts = count // GROUP
    shape = (count, taps, chans // GROUP, 2 * block // parts)
    return pl.pallas_call(
        functools.partial(kernel_terms_kernel, count),
        grid_spec=pltpu.PrefetchScalarGridSpec(
            num_scalar_prefetch=1,
            grid=(3,),
            in_specs=[
                pl.BlockSpec((TAPS * chans, cols * rows), lambda k, s: (k, 0)),
                pl.BlockSpec(first.shape, lambda k, s: (0, 0, 0)),
                pl.BlockSpec(second.shape, lambda k, s: (0, 0, 0)),
            ],
            out_specs=pl.BlockSpec((count, TAPS) + shape[2:], lambda k, s: (0, k, 0, 0)),
            scratch_shapes=[pltpu.VMEM((2 * block, cols * rows), jnp.bfloat16)],
        ),
        out_shape=jax.ShapeDtypeStruct(shape, jnp.float32),
        compiler_params=pltpu.CompilerParams(vmem_limit_bytes=VMEM),
        cost_estimate=pl.CostEstimate(
            flops=4 * taps * chans * block * cols * rows, bytes_accessed=16_000_000, transcendentals=0
        ),
        name="kernel_terms",
    )(place, grid, first, second)


def input_terms_kernel(place_ref, weight_ref, grid_ref, *refs):
    out_ref = refs[-1]
    cols, block, rows = out_ref.shape
    sums = jnp.dot(weight_ref[...], grid_ref[...], preferred_element_type=jnp.float32)
    for col in range(cols):
        part = sums[:, col * rows : (col + 1) * rows]
        if len(refs) == 2:
            part = part + refs[0][col]
        out_ref[col] = part


def input_terms(place, weight_rows, grid, block, cols, rows, added=None):
    steps = 3
    depth = weight_rows.shape[1]
    wide = pl.BlockSpec((cols // steps, block, rows), lambda t, s: (t, 0, 0))
    operands = [weight_rows, grid] + ([] if added is None else [added])
    return pl.pallas_call(
        input_terms_kernel,
        grid_spec=pltpu.PrefetchScalarGridSpec(
            num_scalar_prefetch=1,
            grid=(steps,),
            in_specs=[
                pl.BlockSpec((block, depth), lambda t, s: (s[0], 0)),
                pl.BlockSpec((depth, cols * rows // steps), lambda t, s: (0, t)),
            ]
            + ([] if added is None else [wide]),
            out_specs=wide,
        ),
        out_shape=jax.ShapeDtypeStruct((cols, block, rows), jnp.float32),
        compiler_params=pltpu.CompilerParams(vmem_limit_bytes=VMEM),
        cost_estimate=pl.CostEstimate(
            flops=2 * block * depth * cols * rows, bytes_accessed=12_000_000, transcendentals=0
        ),
        name="input_terms",
    )(place, *operands)


def unfold_kernel(count, place_ref, unit_ref, *refs):
    out_ref = refs[-1]
    height, width = refs[0].shape[1:]
    for ahead in range(count):
        owner = lax.rem(place_ref[0] + ahead, count)
        top = pl.multiple_of(lax.rem(owner, GROUP) * height, height)
        side = pl.multiple_of(lax.div(owner, GROUP) * width, width)
        out_ref[:, pl.ds(top, height), pl.ds(side, width)] = decode(refs[ahead][...], unit_ref[0])


def unfold(place, unit, codes, total, before=None):
    count = len(codes)
    taps, height, width = codes[0].shape
    rows, side = height * GROUP, width * (count // GROUP)
    out_shape = jax.ShapeDtypeStruct((taps, rows, total), jnp.float32)
    operands = [unit] + codes + ([] if before is None else [before])
    return pl.pallas_call(
        functools.partial(unfold_kernel, count),
        grid_spec=pltpu.PrefetchScalarGridSpec(
            num_scalar_prefetch=1,
            grid=(3,),
            in_specs=[pl.BlockSpec(memory_space=pltpu.SMEM)]
            + [pl.BlockSpec((TAPS, height, width), lambda k, s: (k, 0, 0))] * count
            + ([] if before is None else [pl.BlockSpec(memory_space=pl.ANY)]),
            out_specs=pl.BlockSpec((TAPS, rows, side), lambda k, s: (k, 0, s[1])),
        ),
        out_shape=out_shape,
        input_output_aliases={} if before is None else {len(operands): 0},
        compiler_params=pltpu.CompilerParams(vmem_limit_bytes=VMEM),
        name="unfold",
    )(place, *operands)


def ring_sum(terms, scale, unit):
    count, taps = terms.shape[:2]
    order = ring_order(count)
    ahead = [(order[i], order[(i + 1) % count]) for i in range(count)]
    behind = [(b, a) for a, b in ahead]
    half = count // 2
    cut = (taps + 1) // 2
    up = encode(terms[half, :cut], scale)
    down = encode(terms[half, cut:], scale)
    for left in range(half, 0, -1):
        up = decode(lax.ppermute(up, "lon", ahead), unit)
        down = decode(lax.ppermute(down, "lon", behind), unit)
        if left == 1:
            break
        to_up = terms[left - 1]
        to_down = terms[count - left + 1]
        if left == half:
            up = jnp.concatenate([to_up[:cut] + up, to_up[cut:]], axis=0)
            down = jnp.concatenate([to_down[:cut], to_down[cut:] + down], axis=0)
        else:
            up = to_up + up
            down = to_down + down
        up = encode(up, scale)
        down = encode(down, scale)
    own = encode(terms[0] + up + down, scale)
    codes = [own] + [None] * (count - 1)
    up = down = own
    for step in range(1, half):
        up = lax.ppermute(up, "lon", ahead)
        down = lax.ppermute(down, "lon", behind)
        codes[count - step] = up
        codes[step] = down
    codes[half] = jnp.concatenate(
        [lax.ppermute(up[:cut], "lon", ahead), lax.ppermute(down[cut:], "lon", behind)], axis=0
    )
    return codes


def local(features, cotangent, weights):
    block, _, cols, rows = features.shape
    chans = cotangent.shape[1]
    total = weights.shape[4]
    count = lax.axis_size("lon")
    cells = cols * count * rows
    lon = lax.axis_index("lon")
    ch = lax.axis_index("ch")
    place_x, place_core = ch // 2, ch % 2
    spot = ring_position(lon, count)

    feat = jnp.transpose(features.reshape(block, cols, rows), (1, 0, 2))
    cot = jnp.transpose(cotangent.reshape(3, chans, cols, rows), (0, 2, 1, 3))

    tails = jnp.concatenate([cot[k, cols - DILATIONS[k] :] for k in range(3)], axis=0)
    heads = jnp.concatenate([cot[k, : DILATIONS[k]] for k in range(3)], axis=0)
    left = lax.ppermute(tails, "lon", [(i, (i + 1) % count) for i in range(count)])
    right = lax.ppermute(heads, "lon", [((i + 1) % count, i) for i in range(count)])

    to_core = [(i, i ^ 1) for i in range(4)]
    to_x = [(i, i ^ 2) for i in range(4)]
    far = lax.ppermute(feat, "ch", to_x)
    near = lax.ppermute(feat, "ch", to_core)
    far_near = lax.ppermute(far, "ch", to_core)

    sizes = jnp.stack(
        [jnp.max(jnp.abs(feat)).astype(jnp.float32), jnp.max(jnp.abs(cot)).astype(jnp.float32)]
    )
    sizes = jnp.maximum(lax.pmax(sizes, ("lon", "ch")), 1e-15)
    bound = cells * sizes[0] * sizes[1]
    scale = 2.0**15.5 / bound
    unit = bound / 2.0**15.5
    unit_out = (unit / jnp.sqrt(jnp.float32(cells))).reshape(1)

    weight_rows = jnp.transpose(weights.reshape(-1, total))
    grid = spread(cot, left, right)

    place = jnp.stack([spot, place_core]).astype(jnp.int32)
    terms_near = kernel_terms(place, grid, feat, near, count)
    terms_far = kernel_terms(place, grid, far, far_near, count)

    def terms_of(x, core, added=None):
        at = (2 * x + core).astype(jnp.int32).reshape(1)
        return input_terms(at, weight_rows, grid, block, cols, rows, added)

    away = lax.ppermute(terms_of(1 - place_x, 1 - place_core), "ch", to_core)
    beside = lax.ppermute(terms_of(place_x, 1 - place_core), "ch", to_core)
    across = lax.ppermute(terms_of(1 - place_x, place_core, away), "ch", to_x)
    mine = terms_of(place_x, place_core)

    codes_near = ring_sum(terms_near, scale, unit)
    codes_far = ring_sum(terms_far, scale, unit)
    kernel_grad = unfold(
        jnp.stack([spot, place_x]).astype(jnp.int32), unit_out, codes_near, total
    )
    kernel_grad = unfold(
        jnp.stack([spot, 1 - place_x]).astype(jnp.int32), unit_out, codes_far, total, kernel_grad
    )
    input_grad = (mine + beside + across).astype(jnp.bfloat16)
    input_grad = jnp.transpose(input_grad, (1, 0, 2)).reshape(block, 1, cols, rows)
    return (input_grad, kernel_grad.reshape(3, 3, 3, chans, total))


def solution(mesh):
    return jax.shard_map(
        local,
        mesh=mesh,
        in_specs=(
            P("ch", None, "lon", None),
            P(None, "ch", None, "lon", None),
            P(None, None, None, "ch", None),
        ),
        out_specs=(P("ch", None, "lon", None), P(None, None, None, "ch", None)),
        check_vma=False,
    )
```

```python
import functools

import jax
import jax.numpy as jnp
from jax import lax
from jax.experimental import pallas as pl
from jax.experimental.pallas import tpu as pltpu
from jax.sharding import PartitionSpec as P

DILATIONS = (6, 12, 18)
TAPS = 9
GROUP = 8
REACH = 2.0**15.5
TINY = 1e-30
VMEM = 40 * 1024 * 1024


def ring_order(count):
    return list(range(0, count, 2)) + list(range(count - 1, 0, -2))


def ring_position(index, count):
    return jnp.where(index % 2 == 0, index // 2, count - 1 - index // 2)


def pack(value, bound):
    bound = lax.reduce_precision(bound * 1.01, 8, 7)
    power = value * (REACH / bound)
    power = power * power
    power = power * power
    power = power * power
    code = jnp.where(value < 0, -power, power).astype(jnp.bfloat16)
    return jnp.concatenate([code, bound.astype(jnp.bfloat16)], axis=0)


def decode(code, unit):
    wide = code.astype(jnp.float32)
    root = jnp.exp2(0.125 * jnp.log2(jnp.abs(wide))) * unit
    return jnp.where(wide < 0, -root, root)


def unpack(message):
    bound = message[-1:].astype(jnp.float32)
    return decode(message[:-1], bound * (1.0 / REACH)), bound


def spread_kernel(cot_ref, left_ref, right_ref, out_ref):
    branch_at = pl.program_id(0)
    cols, chans, rows = cot_ref.shape[1:]
    lane = lax.broadcasted_iota(jnp.int32, (chans, rows), 1)
    start = 0
    for branch in range(3):
        dilation = DILATIONS[branch]

        @pl.when(branch_at == branch)
        def _(dilation=dilation, start=start):
            for place in range(-dilation, cols + dilation):
                if place < 0:
                    column = left_ref[start + place + dilation]
                elif place >= cols:
                    column = right_ref[start + place - cols]
                else:
                    column = cot_ref[0, place]
                wide = column.astype(jnp.float32)
                for lat_tap in range(3):
                    shift = dilation * (lat_tap - 1)
                    if shift == 0:
                        moved = column
                    else:
                        keep = lane >= shift if shift > 0 else lane < rows + shift
                        moved = jnp.where(keep, pltpu.roll(wide, shift % rows, 1), 0.0)
                        moved = moved.astype(jnp.bfloat16)
                    for lon_tap in range(3):
                        target = place + dilation * (lon_tap - 1)
                        if 0 <= target < cols:
                            tap = 3 * lat_tap + lon_tap
                            out_ref[
                                tap * chans : (tap + 1) * chans, target * rows : (target + 1) * rows
                            ] = moved

        start += dilation


def spread(cot, left, right):
    branches, cols, chans, rows = cot.shape
    return pl.pallas_call(
        spread_kernel,
        grid=(branches,),
        in_specs=[
            pl.BlockSpec((1, cols, chans, rows), lambda k: (k, 0, 0, 0)),
            pl.BlockSpec(left.shape, lambda k: (0, 0, 0)),
            pl.BlockSpec(right.shape, lambda k: (0, 0, 0)),
        ],
        out_specs=pl.BlockSpec((TAPS * chans, cols * rows), lambda k: (k, 0)),
        out_shape=jax.ShapeDtypeStruct((branches * TAPS * chans, cols * rows), jnp.bfloat16),
        compiler_params=pltpu.CompilerParams(vmem_limit_bytes=VMEM),
        cost_estimate=pl.CostEstimate(flops=0, bytes_accessed=20_000_000, transcendentals=0),
        name="spread",
    )(cot, left, right)


def kernel_terms_kernel(count, place_ref, grid_ref, first_ref, second_ref, out_ref, top_ref, flat_ref):
    cols, block, rows = first_ref.shape
    chans = grid_ref.shape[0] // TAPS
    parts = count // GROUP
    height = chans // GROUP
    width = 2 * block // parts

    @pl.when(pl.program_id(0) == 0)
    def _():
        for ref, core in ((first_ref, place_ref[1]), (second_ref, 1 - place_ref[1])):
            at = pl.ds(pl.multiple_of(core * block, block), block)
            for col in range(cols):
                flat_ref[at, col * rows : (col + 1) * rows] = ref[col]

    sums = lax.dot_general(
        grid_ref[...], flat_ref[...], (((1,), (1,)), ((), ())), preferred_element_type=jnp.float32
    )
    largest = jnp.max(jnp.abs(sums))

    @pl.when(pl.program_id(0) == 0)
    def _():
        top_ref[...] = jnp.full(top_ref.shape, TINY, jnp.float32)

    top_ref[...] = jnp.maximum(top_ref[...], largest)
    for owner in range(count):
        at = lax.rem(owner - place_ref[0] + count, count)
        top = (owner % GROUP) * height
        side = (owner // GROUP) * width
        for tap in range(TAPS):
            low = tap * chans + top
            out_ref[at, tap] = sums[low : low + height, side : side + width]


def kernel_terms(place, grid, first, second, count):
    cols, block, rows = first.shape
    taps = 3 * TAPS
    chans = grid.shape[0] // taps
    parts = count // GROUP
    shape = (count, taps, chans // GROUP, 2 * block // parts)
    return pl.pallas_call(
        functools.partial(kernel_terms_kernel, count),
        grid_spec=pltpu.PrefetchScalarGridSpec(
            num_scalar_prefetch=1,
            grid=(3,),
            in_specs=[
                pl.BlockSpec((TAPS * chans, cols * rows), lambda k, s: (k, 0)),
                pl.BlockSpec(first.shape, lambda k, s: (0, 0, 0)),
                pl.BlockSpec(second.shape, lambda k, s: (0, 0, 0)),
            ],
            out_specs=[
                pl.BlockSpec((count, TAPS) + shape[2:], lambda k, s: (0, k, 0, 0)),
                pl.BlockSpec((1,) + shape[2:], lambda k, s: (0, 0, 0)),
            ],
            scratch_shapes=[pltpu.VMEM((2 * block, cols * rows), jnp.bfloat16)],
        ),
        out_shape=[
            jax.ShapeDtypeStruct(shape, jnp.float32),
            jax.ShapeDtypeStruct((1,) + shape[2:], jnp.float32),
        ],
        compiler_params=pltpu.CompilerParams(vmem_limit_bytes=VMEM),
        cost_estimate=pl.CostEstimate(
            flops=4 * taps * chans * block * cols * rows, bytes_accessed=16_000_000, transcendentals=0
        ),
        name="kernel_terms",
    )(place, grid, first, second)


def input_terms_kernel(place_ref, weight_ref, grid_ref, *refs):
    out_ref = refs[-1]
    cols, block, rows = out_ref.shape
    sums = jnp.dot(weight_ref[...], grid_ref[...], preferred_element_type=jnp.float32)
    for col in range(cols):
        part = sums[:, col * rows : (col + 1) * rows]
        if len(refs) == 2:
            part = part + refs[0][col]
        out_ref[col] = part


def input_terms(place, weight_rows, grid, block, cols, rows, added=None):
    steps = 3
    depth = weight_rows.shape[1]
    wide = pl.BlockSpec((cols // steps, block, rows), lambda t, s: (t, 0, 0))
    operands = [weight_rows, grid] + ([] if added is None else [added])
    return pl.pallas_call(
        input_terms_kernel,
        grid_spec=pltpu.PrefetchScalarGridSpec(
            num_scalar_prefetch=1,
            grid=(steps,),
            in_specs=[
                pl.BlockSpec((block, depth), lambda t, s: (s[0], 0)),
                pl.BlockSpec((depth, cols * rows // steps), lambda t, s: (0, t)),
            ]
            + ([] if added is None else [wide]),
            out_specs=wide,
        ),
        out_shape=jax.ShapeDtypeStruct((cols, block, rows), jnp.float32),
        compiler_params=pltpu.CompilerParams(vmem_limit_bytes=VMEM),
        cost_estimate=pl.CostEstimate(
            flops=2 * block * depth * cols * rows, bytes_accessed=12_000_000, transcendentals=0
        ),
        name="input_terms",
    )(place, *operands)


def unfold_kernel(count, norm, place_ref, *refs):
    out_ref = refs[-1]
    height, width = refs[0].shape[1:]
    for ahead in range(count):
        owner = lax.rem(place_ref[0] + ahead, count)
        top = pl.multiple_of(lax.rem(owner, GROUP) * height, height)
        side = pl.multiple_of(lax.div(owner, GROUP) * width, width)
        unit = refs[count + ahead][...].astype(jnp.float32) * norm
        out_ref[:, pl.ds(top, height), pl.ds(side, width)] = decode(refs[ahead][...], unit)


def unfold(place, norm, codes, total, before=None):
    count = len(codes)
    taps, height, width = codes[0].shape
    taps -= 1
    rows, side = height * GROUP, width * (count // GROUP)
    out_shape = jax.ShapeDtypeStruct((taps, rows, total), jnp.float32)
    operands = codes + codes + ([] if before is None else [before])
    return pl.pallas_call(
        functools.partial(unfold_kernel, count, norm),
        grid_spec=pltpu.PrefetchScalarGridSpec(
            num_scalar_prefetch=1,
            grid=(3,),
            in_specs=[pl.BlockSpec((TAPS, height, width), lambda k, s: (k, 0, 0))] * count
            + [pl.BlockSpec((1, height, width), lambda k, s: (taps, 0, 0))] * count
            + ([] if before is None else [pl.BlockSpec(memory_space=pl.ANY)]),
            out_specs=pl.BlockSpec((TAPS, rows, side), lambda k, s: (k, 0, s[1])),
        ),
        out_shape=out_shape,
        input_output_aliases={} if before is None else {len(operands): 0},
        compiler_params=pltpu.CompilerParams(vmem_limit_bytes=VMEM),
        cost_estimate=pl.CostEstimate(
            flops=0, bytes_accessed=10_000_000, transcendentals=2 * taps * rows * side
        ),
        name="unfold",
    )(place, *operands)


def ring_sum(terms, top):
    count, taps = terms.shape[:2]
    order = ring_order(count)
    ahead = [(order[i], order[(i + 1) % count]) for i in range(count)]
    behind = [(b, a) for a, b in ahead]
    half = count // 2
    cut = (taps + 1) // 2
    up = pack(terms[half, :cut], top)
    down = pack(terms[half, cut:], top)
    for left in range(half, 0, -1):
        up, up_bound = unpack(lax.ppermute(up, "lon", ahead))
        down, down_bound = unpack(lax.ppermute(down, "lon", behind))
        if left == 1:
            break
        to_up = terms[left - 1]
        to_down = terms[count - left + 1]
        if left == half:
            up = jnp.concatenate([to_up[:cut] + up, to_up[cut:]], axis=0)
            down = jnp.concatenate([to_down[:cut], to_down[cut:] + down], axis=0)
        else:
            up = to_up + up
            down = to_down + down
        up = pack(up, up_bound + top)
        down = pack(down, down_bound + top)
    own = pack(terms[0] + up + down, up_bound + down_bound + top)
    codes = [own] + [None] * (count - 1)
    up = down = own
    for step in range(1, half):
        up = lax.ppermute(up, "lon", ahead)
        down = lax.ppermute(down, "lon", behind)
        codes[count - step] = up
        codes[step] = down
    codes[half] = jnp.concatenate(
        [lax.ppermute(up[:cut], "lon", ahead), lax.ppermute(down[cut:], "lon", behind)], axis=0
    )
    return codes


def local(features, cotangent, weights):
    block, _, cols, rows = features.shape
    chans = cotangent.shape[1]
    total = weights.shape[4]
    count = lax.axis_size("lon")
    cells = cols * count * rows
    lon = lax.axis_index("lon")
    ch = lax.axis_index("ch")
    place_x, place_core = ch // 2, ch % 2
    spot = ring_position(lon, count)

    feat = jnp.transpose(features.reshape(block, cols, rows), (1, 0, 2))
    cot = jnp.transpose(cotangent.reshape(3, chans, cols, rows), (0, 2, 1, 3))

    tails = jnp.concatenate([cot[k, cols - DILATIONS[k] :] for k in range(3)], axis=0)
    heads = jnp.concatenate([cot[k, : DILATIONS[k]] for k in range(3)], axis=0)
    left = lax.ppermute(tails, "lon", [(i, (i + 1) % count) for i in range(count)])
    right = lax.ppermute(heads, "lon", [((i + 1) % count, i) for i in range(count)])

    to_core = [(i, i ^ 1) for i in range(4)]
    to_x = [(i, i ^ 2) for i in range(4)]
    far = lax.ppermute(feat, "ch", to_x)
    near = lax.ppermute(feat, "ch", to_core)
    far_near = lax.ppermute(far, "ch", to_core)

    norm = 1.0 / (REACH * cells**0.5)
    weight_rows = jnp.transpose(weights.reshape(-1, total))
    grid = spread(cot, left, right)

    place = jnp.stack([spot, place_core]).astype(jnp.int32)
    terms_near, top_near = kernel_terms(place, grid, feat, near, count)
    terms_far, top_far = kernel_terms(place, grid, far, far_near, count)

    def terms_of(x, core, added=None):
        at = (2 * x + core).astype(jnp.int32).reshape(1)
        return input_terms(at, weight_rows, grid, block, cols, rows, added)

    away = lax.ppermute(terms_of(1 - place_x, 1 - place_core), "ch", to_core)
    beside = lax.ppermute(terms_of(place_x, 1 - place_core), "ch", to_core)
    across = lax.ppermute(terms_of(1 - place_x, place_core, away), "ch", to_x)
    mine = terms_of(place_x, place_core)

    codes_near = ring_sum(terms_near, top_near)
    codes_far = ring_sum(terms_far, top_far)
    kernel_grad = unfold(
        jnp.stack([spot, place_x]).astype(jnp.int32), norm, codes_near, total
    )
    kernel_grad = unfold(
        jnp.stack([spot, 1 - place_x]).astype(jnp.int32), norm, codes_far, total, kernel_grad
    )
    input_grad = (mine + beside + across).astype(jnp.bfloat16)
    input_grad = jnp.transpose(input_grad, (1, 0, 2)).reshape(block, 1, cols, rows)
    return (input_grad, kernel_grad.reshape(3, 3, 3, chans, total))


def solution(mesh):
    return jax.shard_map(
        local,
        mesh=mesh,
        in_specs=(
            P("ch", None, "lon", None),
            P(None, "ch", None, "lon", None),
            P(None, None, None, "ch", None),
        ),
        out_specs=(P("ch", None, "lon", None), P(None, None, None, "ch", None)),
        check_vma=False,
    )
```

```python
import functools

import jax
import jax.numpy as jnp
from jax import lax
from jax.experimental import pallas as pl
from jax.experimental.pallas import tpu as pltpu
from jax.sharding import PartitionSpec as P

DILATIONS = (6, 12, 18)
TAPS = 9
GROUP = 8
REACH = 2.0**15.5
TINY = 1e-30
VMEM = 24 * 1024 * 1024


def ring_order(count):
    return list(range(0, count, 2)) + list(range(count - 1, 0, -2))


def ring_position(index, count):
    return jnp.where(index % 2 == 0, index // 2, count - 1 - index // 2)


def pack(value, bound):
    bound = lax.reduce_precision(bound * 1.01, 8, 7)
    power = value * (REACH / bound)
    power = power * power
    power = power * power
    power = power * power
    code = jnp.where(value < 0, -power, power).astype(jnp.bfloat16)
    return jnp.concatenate([code, bound.astype(jnp.bfloat16)], axis=0)


def decode(code, unit):
    wide = code.astype(jnp.float32)
    root = jnp.exp(0.125 * jnp.log(jnp.abs(wide))) * unit
    return jnp.where(wide < 0, -root, root)


def unpack(message):
    bound = message[-1:].astype(jnp.float32)
    return decode(message[:-1], bound * (1.0 / REACH)), bound


def spread_kernel(cot_ref, left_ref, right_ref, out_ref):
    branch_at = pl.program_id(0)
    cols, chans, rows = cot_ref.shape[1:]
    lane = lax.broadcasted_iota(jnp.int32, (chans, rows), 1)
    start = 0
    for branch in range(3):
        dilation = DILATIONS[branch]

        @pl.when(branch_at == branch)
        def _(dilation=dilation, start=start):
            for place in range(-dilation, cols + dilation):
                if place < 0:
                    column = left_ref[start + place + dilation]
                elif place >= cols:
                    column = right_ref[start + place - cols]
                else:
                    column = cot_ref[0, place]
                wide = column.astype(jnp.float32)
                for lat_tap in range(3):
                    shift = dilation * (lat_tap - 1)
                    if shift == 0:
                        moved = column
                    else:
                        keep = lane >= shift if shift > 0 else lane < rows + shift
                        moved = jnp.where(keep, pltpu.roll(wide, shift % rows, 1), 0.0)
                        moved = moved.astype(jnp.bfloat16)
                    for lon_tap in range(3):
                        target = place + dilation * (lon_tap - 1)
                        if 0 <= target < cols:
                            tap = 3 * lat_tap + lon_tap
                            out_ref[
                                tap * chans : (tap + 1) * chans, target * rows : (target + 1) * rows
                            ] = moved

        start += dilation


def spread(cot, left, right):
    branches, cols, chans, rows = cot.shape
    return pl.pallas_call(
        spread_kernel,
        grid=(branches,),
        in_specs=[
            pl.BlockSpec((1, cols, chans, rows), lambda k: (k, 0, 0, 0)),
            pl.BlockSpec(left.shape, lambda k: (0, 0, 0)),
            pl.BlockSpec(right.shape, lambda k: (0, 0, 0)),
        ],
        out_specs=pl.BlockSpec((TAPS * chans, cols * rows), lambda k: (k, 0)),
        out_shape=jax.ShapeDtypeStruct((branches * TAPS * chans, cols * rows), jnp.bfloat16),
        compiler_params=pltpu.CompilerParams(vmem_limit_bytes=VMEM),
        cost_estimate=pl.CostEstimate(flops=0, bytes_accessed=20_000_000, transcendentals=0),
        name="spread",
    )(cot, left, right)


def flatten_kernel(place_ref, first_ref, second_ref, out_ref):
    block = first_ref.shape[1]
    for ref, core in ((first_ref, place_ref[1]), (second_ref, 1 - place_ref[1])):
        at = pl.ds(pl.multiple_of(core * block, block), block)
        out_ref[:, at] = jnp.transpose(ref[0])


def flatten(place, first, second):
    cols, block, rows = first.shape
    return pl.pallas_call(
        flatten_kernel,
        grid_spec=pltpu.PrefetchScalarGridSpec(
            num_scalar_prefetch=1,
            grid=(cols,),
            in_specs=[pl.BlockSpec((1, block, rows), lambda k, s: (k, 0, 0))] * 2,
            out_specs=pl.BlockSpec((rows, 2 * block), lambda k, s: (k, 0)),
        ),
        out_shape=jax.ShapeDtypeStruct((cols * rows, 2 * block), jnp.bfloat16),
        compiler_params=pltpu.CompilerParams(vmem_limit_bytes=VMEM),
        cost_estimate=pl.CostEstimate(flops=0, bytes_accessed=10_000_000, transcendentals=0),
        name="flatten",
    )(place, first, second)


def kernel_terms_kernel(count, place_ref, grid_ref, feat_ref, out_ref, top_ref):
    chans = grid_ref.shape[0] // TAPS
    parts = count // GROUP
    height = chans // GROUP
    width = feat_ref.shape[1] // parts
    sums = jnp.dot(grid_ref[...], feat_ref[...], preferred_element_type=jnp.float32)
    largest = jnp.max(jnp.abs(sums))

    @pl.when(pl.program_id(0) == 0)
    def _():
        top_ref[...] = jnp.full(top_ref.shape, TINY, jnp.float32)

    top_ref[...] = jnp.maximum(top_ref[...], largest)
    for owner in range(count):
        at = lax.rem(owner - place_ref[0] + count, count)
        top = (owner % GROUP) * height
        side = (owner // GROUP) * width
        for tap in range(TAPS):
            low = tap * chans + top
            out_ref[at, tap] = sums[low : low + height, side : side + width]


def kernel_terms(place, grid, feat, count):
    depth, wide = feat.shape
    taps = 3 * TAPS
    chans = grid.shape[0] // taps
    shape = (count, taps, chans // GROUP, wide // (count // GROUP))
    return pl.pallas_call(
        functools.partial(kernel_terms_kernel, count),
        grid_spec=pltpu.PrefetchScalarGridSpec(
            num_scalar_prefetch=1,
            grid=(3,),
            in_specs=[
                pl.BlockSpec((TAPS * chans, depth), lambda k, s: (k, 0)),
                pl.BlockSpec((depth, wide), lambda k, s: (0, 0)),
            ],
            out_specs=[
                pl.BlockSpec((count, TAPS) + shape[2:], lambda k, s: (0, k, 0, 0)),
                pl.BlockSpec((1,) + shape[2:], lambda k, s: (0, 0, 0)),
            ],
        ),
        out_shape=[
            jax.ShapeDtypeStruct(shape, jnp.float32),
            jax.ShapeDtypeStruct((1,) + shape[2:], jnp.float32),
        ],
        compiler_params=pltpu.CompilerParams(vmem_limit_bytes=VMEM),
        cost_estimate=pl.CostEstimate(
            flops=2 * taps * chans * wide * depth, bytes_accessed=16_000_000, transcendentals=0
        ),
        name="kernel_terms",
    )(place, grid, feat)


def input_terms_kernel(place_ref, weight_ref, grid_ref, *refs):
    out_ref = refs[-1]
    cols, block, rows = out_ref.shape
    sums = jnp.dot(weight_ref[...], grid_ref[...], preferred_element_type=jnp.float32)
    for col in range(cols):
        part = sums[:, col * rows : (col + 1) * rows]
        if len(refs) == 2:
            part = part + refs[0][col]
        out_ref[col] = part


def input_terms(place, weight_rows, grid, block, cols, rows, added=None):
    steps = 3
    depth = weight_rows.shape[1]
    wide = pl.BlockSpec((cols // steps, block, rows), lambda t, s: (t, 0, 0))
    operands = [weight_rows, grid] + ([] if added is None else [added])
    return pl.pallas_call(
        input_terms_kernel,
        grid_spec=pltpu.PrefetchScalarGridSpec(
            num_scalar_prefetch=1,
            grid=(steps,),
            in_specs=[
                pl.BlockSpec((block, depth), lambda t, s: (s[0], 0)),
                pl.BlockSpec((depth, cols * rows // steps), lambda t, s: (0, t)),
            ]
            + ([] if added is None else [wide]),
            out_specs=wide,
        ),
        out_shape=jax.ShapeDtypeStruct((cols, block, rows), jnp.float32),
        compiler_params=pltpu.CompilerParams(vmem_limit_bytes=VMEM),
        cost_estimate=pl.CostEstimate(
            flops=2 * block * depth * cols * rows, bytes_accessed=12_000_000, transcendentals=0
        ),
        name="input_terms",
    )(place, *operands)


def unfold_kernel(count, norm, place_ref, *refs):
    out_ref = refs[-1]
    height, width = refs[0].shape[1:]
    for ahead in range(count):
        owner = lax.rem(place_ref[0] + ahead, count)
        top = pl.multiple_of(lax.rem(owner, GROUP) * height, height)
        side = pl.multiple_of(lax.div(owner, GROUP) * width, width)
        unit = refs[count + ahead][...].astype(jnp.float32) * norm
        out_ref[:, pl.ds(top, height), pl.ds(side, width)] = decode(refs[ahead][...], unit)


def unfold(place, norm, codes, total, before=None):
    count = len(codes)
    taps, height, width = codes[0].shape
    taps -= 1
    rows, side = height * GROUP, width * (count // GROUP)
    out_shape = jax.ShapeDtypeStruct((taps, rows, total), jnp.float32)
    operands = codes + codes + ([] if before is None else [before])
    return pl.pallas_call(
        functools.partial(unfold_kernel, count, norm),
        grid_spec=pltpu.PrefetchScalarGridSpec(
            num_scalar_prefetch=1,
            grid=(3,),
            in_specs=[pl.BlockSpec((TAPS, height, width), lambda k, s: (k, 0, 0))] * count
            + [pl.BlockSpec((1, height, width), lambda k, s: (taps, 0, 0))] * count
            + ([] if before is None else [pl.BlockSpec(memory_space=pl.ANY)]),
            out_specs=pl.BlockSpec((TAPS, rows, side), lambda k, s: (k, 0, s[1])),
        ),
        out_shape=out_shape,
        input_output_aliases={} if before is None else {len(operands): 0},
        compiler_params=pltpu.CompilerParams(vmem_limit_bytes=VMEM),
        cost_estimate=pl.CostEstimate(
            flops=0, bytes_accessed=10_000_000, transcendentals=2 * taps * rows * side
        ),
        name="unfold",
    )(place, *operands)


def ring_sum(terms, top):
    count, taps = terms.shape[:2]
    order = ring_order(count)
    ahead = [(order[i], order[(i + 1) % count]) for i in range(count)]
    behind = [(b, a) for a, b in ahead]
    half = count // 2
    cut = (taps + 1) // 2
    up = pack(terms[half, :cut], top)
    down = pack(terms[half, cut:], top)
    for left in range(half, 0, -1):
        up, up_bound = unpack(lax.ppermute(up, "lon", ahead))
        down, down_bound = unpack(lax.ppermute(down, "lon", behind))
        if left == 1:
            break
        to_up = terms[left - 1]
        to_down = terms[count - left + 1]
        if left == half:
            up = jnp.concatenate([to_up[:cut] + up, to_up[cut:]], axis=0)
            down = jnp.concatenate([to_down[:cut], to_down[cut:] + down], axis=0)
        else:
            up = to_up + up
            down = to_down + down
        up = pack(up, up_bound + top)
        down = pack(down, down_bound + top)
    own = pack(terms[0] + up + down, up_bound + down_bound + top)
    codes = [own] + [None] * (count - 1)
    up = down = own
    for step in range(1, half):
        up = lax.ppermute(up, "lon", ahead)
        down = lax.ppermute(down, "lon", behind)
        codes[count - step] = up
        codes[step] = down
    codes[half] = jnp.concatenate(
        [lax.ppermute(up[:cut], "lon", ahead), lax.ppermute(down[cut:], "lon", behind)], axis=0
    )
    return codes


def local(features, cotangent, weights):
    block, _, cols, rows = features.shape
    chans = cotangent.shape[1]
    total = weights.shape[4]
    count = lax.axis_size("lon")
    cells = cols * count * rows
    lon = lax.axis_index("lon")
    ch = lax.axis_index("ch")
    place_x, place_core = ch // 2, ch % 2
    spot = ring_position(lon, count)

    feat = jnp.transpose(features.reshape(block, cols, rows), (1, 0, 2))
    cot = jnp.transpose(cotangent.reshape(3, chans, cols, rows), (0, 2, 1, 3))

    tails = jnp.concatenate([cot[k, cols - DILATIONS[k] :] for k in range(3)], axis=0)
    heads = jnp.concatenate([cot[k, : DILATIONS[k]] for k in range(3)], axis=0)
    left = lax.ppermute(tails, "lon", [(i, (i + 1) % count) for i in range(count)])
    right = lax.ppermute(heads, "lon", [((i + 1) % count, i) for i in range(count)])

    to_core = [(i, i ^ 1) for i in range(4)]
    to_x = [(i, i ^ 2) for i in range(4)]
    far = lax.ppermute(feat, "ch", to_x)
    near = lax.ppermute(feat, "ch", to_core)
    far_near = lax.ppermute(far, "ch", to_core)

    norm = 1.0 / (REACH * cells**0.5)
    place = jnp.stack([spot, place_core]).astype(jnp.int32)
    weight_rows = jnp.transpose(weights.reshape(-1, total))
    flat_near = flatten(place, feat, near)
    left, right, weight_rows, flat_near = lax.optimization_barrier(
        (left, right, weight_rows, flat_near)
    )
    grid = spread(cot, left, right)

    def terms_of(grid, x, core, added=None):
        at = (2 * x + core).astype(jnp.int32).reshape(1)
        return input_terms(at, weight_rows, grid, block, cols, rows, added)

    terms_near, top_near = kernel_terms(place, grid, flat_near, count)
    grid, terms_near, top_near = lax.optimization_barrier((grid, terms_near, top_near))
    away = terms_of(grid, 1 - place_x, 1 - place_core)
    grid, away = lax.optimization_barrier((grid, away))
    away = lax.ppermute(away, "ch", to_core)
    terms_far, top_far = kernel_terms(place, grid, flatten(place, far, far_near), count)
    grid, terms_far, top_far = lax.optimization_barrier((grid, terms_far, top_far))
    across = terms_of(grid, 1 - place_x, place_core, away)
    grid, across = lax.optimization_barrier((grid, across))
    across = lax.ppermute(across, "ch", to_x)
    beside = lax.ppermute(terms_of(grid, place_x, 1 - place_core), "ch", to_core)
    mine = terms_of(grid, place_x, place_core)

    codes_near = ring_sum(terms_near, top_near)
    codes_far = ring_sum(terms_far, top_far)
    kernel_grad = unfold(
        jnp.stack([spot, place_x]).astype(jnp.int32), norm, codes_near, total
    )
    kernel_grad = unfold(
        jnp.stack([spot, 1 - place_x]).astype(jnp.int32), norm, codes_far, total, kernel_grad
    )
    input_grad = (mine + beside + across).astype(jnp.bfloat16)
    input_grad = jnp.transpose(input_grad, (1, 0, 2)).reshape(block, 1, cols, rows)
    return (input_grad, kernel_grad.reshape(3, 3, 3, chans, total))


def solution(mesh):
    return jax.shard_map(
        local,
        mesh=mesh,
        in_specs=(
            P("ch", None, "lon", None),
            P(None, "ch", None, "lon", None),
            P(None, None, None, "ch", None),
        ),
        out_specs=(P("ch", None, "lon", None), P(None, None, None, "ch", None)),
        check_vma=False,
    )
```

```python
import functools

import jax
import jax.numpy as jnp
from jax import lax
from jax.experimental import pallas as pl
from jax.experimental.pallas import tpu as pltpu
from jax.sharding import PartitionSpec as P

DILATIONS = (6, 12, 18)
TAPS = 9
GROUP = 8
REACH = 2.0**15.5
TINY = 1e-30
MIB = 1024 * 1024
GRANT = 20 * MIB
PACE = 3e8


def cost(micros):
    return pl.CostEstimate(flops=int(micros * PACE), bytes_accessed=0, transcendentals=0)


def in_hbm(value):
    return pltpu.with_memory_space_constraint(value, pltpu.HBM)


def ring_order(count):
    return list(range(0, count, 2)) + list(range(count - 1, 0, -2))


def ring_position(index, count):
    return jnp.where(index % 2 == 0, index // 2, count - 1 - index // 2)


def bound_code(bound):
    return (bound * 1.01).astype(jnp.bfloat16)


def encode(value, bound):
    power = value * (REACH / bound.astype(jnp.float32))
    power = power * power
    power = power * power
    power = power * power
    return jnp.where(value < 0, -power, power).astype(jnp.bfloat16)


def decode(code, bound, norm):
    wide = code.astype(jnp.float32)
    root = jnp.exp(0.125 * jnp.log(jnp.abs(wide))) * (bound.astype(jnp.float32) * norm)
    return jnp.where(wide < 0, -root, root)


def edge_kernel(cot_ref, tail_ref, head_ref):
    cols = cot_ref.shape[1]
    start = 0
    for branch in range(3):
        dilation = DILATIONS[branch]
        tail_ref[start : start + dilation] = cot_ref[branch, cols - dilation :]
        head_ref[start : start + dilation] = cot_ref[branch, :dilation]
        start += dilation


def edges(cot):
    shape = (sum(DILATIONS),) + cot.shape[2:]
    return pl.pallas_call(
        edge_kernel,
        out_shape=[jax.ShapeDtypeStruct(shape, cot.dtype)] * 2,
        compiler_params=pltpu.CompilerParams(vmem_limit_bytes=GRANT),
        cost_estimate=cost(1),
        name="edges",
    )(cot)


def spread_kernel(cot_ref, left_ref, right_ref, out_ref):
    branch_at = pl.program_id(0)
    cols, chans, rows = cot_ref.shape[1:]
    lane = lax.broadcasted_iota(jnp.int32, (chans, rows), 1)
    start = 0
    for branch in range(3):
        dilation = DILATIONS[branch]

        @pl.when(branch_at == branch)
        def _(dilation=dilation, start=start):
            for place in range(-dilation, cols + dilation):
                if place < 0:
                    column = left_ref[start + place + dilation]
                elif place >= cols:
                    column = right_ref[start + place - cols]
                else:
                    column = cot_ref[0, place]
                wide = column.astype(jnp.float32)
                for lat_tap in range(3):
                    shift = dilation * (lat_tap - 1)
                    if shift == 0:
                        moved = column
                    else:
                        keep = lane >= shift if shift > 0 else lane < rows + shift
                        moved = jnp.where(keep, pltpu.roll(wide, shift % rows, 1), 0.0)
                        moved = moved.astype(jnp.bfloat16)
                    for lon_tap in range(3):
                        target = place + dilation * (lon_tap - 1)
                        if 0 <= target < cols:
                            tap = 3 * lat_tap + lon_tap
                            out_ref[
                                tap * chans : (tap + 1) * chans, target * rows : (target + 1) * rows
                            ] = moved

        start += dilation


def spread(cot, left, right):
    branches, cols, chans, rows = cot.shape
    return pl.pallas_call(
        spread_kernel,
        grid=(branches,),
        in_specs=[
            pl.BlockSpec((1, cols, chans, rows), lambda k: (k, 0, 0, 0)),
            pl.BlockSpec(left.shape, lambda k: (0, 0, 0)),
            pl.BlockSpec(right.shape, lambda k: (0, 0, 0)),
        ],
        out_specs=pl.BlockSpec((TAPS * chans, cols * rows), lambda k: (k, 0)),
        out_shape=pltpu.HBM((branches * TAPS * chans, cols * rows), jnp.bfloat16),
        compiler_params=pltpu.CompilerParams(vmem_limit_bytes=GRANT),
        cost_estimate=cost(2.5),
        name="spread",
    )(cot, left, right)


def flatten_kernel(place_ref, first_ref, second_ref, out_ref):
    cols, block, rows = first_ref.shape
    for ref, core in ((first_ref, place_ref[1]), (second_ref, 1 - place_ref[1])):
        at = pl.ds(pl.multiple_of(core * block, block), block)
        for col in range(cols):
            out_ref[col * rows : (col + 1) * rows, at] = jnp.transpose(ref[col])


def flatten(place, first, second):
    cols, block, rows = first.shape
    steps = 3
    each = cols // steps
    return pl.pallas_call(
        flatten_kernel,
        grid_spec=pltpu.PrefetchScalarGridSpec(
            num_scalar_prefetch=1,
            grid=(steps,),
            in_specs=[pl.BlockSpec((each, block, rows), lambda k, s: (k, 0, 0))] * 2,
            out_specs=pl.BlockSpec((each * rows, 2 * block), lambda k, s: (k, 0)),
        ),
        out_shape=jax.ShapeDtypeStruct((cols * rows, 2 * block), jnp.bfloat16),
        compiler_params=pltpu.CompilerParams(vmem_limit_bytes=GRANT),
        cost_estimate=cost(3),
        name="flatten",
    )(place, first, second)


def kernel_terms_kernel(count, place_ref, grid_ref, feat_ref, out_ref, top_ref):
    chans = grid_ref.shape[0] // TAPS
    parts = count // GROUP
    height = chans // GROUP
    width = feat_ref.shape[1] // parts
    sums = jnp.dot(grid_ref[...], feat_ref[...], preferred_element_type=jnp.float32)
    largest = jnp.max(jnp.abs(sums))

    @pl.when(pl.program_id(0) == 0)
    def _():
        top_ref[...] = jnp.full(top_ref.shape, TINY, jnp.float32)

    top_ref[...] = jnp.maximum(top_ref[...], largest)
    for owner in range(count):
        at = lax.rem(owner - place_ref[0] + count, count)
        top = (owner % GROUP) * height
        side = (owner // GROUP) * width
        for tap in range(TAPS):
            low = tap * chans + top
            out_ref[at, tap] = sums[low : low + height, side : side + width]


def kernel_terms(place, grid, feat, count):
    depth, wide = feat.shape
    taps = 3 * TAPS
    chans = grid.shape[0] // taps
    shape = (count, taps, chans // GROUP, wide // (count // GROUP))
    return pl.pallas_call(
        functools.partial(kernel_terms_kernel, count),
        grid_spec=pltpu.PrefetchScalarGridSpec(
            num_scalar_prefetch=1,
            grid=(3,),
            in_specs=[
                pl.BlockSpec((TAPS * chans, depth), lambda k, s: (k, 0)),
                pl.BlockSpec((depth, wide), lambda k, s: (0, 0)),
            ],
            out_specs=[
                pl.BlockSpec((count, TAPS) + shape[2:], lambda k, s: (0, k, 0, 0)),
                pl.BlockSpec((1,) + shape[2:], lambda k, s: (0, 0, 0)),
            ],
        ),
        out_shape=[
            pltpu.HBM(shape, jnp.float32),
            jax.ShapeDtypeStruct((1,) + shape[2:], jnp.float32),
        ],
        compiler_params=pltpu.CompilerParams(vmem_limit_bytes=GRANT),
        cost_estimate=cost(6),
        name="kernel_terms",
    )(place, in_hbm(grid), feat)


def input_terms_kernel(place_ref, weight_ref, grid_ref, *refs):
    out_ref = refs[-1]
    cols, block, rows = out_ref.shape
    sums = jnp.dot(weight_ref[...], grid_ref[...], preferred_element_type=jnp.float32)
    for col in range(cols):
        part = sums[:, col * rows : (col + 1) * rows]
        if len(refs) == 2:
            part = part + refs[0][col]
        out_ref[col] = part


def input_terms(place, weight_rows, grid, added=None, *, block, cols, rows):
    steps = 3
    depth = weight_rows.shape[1]
    wide = pl.BlockSpec((cols // steps, block, rows), lambda t, s: (t, 0, 0))
    operands = [in_hbm(weight_rows), in_hbm(grid)] + ([] if added is None else [added])
    return pl.pallas_call(
        input_terms_kernel,
        grid_spec=pltpu.PrefetchScalarGridSpec(
            num_scalar_prefetch=1,
            grid=(steps,),
            in_specs=[
                pl.BlockSpec((block, depth), lambda t, s: (s[0], 0)),
                pl.BlockSpec((depth, cols * rows // steps), lambda t, s: (0, t)),
            ]
            + ([] if added is None else [wide]),
            out_specs=wide,
        ),
        out_shape=jax.ShapeDtypeStruct((cols, block, rows), jnp.float32),
        compiler_params=pltpu.CompilerParams(vmem_limit_bytes=GRANT),
        cost_estimate=cost(3.5),
        name="input_terms",
    )(place, *operands)


def unfold_kernel(norm, held, place_ref, *refs):
    out_ref = refs[-1]
    taps = out_ref.shape[0]
    half = pl.program_id(1)
    for at in range(held):

        @pl.when(pl.program_id(0) == at)
        def _(code_ref=refs[at]):
            codes = code_ref[pl.ds(half * taps, taps)]
            out_ref[...] = decode(codes, code_ref[pl.ds(2 * taps + half, 1)], norm)


def unfold(place, norm, shape, codes, before=None):
    held = len(codes)
    taps = shape[0]
    height, width = codes[0].shape[1:]
    operands = codes + ([] if before is None else [before])
    return pl.pallas_call(
        functools.partial(unfold_kernel, norm, held),
        grid_spec=pltpu.PrefetchScalarGridSpec(
            num_scalar_prefetch=1,
            grid=(held, 2),
            in_specs=[pl.BlockSpec(codes[0].shape, lambda j, p, s: (0, 0, 0))] * held
            + ([] if before is None else [pl.BlockSpec(memory_space=pl.ANY)]),
            out_specs=pl.BlockSpec(
                (taps, height, width), lambda j, p, s: (0, s[j], s[held + 2 * j + p])
            ),
        ),
        out_shape=jax.ShapeDtypeStruct(shape, jnp.float32),
        input_output_aliases={} if before is None else {held + 1: 0},
        compiler_params=pltpu.CompilerParams(vmem_limit_bytes=GRANT),
        cost_estimate=cost(3),
        name="unfold",
    )(place, *operands)


def first_hop_kernel(cut, terms_ref, top_ref, up_ref, down_ref):
    taps = terms_ref.shape[1]
    bound = bound_code(top_ref[...])
    up_ref[:cut] = encode(terms_ref[0, :cut], bound)
    up_ref[cut:] = bound
    down_ref[: taps - cut] = encode(terms_ref[0, cut:], bound)
    down_ref[taps - cut :] = bound


def next_hop_kernel(cut, up_ref, down_ref, to_up_ref, to_down_ref, top_ref, up_out, down_out):
    taps = to_up_ref.shape[1]
    top = top_ref[...]
    for ref, terms_ref, out_ref, low, high in (
        (up_ref, to_up_ref, up_out, 0, cut),
        (down_ref, to_down_ref, down_out, cut if cut < taps else 0, taps),
    ):
        arrived = ref[high - low :]
        bound = bound_code(arrived.astype(jnp.float32) + top)
        value = decode(ref[: high - low], arrived, 1.0 / REACH) + terms_ref[0, low:high]
        out_ref[low:high] = encode(value, bound)
        if low > 0:
            out_ref[:low] = encode(terms_ref[0, :low], bound)
        if high < taps:
            out_ref[high:taps] = encode(terms_ref[0, high:], bound)
        out_ref[taps:] = bound


def last_hop_kernel(*refs):
    out_ref = refs[-1]
    taps = refs[3].shape[1]
    for part in range(2):
        up_ref, down_ref, top_ref, own_ref = refs[4 * part : 4 * part + 4]
        up_bound, down_bound = up_ref[taps:], down_ref[taps:]
        bound = bound_code(
            up_bound.astype(jnp.float32) + down_bound.astype(jnp.float32) + top_ref[...]
        )
        value = own_ref[0] + decode(up_ref[:taps], up_bound, 1.0 / REACH)
        value = value + decode(down_ref[:taps], down_bound, 1.0 / REACH)
        out_ref[part * taps : (part + 1) * taps] = encode(value, bound)
        out_ref[2 * taps + part : 2 * taps + part + 1] = bound


def chunk_spec(terms, at):
    return pl.BlockSpec((1,) + terms.shape[1:], lambda i: (at, 0, 0, 0))


def whole_spec(array):
    return pl.BlockSpec(array.shape, lambda i: (0,) * array.ndim)


def hop_call(kernel, out_rows, operands, specs, name):
    tail = operands[-1].shape[-2:]
    shapes = [jax.ShapeDtypeStruct((rows,) + tail, jnp.bfloat16) for rows in out_rows]
    return pl.pallas_call(
        kernel,
        grid=(1,),
        in_specs=specs,
        out_specs=[whole_spec(shape) for shape in shapes],
        out_shape=shapes,
        compiler_params=pltpu.CompilerParams(vmem_limit_bytes=GRANT),
        cost_estimate=cost(2),
        name=name,
    )(*operands)


class Order:
    def __init__(self):
        self.last = ()

    def gate(self, *values):
        return lax.optimization_barrier(values + self.last)[: len(values)]

    def pin(self, value):
        out = self.gate(value)[0]
        self.last = (out,)
        return out

    def __call__(self, kernel, *values):
        result = kernel(*self.gate(*values))
        self.last = (jax.tree.leaves(result)[0],)
        return result


class Ring:
    def __init__(self, count, taps):
        order = ring_order(count)
        self.ahead = [(order[i], order[(i + 1) % count]) for i in range(count)]
        self.behind = [(b, a) for a, b in self.ahead]
        self.count, self.half = count, count // 2
        self.taps, self.cut = taps, (taps + 1) // 2

    def send(self, messages):
        up, down = messages
        return lax.ppermute(up, "lon", self.ahead), lax.ppermute(down, "lon", self.behind)

    def first(self, terms, top):
        return hop_call(
            functools.partial(first_hop_kernel, self.cut),
            [self.cut + 1, self.taps - self.cut + 1],
            [in_hbm(terms), top],
            [chunk_spec(terms, self.half), whole_spec(top)],
            "first_hop",
        )

    def next(self, left, messages, terms, top):
        up, down = messages
        cut = self.cut if left == self.half else self.taps
        return hop_call(
            functools.partial(next_hop_kernel, cut),
            [self.taps + 1] * 2,
            [up, down, in_hbm(terms), in_hbm(terms), top],
            [
                whole_spec(up),
                whole_spec(down),
                chunk_spec(terms, left - 1),
                chunk_spec(terms, self.count - left + 1),
                whole_spec(top),
            ],
            "next_hop",
        )

    def last(self, parts):
        operands, specs = [], []
        for (up, down), top, terms in parts:
            operands += [up, down, top, in_hbm(terms)]
            specs += [whole_spec(up), whole_spec(down), whole_spec(top), chunk_spec(terms, 0)]
        return hop_call(last_hop_kernel, [2 * self.taps + 2], operands, specs, "last_hop")[0]


def local(features, cotangent, weights):
    block, _, cols, rows = features.shape
    chans = cotangent.shape[1]
    total = weights.shape[4]
    count = lax.axis_size("lon")
    cells = cols * count * rows
    lon = lax.axis_index("lon")
    ch = lax.axis_index("ch")
    place_x, place_core = ch // 2, ch % 2
    spot = ring_position(lon, count)

    feat = jnp.transpose(features.reshape(block, cols, rows), (1, 0, 2))
    cot = jnp.transpose(cotangent.reshape(3, chans, cols, rows), (0, 2, 1, 3))

    tails, heads = edges(cot)
    left = lax.ppermute(tails, "lon", [(i, (i + 1) % count) for i in range(count)])
    right = lax.ppermute(heads, "lon", [((i + 1) % count, i) for i in range(count)])

    to_core = [(i, i ^ 1) for i in range(4)]
    to_x = [(i, i ^ 2) for i in range(4)]
    far = lax.ppermute(feat, "ch", to_x)
    near = lax.ppermute(feat, "ch", to_core)
    far_near = lax.ppermute(far, "ch", to_core)

    norm = 1.0 / (REACH * cells**0.5)
    place = jnp.stack([spot, place_core]).astype(jnp.int32)
    ring = Ring(count, 3 * TAPS)
    order = Order()

    weight_rows = order(jnp.transpose, weights.reshape(-1, total))
    flat_near = order(functools.partial(flatten, place), feat, near)
    grid = order(spread, cot, left, right)

    def terms_of(x, core, *added):
        at = (2 * x + core).astype(jnp.int32).reshape(1)
        run = functools.partial(input_terms, at, block=block, cols=cols, rows=rows)
        return order(run, weight_rows, grid, *added)

    def features_with(flat):
        return order(functools.partial(kernel_terms, place, count=count), grid, flat)

    def hop(left_over, sent, terms, top):
        return order(functools.partial(ring.next, left_over), ring.send(sent), terms, top)

    half = ring.half
    terms_near, top_near = features_with(flat_near)
    out_near = order(ring.first, terms_near, top_near)
    flat_far = order(functools.partial(flatten, place), far, far_near)
    out_near = hop(half, out_near, terms_near, top_near)
    terms_far, top_far = features_with(flat_far)
    away = terms_of(1 - place_x, 1 - place_core)
    out_near = hop(half - 1, out_near, terms_near, top_near)
    away = lax.ppermute(order.gate(away)[0], "ch", to_core)
    out_far = order(ring.first, terms_far, top_far)
    for left_over in range(half - 2, 1, -1):
        out_near = hop(left_over, out_near, terms_near, top_near)
        if left_over == half - 2:
            across = terms_of(1 - place_x, place_core, away)
            across = [
                lax.ppermute(across[cols * k // 2 : cols * (k + 1) // 2], "ch", to_x)
                for k in range(2)
            ]
        out_far = hop(left_over + 2, out_far, terms_far, top_far)
    out_far = hop(3, out_far, terms_far, top_far)
    out_far = hop(2, out_far, terms_far, top_far)
    own = order(
        lambda got_near, got_far: ring.last(
            [(got_near, top_near, terms_near), (got_far, top_far, terms_far)]
        ),
        ring.send(out_near),
        ring.send(out_far),
    )

    shape = (3 * TAPS, chans, total)
    parts = count // GROUP

    def write(codes, *before):
        owners = [lax.rem(spot + ahead, count) for ahead, _ in codes]
        at = [lax.rem(owner, GROUP) for owner in owners]
        for owner in owners:
            at += [lax.div(owner, GROUP) + parts * x for x in (place_x, 1 - place_x)]
        place = jnp.stack(at).astype(jnp.int32)
        return order(functools.partial(unfold, place, norm, shape), [c for _, c in codes], *before)

    up = down = own
    held = [(0, own)]
    written = ()
    for step in range(1, half):
        up, down = ring.send((up, down))
        if step == 1:
            beside = terms_of(place_x, 1 - place_core)
            across[0] = order.pin(across[0])
        else:
            written = (write(held, *written),)
            held = []
        if step == 2:
            mine = terms_of(place_x, place_core)
        held += [(count - step, up), (step, down)]
        up, down = order.gate(up, down)
        if step == 1:
            beside = lax.ppermute(lax.optimization_barrier((beside, up))[0], "ch", to_core)
    middle = ring.send((up[: ring.taps], down[ring.taps :]))
    written = (write(held, *written),)
    across = jnp.concatenate(across, axis=0)
    input_grad = order(lambda *parts: sum(parts).astype(jnp.bfloat16), mine, beside, across)
    kernel_grad = write([(half, jnp.concatenate(middle, axis=0))], *written)

    input_grad = jnp.transpose(input_grad, (1, 0, 2)).reshape(block, 1, cols, rows)
    return (input_grad, kernel_grad.reshape(3, 3, 3, chans, total))


def solution(mesh):
    return jax.shard_map(
        local,
        mesh=mesh,
        in_specs=(
            P("ch", None, "lon", None),
            P(None, "ch", None, "lon", None),
            P(None, None, None, "ch", None),
        ),
        out_specs=(P("ch", None, "lon", None), P(None, None, None, "ch", None)),
        check_vma=False,
    )
```

```python
import functools

import jax
import jax.numpy as jnp
from jax import lax
from jax.experimental import pallas as pl
from jax.experimental.pallas import tpu as pltpu
from jax.sharding import PartitionSpec as P

DILATIONS = (6, 12, 18)
TAPS = 9
GROUP = 8
REACH = 2.0**15.5
TINY = 1e-30
MIB = 1024 * 1024
GRANT = 20 * MIB
PACE = 3e8
BLOCKS_AT = 2
ROWS_AT = 6


def cost(micros):
    return pl.CostEstimate(flops=int(micros * PACE), bytes_accessed=0, transcendentals=0)


def in_hbm(value):
    return pltpu.with_memory_space_constraint(value, pltpu.HBM)


def ring_order(count):
    return list(range(0, count, 2)) + list(range(count - 1, 0, -2))


def ring_position(index, count):
    return jnp.where(index % 2 == 0, index // 2, count - 1 - index // 2)


def bound_code(bound):
    return (bound * 1.01).astype(jnp.bfloat16)


def encode(value, bound):
    power = value * (REACH / bound.astype(jnp.float32))
    power = power * power
    power = power * power
    power = power * power
    return jnp.where(value < 0, -power, power).astype(jnp.bfloat16)


def decode(code, bound, norm):
    wide = code.astype(jnp.float32)
    root = jnp.exp(0.125 * jnp.log(jnp.abs(wide))) * (bound.astype(jnp.float32) * norm)
    return jnp.where(wide < 0, -root, root)


def edge_kernel(cot_ref, tail_ref, head_ref):
    cols = cot_ref.shape[1]
    start = 0
    for branch in range(3):
        dilation = DILATIONS[branch]
        tail_ref[start : start + dilation] = cot_ref[branch, cols - dilation :]
        head_ref[start : start + dilation] = cot_ref[branch, :dilation]
        start += dilation


def edges(cot):
    shape = (sum(DILATIONS),) + cot.shape[2:]
    return pl.pallas_call(
        edge_kernel,
        out_shape=[jax.ShapeDtypeStruct(shape, cot.dtype)] * 2,
        compiler_params=pltpu.CompilerParams(vmem_limit_bytes=GRANT),
        cost_estimate=cost(1),
        name="edges",
    )(cot)


def spread_kernel(cot_ref, left_ref, right_ref, out_ref):
    branch_at = pl.program_id(0)
    cols, chans, rows = cot_ref.shape[1:]
    lane = lax.broadcasted_iota(jnp.int32, (chans, rows), 1)
    start = 0
    for branch in range(3):
        dilation = DILATIONS[branch]

        @pl.when(branch_at == branch)
        def _(dilation=dilation, start=start):
            for place in range(-dilation, cols + dilation):
                if place < 0:
                    column = left_ref[start + place + dilation]
                elif place >= cols:
                    column = right_ref[start + place - cols]
                else:
                    column = cot_ref[0, place]
                wide = column.astype(jnp.float32)
                for lat_tap in range(3):
                    shift = dilation * (lat_tap - 1)
                    if shift == 0:
                        moved = column
                    else:
                        keep = lane >= shift if shift > 0 else lane < rows + shift
                        moved = jnp.where(keep, pltpu.roll(wide, shift % rows, 1), 0.0)
                        moved = moved.astype(jnp.bfloat16)
                    for lon_tap in range(3):
                        target = place + dilation * (lon_tap - 1)
                        if 0 <= target < cols:
                            tap = 3 * lat_tap + lon_tap
                            out_ref[
                                tap * chans : (tap + 1) * chans, target * rows : (target + 1) * rows
                            ] = moved

        start += dilation


def spread(cot, left, right):
    branches, cols, chans, rows = cot.shape
    return pl.pallas_call(
        spread_kernel,
        grid=(branches,),
        in_specs=[
            pl.BlockSpec((1, cols, chans, rows), lambda k: (k, 0, 0, 0)),
            pl.BlockSpec(left.shape, lambda k: (0, 0, 0)),
            pl.BlockSpec(right.shape, lambda k: (0, 0, 0)),
        ],
        out_specs=pl.BlockSpec((TAPS * chans, cols * rows), lambda k: (k, 0)),
        out_shape=jax.ShapeDtypeStruct((branches * TAPS * chans, cols * rows), jnp.bfloat16),
        compiler_params=pltpu.CompilerParams(vmem_limit_bytes=GRANT),
        cost_estimate=cost(2.5),
        name="spread",
    )(cot, left, right)


def flatten_kernel(place_ref, first_ref, second_ref, out_ref):
    cols, block, rows = first_ref.shape
    for ref, core in ((first_ref, place_ref[1]), (second_ref, 1 - place_ref[1])):
        at = pl.ds(pl.multiple_of(core * block, block), block)
        for col in range(cols):
            out_ref[col * rows : (col + 1) * rows, at] = jnp.transpose(ref[col])


def flatten(table, first, second):
    cols, block, rows = first.shape
    steps = 3
    each = cols // steps
    return pl.pallas_call(
        flatten_kernel,
        grid_spec=pltpu.PrefetchScalarGridSpec(
            num_scalar_prefetch=1,
            grid=(steps,),
            in_specs=[pl.BlockSpec((each, block, rows), lambda k, s: (k, 0, 0))] * 2,
            out_specs=pl.BlockSpec((each * rows, 2 * block), lambda k, s: (k, 0)),
        ),
        out_shape=jax.ShapeDtypeStruct((cols * rows, 2 * block), jnp.bfloat16),
        compiler_params=pltpu.CompilerParams(vmem_limit_bytes=GRANT),
        cost_estimate=cost(3),
        name="flatten",
    )(table, first, second)


def kernel_terms_kernel(count, place_ref, grid_ref, feat_ref, out_ref, top_ref):
    chans = grid_ref.shape[0] // TAPS
    parts = count // GROUP
    height = chans // GROUP
    width = feat_ref.shape[1] // parts
    sums = jnp.dot(grid_ref[...], feat_ref[...], preferred_element_type=jnp.float32)
    largest = jnp.max(jnp.abs(sums))

    @pl.when(pl.program_id(0) == 0)
    def _():
        top_ref[...] = jnp.full(top_ref.shape, TINY, jnp.float32)

    top_ref[...] = jnp.maximum(top_ref[...], largest)
    for owner in range(count):
        at = lax.rem(owner - place_ref[0] + count, count)
        top = (owner % GROUP) * height
        side = (owner // GROUP) * width
        for tap in range(TAPS):
            low = tap * chans + top
            out_ref[at, tap] = sums[low : low + height, side : side + width]


def kernel_terms(table, grid, feat, count):
    depth, wide = feat.shape
    taps = 3 * TAPS
    chans = grid.shape[0] // taps
    shape = (count, taps, chans // GROUP, wide // (count // GROUP))
    return pl.pallas_call(
        functools.partial(kernel_terms_kernel, count),
        grid_spec=pltpu.PrefetchScalarGridSpec(
            num_scalar_prefetch=1,
            grid=(3,),
            in_specs=[
                pl.BlockSpec((TAPS * chans, depth), lambda k, s: (k, 0)),
                pl.BlockSpec((depth, wide), lambda k, s: (0, 0)),
            ],
            out_specs=[
                pl.BlockSpec((count, TAPS) + shape[2:], lambda k, s: (0, k, 0, 0)),
                pl.BlockSpec((1,) + shape[2:], lambda k, s: (0, 0, 0)),
            ],
        ),
        out_shape=[
            pltpu.HBM(shape, jnp.float32),
            jax.ShapeDtypeStruct((1,) + shape[2:], jnp.float32),
        ],
        compiler_params=pltpu.CompilerParams(vmem_limit_bytes=GRANT),
        cost_estimate=cost(6),
        name="kernel_terms",
    )(table, grid, feat)


def input_terms_kernel(place_ref, weight_ref, grid_ref, *refs):
    out_ref = refs[-1]
    cols, block, rows = out_ref.shape
    sums = jnp.dot(weight_ref[...], grid_ref[...], preferred_element_type=jnp.float32)
    for col in range(cols):
        part = sums[:, col * rows : (col + 1) * rows]
        if len(refs) == 2:
            part = part + refs[0][col]
        out_ref[col] = part


def input_terms(at, table, weight_rows, grid, added=None, *, block, span, rows):
    first, cols = span
    depth = weight_rows.shape[1]
    each = 6 if cols % 6 == 0 else 3
    steps = cols // each
    skip = first // each
    wide = pl.BlockSpec((each, block, rows), lambda t, s: (t, 0, 0))
    operands = [weight_rows, grid] + ([] if added is None else [added])
    return pl.pallas_call(
        input_terms_kernel,
        grid_spec=pltpu.PrefetchScalarGridSpec(
            num_scalar_prefetch=1,
            grid=(steps,),
            in_specs=[
                pl.BlockSpec((block, depth), lambda t, s: (s[at], 0)),
                pl.BlockSpec((depth, each * rows), lambda t, s: (0, t + skip)),
            ]
            + (
                []
                if added is None
                else [pl.BlockSpec((each, block, rows), lambda t, s: (t + skip, 0, 0))]
            ),
            out_specs=wide,
        ),
        out_shape=jax.ShapeDtypeStruct((cols, block, rows), jnp.float32),
        compiler_params=pltpu.CompilerParams(vmem_limit_bytes=GRANT),
        cost_estimate=cost(3.5),
        name="input_terms",
    )(table, *operands)


def unfold_kernel(norm, held, place_ref, *refs):
    out_ref = refs[-1]
    taps = out_ref.shape[0]
    half = pl.program_id(1)
    for at in range(held):

        @pl.when(pl.program_id(0) == at)
        def _(code_ref=refs[at]):
            codes = code_ref[pl.ds(half * taps, taps)]
            out_ref[...] = decode(codes, code_ref[pl.ds(2 * taps + half, 1)], norm)


def unfold(aheads, norm, shape, table, codes, before=None):
    held = len(codes)
    count = shape[1] // codes[0].shape[1] * (shape[2] // codes[0].shape[2]) // 2
    taps = shape[0]
    height, width = codes[0].shape[1:]
    operands = codes + ([] if before is None else [before])

    def pick(j, values):
        chosen = values[0]
        for k in range(1, held):
            chosen = jnp.where(j == k, values[k], chosen)
        return chosen

    def place(j, p, s):
        return (
            0,
            s[ROWS_AT + pick(j, aheads)],
            s[ROWS_AT + count + 2 * pick(j, aheads) + p],
        )

    return pl.pallas_call(
        functools.partial(unfold_kernel, norm, held),
        grid_spec=pltpu.PrefetchScalarGridSpec(
            num_scalar_prefetch=1,
            grid=(held, 2),
            in_specs=[pl.BlockSpec(codes[0].shape, lambda j, p, s: (0, 0, 0))] * held
            + ([] if before is None else [pl.BlockSpec(memory_space=pl.ANY)]),
            out_specs=pl.BlockSpec((taps, height, width), place),
        ),
        out_shape=jax.ShapeDtypeStruct(shape, jnp.float32),
        input_output_aliases={} if before is None else {held + 1: 0},
        compiler_params=pltpu.CompilerParams(vmem_limit_bytes=GRANT),
        cost_estimate=cost(3),
        name="unfold",
    )(table, *operands)


def first_hop_kernel(cut, terms_ref, top_ref, up_ref, down_ref):
    taps = terms_ref.shape[1]
    bound = bound_code(top_ref[...])
    up_ref[:cut] = encode(terms_ref[0, :cut], bound)
    up_ref[cut:] = bound
    down_ref[: taps - cut] = encode(terms_ref[0, cut:], bound)
    down_ref[taps - cut :] = bound


def next_hop_kernel(cut, up_ref, down_ref, to_up_ref, to_down_ref, top_ref, up_out, down_out):
    taps = to_up_ref.shape[1]
    top = top_ref[...]
    for ref, terms_ref, out_ref, low, high in (
        (up_ref, to_up_ref, up_out, 0, cut),
        (down_ref, to_down_ref, down_out, cut if cut < taps else 0, taps),
    ):
        arrived = ref[high - low :]
        bound = bound_code(arrived.astype(jnp.float32) + top)
        value = decode(ref[: high - low], arrived, 1.0 / REACH) + terms_ref[0, low:high]
        out_ref[low:high] = encode(value, bound)
        if low > 0:
            out_ref[:low] = encode(terms_ref[0, :low], bound)
        if high < taps:
            out_ref[high:taps] = encode(terms_ref[0, high:], bound)
        out_ref[taps:] = bound


def last_hop_kernel(*refs):
    out_ref = refs[-1]
    taps = refs[3].shape[1]
    for part in range(2):
        up_ref, down_ref, top_ref, own_ref = refs[4 * part : 4 * part + 4]
        up_bound, down_bound = up_ref[taps:], down_ref[taps:]
        bound = bound_code(
            up_bound.astype(jnp.float32) + down_bound.astype(jnp.float32) + top_ref[...]
        )
        value = own_ref[0] + decode(up_ref[:taps], up_bound, 1.0 / REACH)
        value = value + decode(down_ref[:taps], down_bound, 1.0 / REACH)
        out_ref[part * taps : (part + 1) * taps] = encode(value, bound)
        out_ref[2 * taps + part : 2 * taps + part + 1] = bound


def chunk_spec(terms, at):
    return pl.BlockSpec((1,) + terms.shape[1:], lambda i: (at, 0, 0, 0))


def whole_spec(array):
    return pl.BlockSpec(array.shape, lambda i: (0,) * array.ndim)


def hop_call(kernel, out_rows, operands, specs, name):
    tail = operands[-1].shape[-2:]
    shapes = [jax.ShapeDtypeStruct((rows,) + tail, jnp.bfloat16) for rows in out_rows]
    return pl.pallas_call(
        kernel,
        grid=(1,),
        in_specs=specs,
        out_specs=[whole_spec(shape) for shape in shapes],
        out_shape=shapes,
        compiler_params=pltpu.CompilerParams(vmem_limit_bytes=GRANT),
        cost_estimate=cost(2),
        name=name,
    )(*operands)


class Order:
    def __init__(self):
        self.last = ()

    def gate(self, *values):
        if not self.last:
            return values
        return lax.optimization_barrier(values + self.last)[: len(values)]

    def pin(self, value):
        out = self.gate(value)[0]
        self.last = (out,)
        return out

    def __call__(self, kernel, *values):
        result = kernel(*self.gate(*values))
        self.last = (jax.tree.leaves(result)[0],)
        return result


class Ring:
    def __init__(self, count, taps):
        order = ring_order(count)
        self.ahead = [(order[i], order[(i + 1) % count]) for i in range(count)]
        self.behind = [(b, a) for a, b in self.ahead]
        self.count, self.half = count, count // 2
        self.taps, self.cut = taps, (taps + 1) // 2

    def send(self, messages):
        up, down = messages
        return lax.ppermute(up, "lon", self.ahead), lax.ppermute(down, "lon", self.behind)

    def first(self, terms, top):
        return hop_call(
            functools.partial(first_hop_kernel, self.cut),
            [self.cut + 1, self.taps - self.cut + 1],
            [in_hbm(terms), top],
            [chunk_spec(terms, self.half), whole_spec(top)],
            "first_hop",
        )

    def next(self, left, messages, terms, top):
        up, down = messages
        cut = self.cut if left == self.half else self.taps
        return hop_call(
            functools.partial(next_hop_kernel, cut),
            [self.taps + 1] * 2,
            [up, down, in_hbm(terms), in_hbm(terms), top],
            [
                whole_spec(up),
                whole_spec(down),
                chunk_spec(terms, left - 1),
                chunk_spec(terms, self.count - left + 1),
                whole_spec(top),
            ],
            "next_hop",
        )

    def last(self, parts):
        operands, specs = [], []
        for (up, down), top, terms in parts:
            operands += [up, down, top, in_hbm(terms)]
            specs += [whole_spec(up), whole_spec(down), whole_spec(top), chunk_spec(terms, 0)]
        return hop_call(last_hop_kernel, [2 * self.taps + 2], operands, specs, "last_hop")[0]


def make_table(lon, ch, count):
    place_x, place_core = ch // 2, ch % 2
    spot = ring_position(lon, count)
    owners = (spot + jnp.arange(count, dtype=jnp.int32)) % count
    sides = jnp.stack([place_x, 1 - place_x]) * (count // GROUP)
    return jnp.concatenate(
        [
            jnp.stack([spot, place_core, 3 - ch, ch ^ 2, ch ^ 1, ch]),
            owners % GROUP,
            (owners[:, None] // GROUP + sides[None]).reshape(-1),
        ]
    ).astype(jnp.int32)


def local(features, cotangent, weights):
    block, _, cols, rows = features.shape
    chans = cotangent.shape[1]
    total = weights.shape[4]
    count = lax.axis_size("lon")
    cells = cols * count * rows

    feat = jnp.transpose(features.reshape(block, cols, rows), (1, 0, 2))
    cot = jnp.transpose(cotangent.reshape(3, chans, cols, rows), (0, 2, 1, 3))
    order = Order()

    tails, heads = order(edges, cot)
    left = lax.ppermute(tails, "lon", [(i, (i + 1) % count) for i in range(count)])
    right = lax.ppermute(heads, "lon", [((i + 1) % count, i) for i in range(count)])

    to_core = [(i, i ^ 1) for i in range(4)]
    to_x = [(i, i ^ 2) for i in range(4)]
    far = lax.ppermute(feat, "ch", to_x)
    near = lax.ppermute(feat, "ch", to_core)

    norm = 1.0 / (REACH * cells**0.5)
    ring = Ring(count, 3 * TAPS)
    table = order(
        functools.partial(make_table, count=count), lax.axis_index("lon"), lax.axis_index("ch")
    )
    weight_rows = order(jnp.transpose, weights.reshape(-1, total))
    flat_near = order(flatten, table, feat, near)
    left, right, far = order.gate(left, right, far)
    grid = order(spread, cot, left, right)
    far_near = lax.ppermute(far, "ch", to_core)

    def terms_of(which, span, *added):
        run = functools.partial(
            input_terms, BLOCKS_AT + which, block=block, span=span, rows=rows
        )
        return order(run, table, weight_rows, grid, *added)

    def features_with(flat):
        return order(functools.partial(kernel_terms, count=count), table, grid, flat)

    def hop(left_over, sent, terms, top):
        return order(functools.partial(ring.next, left_over), ring.send(sent), terms, top)

    half = ring.half
    spans = [(0, cols // 2), (cols // 2, cols // 2)]
    whole = (0, cols)
    terms_near, top_near = features_with(flat_near)
    out_near = order(ring.first, terms_near, top_near)
    flat_far = order(flatten, table, far, far_near)
    out_near = hop(half, out_near, terms_near, top_near)
    terms_far, top_far = features_with(flat_far)
    away = terms_of(0, whole)
    out_near = hop(half - 1, out_near, terms_near, top_near)
    away = lax.ppermute(order.gate(away)[0], "ch", to_core)
    out_far = order(ring.first, terms_far, top_far)
    for left_over in range(half - 2, 1, -1):
        out_near = hop(left_over, out_near, terms_near, top_near)
        if left_over == half - 2:
            across = [lax.ppermute(terms_of(1, span, away), "ch", to_x) for span in spans]
        out_far = hop(left_over + 2, out_far, terms_far, top_far)
    out_far = hop(3, out_far, terms_far, top_far)
    out_far = hop(2, out_far, terms_far, top_far)
    own = order(
        lambda got_near, got_far: ring.last(
            [(got_near, top_near, terms_near), (got_far, top_far, terms_far)]
        ),
        ring.send(out_near),
        ring.send(out_far),
    )

    shape = (3 * TAPS, chans, total)

    def write(codes, *before):
        aheads, values = zip(*codes)
        run = functools.partial(unfold, aheads, norm, shape)
        return order(run, table, list(values), *before)

    up = down = own
    held = [(0, own)]
    written = ()
    for step in range(1, half):
        up, down = ring.send((up, down))
        if step == 1:
            beside = terms_of(2, whole)
            across[0] = order.pin(across[0])
        else:
            written = (write(held, *written),)
            held = []
        if step == 2:
            mine = terms_of(3, whole)
        held += [(count - step, up), (step, down)]
        up, down = order.gate(up, down)
        if step == 1:
            beside = lax.ppermute(lax.optimization_barrier((beside, up))[0], "ch", to_core)
    middle = ring.send((up[: ring.taps], down[ring.taps :]))
    written = (write(held, *written),)
    across = jnp.concatenate(across, axis=0)
    input_grad = order(lambda *parts: sum(parts).astype(jnp.bfloat16), mine, beside, across)
    kernel_grad = write([(half, jnp.concatenate(middle, axis=0))], *written)

    input_grad = jnp.transpose(input_grad, (1, 0, 2)).reshape(block, 1, cols, rows)
    return (input_grad, kernel_grad.reshape(3, 3, 3, chans, total))


def solution(mesh):
    return jax.shard_map(
        local,
        mesh=mesh,
        in_specs=(
            P("ch", None, "lon", None),
            P(None, "ch", None, "lon", None),
            P(None, None, None, "ch", None),
        ),
        out_specs=(P("ch", None, "lon", None), P(None, None, None, "ch", None)),
        check_vma=False,
    )
```

```python
import functools

import jax
import jax.numpy as jnp
from jax import lax
from jax.experimental import pallas as pl
from jax.experimental.pallas import tpu as pltpu
from jax.sharding import PartitionSpec as P

DILATIONS = (6, 12, 18)
TAPS = 9
GROUP = 8
REACH = 2.0**15.5
TINY = 1e-30
MIB = 1024 * 1024
GRANT = 20 * MIB
PACE = 3e8
BLOCKS_AT = 2
ROWS_AT = 6


def cost(micros):
    return pl.CostEstimate(flops=int(micros * PACE), bytes_accessed=0, transcendentals=0)


def in_hbm(value):
    return pltpu.with_memory_space_constraint(value, pltpu.HBM)


def ring_order(count):
    return list(range(0, count, 2)) + list(range(count - 1, 0, -2))


def ring_position(index, count):
    return jnp.where(index % 2 == 0, index // 2, count - 1 - index // 2)


def bound_code(bound):
    return (bound * 1.01).astype(jnp.bfloat16)


def encode(value, bound):
    power = value * (REACH / bound.astype(jnp.float32))
    power = power * power
    power = power * power
    power = power * power
    return jnp.where(value < 0, -power, power).astype(jnp.bfloat16)


def decode(code, bound, norm):
    wide = code.astype(jnp.float32)
    root = jnp.exp(0.125 * jnp.log(jnp.abs(wide))) * (bound.astype(jnp.float32) * norm)
    return jnp.where(wide < 0, -root, root)


def edge_kernel(cot_ref, tail_ref, head_ref):
    cols = cot_ref.shape[1]
    start = 0
    for branch in range(3):
        dilation = DILATIONS[branch]
        tail_ref[start : start + dilation] = cot_ref[branch, cols - dilation :]
        head_ref[start : start + dilation] = cot_ref[branch, :dilation]
        start += dilation


def edges(cot):
    shape = (sum(DILATIONS),) + cot.shape[2:]
    return pl.pallas_call(
        edge_kernel,
        out_shape=[jax.ShapeDtypeStruct(shape, cot.dtype)] * 2,
        compiler_params=pltpu.CompilerParams(vmem_limit_bytes=GRANT),
        cost_estimate=cost(1),
        name="edges",
    )(cot)


def spread_kernel(cot_ref, left_ref, right_ref, out_ref):
    branch_at = pl.program_id(0)
    cols, chans, rows = cot_ref.shape[1:]
    lane = lax.broadcasted_iota(jnp.int32, (chans, rows), 1)
    start = 0
    for branch in range(3):
        dilation = DILATIONS[branch]

        @pl.when(branch_at == branch)
        def _(dilation=dilation, start=start):
            for place in range(-dilation, cols + dilation):
                if place < 0:
                    column = left_ref[start + place + dilation]
                elif place >= cols:
                    column = right_ref[start + place - cols]
                else:
                    column = cot_ref[0, place]
                wide = column.astype(jnp.float32)
                for lat_tap in range(3):
                    shift = dilation * (lat_tap - 1)
                    if shift == 0:
                        moved = column
                    else:
                        keep = lane >= shift if shift > 0 else lane < rows + shift
                        moved = jnp.where(keep, pltpu.roll(wide, shift % rows, 1), 0.0)
                        moved = moved.astype(jnp.bfloat16)
                    for lon_tap in range(3):
                        target = place + dilation * (lon_tap - 1)
                        if 0 <= target < cols:
                            tap = 3 * lat_tap + lon_tap
                            out_ref[
                                tap * chans : (tap + 1) * chans, target * rows : (target + 1) * rows
                            ] = moved

        start += dilation


def spread(cot, left, right):
    branches, cols, chans, rows = cot.shape
    return pl.pallas_call(
        spread_kernel,
        grid=(branches,),
        in_specs=[
            pl.BlockSpec((1, cols, chans, rows), lambda k: (k, 0, 0, 0)),
            pl.BlockSpec(left.shape, lambda k: (0, 0, 0)),
            pl.BlockSpec(right.shape, lambda k: (0, 0, 0)),
        ],
        out_specs=pl.BlockSpec((TAPS * chans, cols * rows), lambda k: (k, 0)),
        out_shape=jax.ShapeDtypeStruct((branches * TAPS * chans, cols * rows), jnp.bfloat16),
        compiler_params=pltpu.CompilerParams(vmem_limit_bytes=GRANT),
        cost_estimate=cost(2.5),
        name="spread",
    )(cot, left, right)


def flatten_kernel(place_ref, first_ref, second_ref, out_ref):
    cols, block, rows = first_ref.shape
    for ref, core in ((first_ref, place_ref[1]), (second_ref, 1 - place_ref[1])):
        at = pl.ds(pl.multiple_of(core * block, block), block)
        for col in range(cols):
            out_ref[col * rows : (col + 1) * rows, at] = jnp.transpose(ref[col])


def flatten(table, first, second):
    cols, block, rows = first.shape
    steps = 3
    each = cols // steps
    return pl.pallas_call(
        flatten_kernel,
        grid_spec=pltpu.PrefetchScalarGridSpec(
            num_scalar_prefetch=1,
            grid=(steps,),
            in_specs=[pl.BlockSpec((each, block, rows), lambda k, s: (k, 0, 0))] * 2,
            out_specs=pl.BlockSpec((each * rows, 2 * block), lambda k, s: (k, 0)),
        ),
        out_shape=jax.ShapeDtypeStruct((cols * rows, 2 * block), jnp.bfloat16),
        compiler_params=pltpu.CompilerParams(vmem_limit_bytes=GRANT),
        cost_estimate=cost(3),
        name="flatten",
    )(table, first, second)


def kernel_terms_kernel(count, place_ref, grid_ref, feat_ref, out_ref, top_ref):
    chans = grid_ref.shape[0] // TAPS
    parts = count // GROUP
    height = chans // GROUP
    width = feat_ref.shape[1] // parts
    sums = jnp.dot(grid_ref[...], feat_ref[...], preferred_element_type=jnp.float32)
    largest = jnp.max(jnp.abs(sums))

    @pl.when(pl.program_id(0) == 0)
    def _():
        top_ref[...] = jnp.full(top_ref.shape, TINY, jnp.float32)

    top_ref[...] = jnp.maximum(top_ref[...], largest)
    for owner in range(count):
        at = lax.rem(owner - place_ref[0] + count, count)
        top = (owner % GROUP) * height
        side = (owner // GROUP) * width
        for tap in range(TAPS):
            low = tap * chans + top
            out_ref[at, tap] = sums[low : low + height, side : side + width]


def kernel_terms(table, grid, feat, count):
    depth, wide = feat.shape
    taps = 3 * TAPS
    chans = grid.shape[0] // taps
    shape = (count, taps, chans // GROUP, wide // (count // GROUP))
    return pl.pallas_call(
        functools.partial(kernel_terms_kernel, count),
        grid_spec=pltpu.PrefetchScalarGridSpec(
            num_scalar_prefetch=1,
            grid=(3,),
            in_specs=[
                pl.BlockSpec((TAPS * chans, depth), lambda k, s: (k, 0)),
                pl.BlockSpec((depth, wide), lambda k, s: (0, 0)),
            ],
            out_specs=[
                pl.BlockSpec((count, TAPS) + shape[2:], lambda k, s: (0, k, 0, 0)),
                pl.BlockSpec((1,) + shape[2:], lambda k, s: (0, 0, 0)),
            ],
        ),
        out_shape=[
            pltpu.HBM(shape, jnp.float32),
            jax.ShapeDtypeStruct((1,) + shape[2:], jnp.float32),
        ],
        compiler_params=pltpu.CompilerParams(vmem_limit_bytes=GRANT),
        cost_estimate=cost(6),
        name="kernel_terms",
    )(table, grid, feat)


def input_terms_kernel(place_ref, weight_ref, grid_ref, *refs):
    out_ref = refs[-1]
    cols, block, rows = out_ref.shape
    sums = jnp.dot(weight_ref[...], grid_ref[...], preferred_element_type=jnp.float32)
    for col in range(cols):
        part = sums[:, col * rows : (col + 1) * rows]
        if len(refs) == 2:
            part = part + refs[0][col]
        out_ref[col] = part


def input_terms(at, table, weight_rows, grid, added=None, *, block, span, rows):
    first, cols = span
    depth = weight_rows.shape[1]
    each = 6 if cols % 6 == 0 else 3
    steps = cols // each
    skip = first // each
    wide = pl.BlockSpec((each, block, rows), lambda t, s: (t, 0, 0))
    operands = [weight_rows, grid] + ([] if added is None else [added])
    return pl.pallas_call(
        input_terms_kernel,
        grid_spec=pltpu.PrefetchScalarGridSpec(
            num_scalar_prefetch=1,
            grid=(steps,),
            in_specs=[
                pl.BlockSpec((block, depth), lambda t, s: (s[at], 0)),
                pl.BlockSpec((depth, each * rows), lambda t, s: (0, t + skip)),
            ]
            + (
                []
                if added is None
                else [pl.BlockSpec((each, block, rows), lambda t, s: (t + skip, 0, 0))]
            ),
            out_specs=wide,
        ),
        out_shape=jax.ShapeDtypeStruct((cols, block, rows), jnp.float32),
        compiler_params=pltpu.CompilerParams(vmem_limit_bytes=GRANT),
        cost_estimate=cost(3.5),
        name="input_terms",
    )(table, *operands)


def unfold_kernel(norm, held, table_ref, *refs):
    out_ref = refs[-1]
    taps = out_ref.shape[0]
    for at in range(held):

        @pl.when(pl.program_id(0) == at)
        def _(code_ref=refs[at]):
            out_ref[...] = decode(code_ref[:taps], code_ref[taps:], norm)


def unfold(places, norm, shape, table, codes, before=None):
    held = len(codes)
    taps = shape[0]
    height, width = codes[0].shape[1:]
    operands = codes + ([] if before is None else [before])

    def pick(j, values):
        chosen = values[0]
        for k in range(1, held):
            chosen = jnp.where(j == k, values[k], chosen)
        return chosen

    def place(j, s):
        row, col = (pick(j, [place[at] for place in places]) for at in range(2))
        return (0, s[row], s[col])

    return pl.pallas_call(
        functools.partial(unfold_kernel, norm, held),
        grid_spec=pltpu.PrefetchScalarGridSpec(
            num_scalar_prefetch=1,
            grid=(held,),
            in_specs=[pl.BlockSpec(codes[0].shape, lambda j, s: (0, 0, 0))] * held
            + ([] if before is None else [pl.BlockSpec(memory_space=pl.ANY)]),
            out_specs=pl.BlockSpec((taps, height, width), place),
        ),
        out_shape=jax.ShapeDtypeStruct(shape, jnp.float32),
        input_output_aliases={} if before is None else {held + 1: 0},
        compiler_params=pltpu.CompilerParams(vmem_limit_bytes=GRANT),
        cost_estimate=cost(3),
        name="unfold",
    )(table, *operands)


def first_hop_kernel(cut, terms_ref, top_ref, up_ref, down_ref):
    taps = terms_ref.shape[1]
    bound = bound_code(top_ref[...])
    up_ref[:cut] = encode(terms_ref[0, :cut], bound)
    up_ref[cut:] = bound
    down_ref[: taps - cut] = encode(terms_ref[0, cut:], bound)
    down_ref[taps - cut :] = bound


def next_hop_kernel(cut, up_ref, down_ref, to_up_ref, to_down_ref, top_ref, up_out, down_out):
    taps = to_up_ref.shape[1]
    top = top_ref[...]
    for ref, terms_ref, out_ref, low, high in (
        (up_ref, to_up_ref, up_out, 0, cut),
        (down_ref, to_down_ref, down_out, cut if cut < taps else 0, taps),
    ):
        arrived = ref[high - low :]
        bound = bound_code(arrived.astype(jnp.float32) + top)
        value = decode(ref[: high - low], arrived, 1.0 / REACH) + terms_ref[0, low:high]
        out_ref[low:high] = encode(value, bound)
        if low > 0:
            out_ref[:low] = encode(terms_ref[0, :low], bound)
        if high < taps:
            out_ref[high:taps] = encode(terms_ref[0, high:], bound)
        out_ref[taps:] = bound


def last_hop_kernel(up_ref, down_ref, top_ref, own_ref, out_ref):
    taps = own_ref.shape[1]
    up_bound, down_bound = up_ref[taps:], down_ref[taps:]
    bound = bound_code(
        up_bound.astype(jnp.float32) + down_bound.astype(jnp.float32) + top_ref[...]
    )
    value = own_ref[0] + decode(up_ref[:taps], up_bound, 1.0 / REACH)
    value = value + decode(down_ref[:taps], down_bound, 1.0 / REACH)
    out_ref[:taps] = encode(value, bound)
    out_ref[taps:] = bound


def chunk_spec(terms, at):
    return pl.BlockSpec((1,) + terms.shape[1:], lambda i: (at, 0, 0, 0))


def whole_spec(array):
    return pl.BlockSpec(array.shape, lambda i: (0,) * array.ndim)


def hop_call(kernel, out_rows, operands, specs, name):
    tail = operands[-1].shape[-2:]
    shapes = [jax.ShapeDtypeStruct((rows,) + tail, jnp.bfloat16) for rows in out_rows]
    return pl.pallas_call(
        kernel,
        grid=(1,),
        in_specs=specs,
        out_specs=[whole_spec(shape) for shape in shapes],
        out_shape=shapes,
        compiler_params=pltpu.CompilerParams(vmem_limit_bytes=GRANT),
        cost_estimate=cost(2),
        name=name,
    )(*operands)


class Order:
    def __init__(self):
        self.last = ()

    def gate(self, *values):
        if not self.last:
            return values
        return lax.optimization_barrier(values + self.last)[: len(values)]

    def pin(self, *values):
        values = self.gate(*values)
        self.last = (values[0],)
        return values

    def __call__(self, kernel, *values):
        result = kernel(*self.gate(*values))
        self.last = (jax.tree.leaves(result)[0],)
        return result


class Ring:
    def __init__(self, count, taps):
        order = ring_order(count)
        self.ahead = [(order[i], order[(i + 1) % count]) for i in range(count)]
        self.behind = [(b, a) for a, b in self.ahead]
        self.count, self.half = count, count // 2
        self.taps, self.cut = taps, (taps + 1) // 2

    def send(self, messages):
        up, down = messages
        return lax.ppermute(up, "lon", self.ahead), lax.ppermute(down, "lon", self.behind)

    def first(self, terms, top):
        return hop_call(
            functools.partial(first_hop_kernel, self.cut),
            [self.cut + 1, self.taps - self.cut + 1],
            [in_hbm(terms), top],
            [chunk_spec(terms, self.half), whole_spec(top)],
            "first_hop",
        )

    def next(self, left, messages, terms, top):
        up, down = messages
        cut = self.cut if left == self.half else self.taps
        return hop_call(
            functools.partial(next_hop_kernel, cut),
            [self.taps + 1] * 2,
            [up, down, in_hbm(terms), in_hbm(terms), top],
            [
                whole_spec(up),
                whole_spec(down),
                chunk_spec(terms, left - 1),
                chunk_spec(terms, self.count - left + 1),
                whole_spec(top),
            ],
            "next_hop",
        )

    def last(self, messages, terms, top):
        up, down = messages
        return hop_call(
            last_hop_kernel,
            [self.taps + 1],
            [up, down, top, in_hbm(terms)],
            [whole_spec(up), whole_spec(down), whole_spec(top), chunk_spec(terms, 0)],
            "last_hop",
        )[0]


class Chain:
    def __init__(self, ring, order, side, terms, top):
        self.ring, self.order, self.side = ring, order, side
        self.terms, self.top, self.left = terms, top, ring.half
        self.out = order(ring.first, terms, top)
        self.codes = []

    def arrive(self):
        self.out = self.order.pin(*self.ring.send(self.out))

    def hop(self):
        run = functools.partial(self.ring.next, self.left)
        self.out = self.order(run, self.out, self.terms, self.top)
        self.left -= 1

    def last(self):
        own = self.order(self.ring.last, self.out, self.terms, self.top)
        self.out = (own, own)
        self.keep(0, own)

    def keep(self, ahead, code):
        count = self.ring.count
        self.codes.append(
            ((ROWS_AT + ahead, ROWS_AT + count + 2 * ahead + self.side), code)
        )

    def take(self):
        taken, self.codes = self.codes, []
        return taken

    def move(self):
        ring, (up, down) = self.ring, self.out
        if self.left < ring.half:
            self.out = self.order.pin(*ring.send((up, down)))
            self.keep(ring.count - self.left, self.out[0])
            self.keep(self.left, self.out[1])
        else:
            cut = ring.cut
            parts = self.order.pin(*ring.send((up[:cut], down[cut:])))
            self.keep(ring.half, jnp.concatenate(parts, axis=0))
        self.left += 1


def make_table(lon, ch, count):
    place_x, place_core = ch // 2, ch % 2
    spot = ring_position(lon, count)
    owners = (spot + jnp.arange(count, dtype=jnp.int32)) % count
    sides = jnp.stack([place_x, 1 - place_x]) * (count // GROUP)
    return jnp.concatenate(
        [
            jnp.stack([spot, place_core, 3 - ch, ch ^ 2, ch ^ 1, ch]),
            owners % GROUP,
            (owners[:, None] // GROUP + sides[None]).reshape(-1),
        ]
    ).astype(jnp.int32)


def local(features, cotangent, weights):
    block, _, cols, rows = features.shape
    chans = cotangent.shape[1]
    total = weights.shape[4]
    count = lax.axis_size("lon")
    cells = cols * count * rows

    feat = jnp.transpose(features.reshape(block, cols, rows), (1, 0, 2))
    cot = jnp.transpose(cotangent.reshape(3, chans, cols, rows), (0, 2, 1, 3))
    order = Order()

    tails, heads = order(edges, cot)
    left = lax.ppermute(tails, "lon", [(i, (i + 1) % count) for i in range(count)])
    right = lax.ppermute(heads, "lon", [((i + 1) % count, i) for i in range(count)])

    to_core = [(i, i ^ 1) for i in range(4)]
    to_x = [(i, i ^ 2) for i in range(4)]
    far = lax.ppermute(feat, "ch", to_x)
    near = lax.ppermute(feat, "ch", to_core)

    norm = 1.0 / (REACH * cells**0.5)
    ring = Ring(count, 3 * TAPS)
    table = order(
        functools.partial(make_table, count=count), lax.axis_index("lon"), lax.axis_index("ch")
    )
    weight_rows = order(jnp.transpose, weights.reshape(-1, total))
    flat_near = order(flatten, table, feat, near)
    left, right, far = order.gate(left, right, far)
    grid = order(spread, cot, left, right)
    far_near = lax.ppermute(far, "ch", to_core)

    def terms_of(which, span, *added):
        run = functools.partial(
            input_terms, BLOCKS_AT + which, block=block, span=span, rows=rows
        )
        return order(run, table, weight_rows, grid, *added)

    def features_with(flat):
        return order(functools.partial(kernel_terms, count=count), table, grid, flat)

    half = ring.half
    spans = [(0, cols // 3), (cols // 3, cols - cols // 3)]
    whole = (0, cols)
    shape = (3 * TAPS, chans, total)
    written = []

    def write(*chains):
        taken = [item for chain in chains for item in chain.take()]
        places, codes = zip(*taken)
        run = functools.partial(unfold, places, norm, shape)
        written[:] = [order(run, table, list(codes), *written)]

    near = Chain(ring, order, 0, *features_with(flat_near))
    flat_far = order(flatten, table, far, far_near)
    near.arrive()
    near.hop()
    terms_far = features_with(flat_far)
    near.arrive()
    near.hop()
    far = Chain(ring, order, 1, *terms_far)
    away = terms_of(0, whole)
    near.arrive()
    far.arrive()
    away = lax.ppermute(order.gate(away)[0], "ch", to_core)
    near.hop()
    far.hop()
    for _ in range(half - 4):
        near.arrive()
        near.hop()
        far.arrive()
        far.hop()
    across = [terms_of(1, span, away) for span in spans]
    near.arrive()
    far.arrive()
    near.last()
    across = [lax.ppermute(part, "ch", to_x) for part in order.gate(*across)]
    far.hop()
    beside = terms_of(2, whole)
    across[0] = order.pin(across[0])[0]
    far.arrive()
    far.hop()
    near.move()
    beside = lax.ppermute(order.gate(beside)[0], "ch", to_core)
    mine = terms_of(3, whole)
    far.arrive()
    far.last()
    near.move()
    write(near)
    for _ in range(half - 4):
        near.move()
        far.move()
    far.move()
    near.move()
    write(near, far)
    far.move()
    near.move()
    write(near, far)
    far.move()
    across = jnp.concatenate(across, axis=0)
    input_grad = order(lambda *parts: sum(parts).astype(jnp.bfloat16), mine, beside, across)
    write(far)
    far.move()
    write(far)
    kernel_grad = written[0]

    input_grad = jnp.transpose(input_grad, (1, 0, 2)).reshape(block, 1, cols, rows)
    return (input_grad, kernel_grad.reshape(3, 3, 3, chans, total))


def solution(mesh):
    return jax.shard_map(
        local,
        mesh=mesh,
        in_specs=(
            P("ch", None, "lon", None),
            P(None, "ch", None, "lon", None),
            P(None, None, None, "ch", None),
        ),
        out_specs=(P("ch", None, "lon", None), P(None, None, None, "ch", None)),
        check_vma=False,
    )
```

```python
import functools

import jax
import jax.numpy as jnp
import numpy as np
from jax import lax
from jax.experimental import pallas as pl
from jax.experimental.pallas import tpu as pltpu
from jax.sharding import PartitionSpec as P

DILATIONS = (6, 12, 18)
TAPS = 9
GROUP = 8
REACH = 2.0**15.5
TINY = 1e-30
MIB = 1024 * 1024
GRANT = 24 * MIB
PACE = 3e8
BLOCKS_AT = 2


def cost(micros):
    return pl.CostEstimate(flops=int(micros * PACE), bytes_accessed=0, transcendentals=0)


def in_hbm(value):
    return pltpu.with_memory_space_constraint(value, pltpu.HBM)


def ring_order(count):
    return list(range(0, count, 2)) + list(range(count - 1, 0, -2))


def ring_position(index, count):
    return jnp.where(index % 2 == 0, index // 2, count - 1 - index // 2)


def bound_code(bound):
    return (bound * 1.01).astype(jnp.bfloat16)


def encode(value, bound):
    power = value * (REACH / bound.astype(jnp.float32))
    power = power * power
    power = power * power
    power = power * power
    return jnp.where(value < 0, -power, power).astype(jnp.bfloat16)


def decode(code, bound, norm):
    wide = code.astype(jnp.float32)
    root = jnp.exp(0.125 * jnp.log(jnp.abs(wide))) * (bound.astype(jnp.float32) * norm)
    return jnp.where(wide < 0, -root, root)


def edge_kernel(cot_ref, *out_refs):
    cols = cot_ref.shape[1]
    for branch in range(3):
        dilation = DILATIONS[branch]
        out_refs[2 * branch][...] = cot_ref[branch, cols - dilation :]
        out_refs[2 * branch + 1][...] = cot_ref[branch, :dilation]


def edges(cot):
    shapes = [
        jax.ShapeDtypeStruct((dilation,) + cot.shape[2:], cot.dtype)
        for dilation in DILATIONS
        for _ in range(2)
    ]
    return pl.pallas_call(
        edge_kernel,
        out_shape=shapes,
        compiler_params=pltpu.CompilerParams(vmem_limit_bytes=GRANT),
        cost_estimate=cost(1),
        name="edges",
    )(in_hbm(cot))


def spread_kernel(branch, cot_ref, left_ref, right_ref, *refs):
    out_ref = refs[-1]
    cols, chans, rows = cot_ref.shape[1:]
    lane = lax.broadcasted_iota(jnp.int32, (chans, rows), 1)
    dilation = DILATIONS[branch]
    for place in range(-dilation, cols + dilation):
        if place < 0:
            column = left_ref[place + dilation]
        elif place >= cols:
            column = right_ref[place - cols]
        else:
            column = cot_ref[0, place]
        wide = column.astype(jnp.float32)
        for lat_tap in range(3):
            shift = dilation * (lat_tap - 1)
            if shift == 0:
                moved = column
            else:
                keep = lane >= shift if shift > 0 else lane < rows + shift
                moved = jnp.where(keep, pltpu.roll(wide, shift % rows, 1), 0.0)
                moved = moved.astype(jnp.bfloat16)
            for lon_tap in range(3):
                target = place + dilation * (lon_tap - 1)
                if 0 <= target < cols:
                    tap = 3 * lat_tap + lon_tap
                    out_ref[
                        tap * chans : (tap + 1) * chans, target * rows : (target + 1) * rows
                    ] = moved


def spread(branch, cot, left, right, before=None):
    branches, cols, chans, rows = cot.shape
    operands = [cot, left, right] + ([] if before is None else [before])
    return pl.pallas_call(
        functools.partial(spread_kernel, branch),
        grid=(1,),
        in_specs=[
            pl.BlockSpec((1, cols, chans, rows), lambda k: (branch, 0, 0, 0)),
            pl.BlockSpec(left.shape, lambda k: (0, 0, 0)),
            pl.BlockSpec(right.shape, lambda k: (0, 0, 0)),
        ]
        + ([] if before is None else [pl.BlockSpec(memory_space=pl.ANY)]),
        out_specs=pl.BlockSpec((TAPS * chans, cols * rows), lambda k: (branch, 0)),
        out_shape=jax.ShapeDtypeStruct((branches * TAPS * chans, cols * rows), jnp.bfloat16),
        input_output_aliases={} if before is None else {3: 0},
        compiler_params=pltpu.CompilerParams(vmem_limit_bytes=GRANT),
        cost_estimate=cost(1),
        name="spread",
    )(*operands)


def flatten_kernel(place_ref, first_ref, second_ref, out_ref):
    cols, block, rows = first_ref.shape
    for ref, core in ((first_ref, place_ref[1]), (second_ref, 1 - place_ref[1])):
        at = pl.ds(pl.multiple_of(core * block, block), block)
        for col in range(cols):
            out_ref[col * rows : (col + 1) * rows, at] = jnp.transpose(ref[col])


def flatten(table, first, second):
    cols, block, rows = first.shape
    steps = 3
    each = cols // steps
    return pl.pallas_call(
        flatten_kernel,
        grid_spec=pltpu.PrefetchScalarGridSpec(
            num_scalar_prefetch=1,
            grid=(steps,),
            in_specs=[pl.BlockSpec((each, block, rows), lambda k, s: (k, 0, 0))] * 2,
            out_specs=pl.BlockSpec((each * rows, 2 * block), lambda k, s: (k, 0)),
        ),
        out_shape=jax.ShapeDtypeStruct((cols * rows, 2 * block), jnp.bfloat16),
        compiler_params=pltpu.CompilerParams(vmem_limit_bytes=GRANT),
        cost_estimate=cost(3),
        name="flatten",
    )(table, first, second)


def kernel_terms_kernel(count, sources, table_ref, grid_ref, *refs):
    feat_refs, (out_ref, top_ref) = refs[:-2], refs[-2:]
    chans = grid_ref.shape[0] // TAPS
    parts = count // GROUP
    height = chans // GROUP
    width = feat_refs[0].shape[1] // parts
    step = pl.program_id(0)

    @pl.when(step == 0)
    def _():
        top_ref[...] = jnp.full(top_ref.shape, TINY, jnp.float32)

    start = 0
    for feat_ref, steps in zip(feat_refs, sources):

        @pl.when((step >= start) & (step < start + steps))
        def _(feat_ref=feat_ref):
            sums = jnp.dot(grid_ref[...], feat_ref[...], preferred_element_type=jnp.float32)
            top_ref[...] = jnp.maximum(top_ref[...], jnp.max(jnp.abs(sums)))
            for owner in range(count):
                at = lax.rem(owner - table_ref[0] + count, count)
                top = (owner % GROUP) * height
                side = (owner // GROUP) * width
                for tap in range(TAPS):
                    low = tap * chans + top
                    out_ref[at, tap] = sums[low : low + height, side : side + width]

        start += steps


def kernel_terms(count, sources, table, grid, *feats):
    depth, wide = feats[0].shape
    steps = sum(sources)
    chans = grid.shape[0] // (3 * TAPS)
    shape = (count, steps * TAPS, chans // GROUP, wide // (count // GROUP))
    return pl.pallas_call(
        functools.partial(kernel_terms_kernel, count, sources),
        grid_spec=pltpu.PrefetchScalarGridSpec(
            num_scalar_prefetch=1,
            grid=(steps,),
            in_specs=[pl.BlockSpec((TAPS * chans, depth), lambda k, s: (jnp.minimum(k, 2), 0))]
            + [pl.BlockSpec((depth, wide), lambda k, s: (0, 0))] * len(feats),
            out_specs=[
                pl.BlockSpec((count, TAPS) + shape[2:], lambda k, s: (0, k, 0, 0)),
                pl.BlockSpec((1,) + shape[2:], lambda k, s: (0, 0, 0)),
            ],
        ),
        out_shape=[
            pltpu.HBM(shape, jnp.float32),
            jax.ShapeDtypeStruct((1,) + shape[2:], jnp.float32),
        ],
        compiler_params=pltpu.CompilerParams(vmem_limit_bytes=GRANT),
        cost_estimate=cost(6),
        name="kernel_terms",
    )(table, grid, *feats)


def input_terms_kernel(place_ref, weight_ref, grid_ref, *refs):
    out_ref = refs[-1]
    cols, block, rows = out_ref.shape
    sums = jnp.dot(weight_ref[...], grid_ref[...], preferred_element_type=jnp.float32)
    for col in range(cols):
        part = sums[:, col * rows : (col + 1) * rows]
        if len(refs) == 2:
            part = part + refs[0][col]
        out_ref[col] = part


def input_terms(at, table, weight_rows, grid, added=None, *, block, span, rows):
    first, cols = span
    depth = weight_rows.shape[1]
    each = 6 if cols % 6 == 0 and first % 6 == 0 else 3
    steps = cols // each
    skip = first // each
    wide = pl.BlockSpec((each, block, rows), lambda t, s: (t, 0, 0))
    operands = [weight_rows, grid] + ([] if added is None else [added])
    return pl.pallas_call(
        input_terms_kernel,
        grid_spec=pltpu.PrefetchScalarGridSpec(
            num_scalar_prefetch=1,
            grid=(steps,),
            in_specs=[
                pl.BlockSpec((block, depth), lambda t, s: (s[at], 0)),
                pl.BlockSpec((depth, each * rows), lambda t, s: (0, t + skip)),
            ]
            + (
                []
                if added is None
                else [pl.BlockSpec((each, block, rows), lambda t, s: (t + skip, 0, 0))]
            ),
            out_specs=wide,
        ),
        out_shape=jax.ShapeDtypeStruct((cols, block, rows), jnp.float32),
        compiler_params=pltpu.CompilerParams(vmem_limit_bytes=GRANT),
        cost_estimate=cost(3.5),
        name="input_terms",
    )(table, *operands)


def unfold_kernel(norm, blocks, table_ref, *refs):
    out_ref = refs[-1]
    taps = out_ref.shape[0]
    step = pl.program_id(0)
    for at in range(len(refs) - 1):

        @pl.when((step >= at * blocks) & (step < (at + 1) * blocks))
        def _(at=at):
            code_ref = refs[at]
            codes = code_ref[pl.ds((step - at * blocks) * taps, taps)]
            out_ref[...] = decode(codes, code_ref[blocks * taps :], norm)


def unfold(start, norm, blocks, shape, table, codes, before=None):
    taps = shape[0] // 3
    height, width = codes[0].shape[1:]
    operands = codes + ([] if before is None else [before])

    def place(j, s):
        return tuple(s[start + 3 * j + at] for at in range(3))

    def kernel(table_ref, *refs):
        refs = refs[: len(codes)] + refs[-1:]
        unfold_kernel(norm, blocks, table_ref, *refs)

    return pl.pallas_call(
        kernel,
        grid_spec=pltpu.PrefetchScalarGridSpec(
            num_scalar_prefetch=1,
            grid=(len(codes) * blocks,),
            in_specs=[pl.BlockSpec(codes[0].shape, lambda j, s: (0, 0, 0))] * len(codes)
            + ([] if before is None else [pl.BlockSpec(memory_space=pl.ANY)]),
            out_specs=pl.BlockSpec((taps, height, width), place),
        ),
        out_shape=jax.ShapeDtypeStruct(shape, jnp.float32),
        input_output_aliases={} if before is None else {len(operands): 0},
        compiler_params=pltpu.CompilerParams(vmem_limit_bytes=GRANT),
        cost_estimate=cost(3),
        name="unfold",
    )(table, *operands)


def first_hop_kernel(cut, terms_ref, top_ref, up_ref, down_ref):
    taps = terms_ref.shape[1]
    bound = bound_code(top_ref[...])
    up_ref[:cut] = encode(terms_ref[0, :cut], bound)
    up_ref[cut:] = bound
    down_ref[: taps - cut] = encode(terms_ref[0, cut:], bound)
    down_ref[taps - cut :] = bound


def next_hop_kernel(cut, up_ref, down_ref, to_up_ref, to_down_ref, top_ref, up_out, down_out):
    taps = to_up_ref.shape[1]
    top = top_ref[...]
    for ref, terms_ref, out_ref, low, high in (
        (up_ref, to_up_ref, up_out, 0, cut),
        (down_ref, to_down_ref, down_out, cut if cut < taps else 0, taps),
    ):
        arrived = ref[high - low :]
        bound = bound_code(arrived.astype(jnp.float32) + top)
        value = decode(ref[: high - low], arrived, 1.0 / REACH) + terms_ref[0, low:high]
        out_ref[low:high] = encode(value, bound)
        if low > 0:
            out_ref[:low] = encode(terms_ref[0, :low], bound)
        if high < taps:
            out_ref[high:taps] = encode(terms_ref[0, high:], bound)
        out_ref[taps:] = bound


def last_hop_kernel(up_ref, down_ref, top_ref, own_ref, out_ref):
    taps = own_ref.shape[1]
    up_bound, down_bound = up_ref[taps:], down_ref[taps:]
    bound = bound_code(
        up_bound.astype(jnp.float32) + down_bound.astype(jnp.float32) + top_ref[...]
    )
    value = own_ref[0] + decode(up_ref[:taps], up_bound, 1.0 / REACH)
    value = value + decode(down_ref[:taps], down_bound, 1.0 / REACH)
    out_ref[:taps] = encode(value, bound)
    out_ref[taps:] = bound


def chunk_spec(terms, at):
    return pl.BlockSpec((1,) + terms.shape[1:], lambda i: (at, 0, 0, 0))


def whole_spec(array):
    return pl.BlockSpec(array.shape, lambda i: (0,) * array.ndim)


def hop_call(kernel, out_rows, operands, specs, name):
    tail = operands[-1].shape[-2:]
    shapes = [jax.ShapeDtypeStruct((rows,) + tail, jnp.bfloat16) for rows in out_rows]
    return pl.pallas_call(
        kernel,
        grid=(1,),
        in_specs=specs,
        out_specs=[whole_spec(shape) for shape in shapes],
        out_shape=shapes,
        compiler_params=pltpu.CompilerParams(vmem_limit_bytes=GRANT),
        cost_estimate=cost(2),
        name=name,
    )(*operands)


class Order:
    def __init__(self):
        self.last = ()

    def gate(self, *values):
        if not self.last:
            return values
        return lax.optimization_barrier(values + self.last)[: len(values)]

    def pin(self, *values):
        values = self.gate(*values)
        self.last = (values[0],)
        return values

    def __call__(self, kernel, *values):
        result = kernel(*self.gate(*values))
        self.last = (jax.tree.leaves(result)[0],)
        return result


class Ring:
    def __init__(self, count, taps):
        order = ring_order(count)
        self.ahead = [(order[i], order[(i + 1) % count]) for i in range(count)]
        self.behind = [(b, a) for a, b in self.ahead]
        self.count, self.half = count, count // 2
        self.taps, self.cut = taps, (taps + 1) // 2

    def send(self, messages):
        up, down = messages
        return lax.ppermute(up, "lon", self.ahead), lax.ppermute(down, "lon", self.behind)

    def first(self, terms, top):
        return hop_call(
            functools.partial(first_hop_kernel, self.cut),
            [self.cut + 1, self.taps - self.cut + 1],
            [in_hbm(terms), top],
            [chunk_spec(terms, self.half), whole_spec(top)],
            "first_hop",
        )

    def next(self, left, messages, terms, top):
        up, down = messages
        cut = self.cut if left == self.half else self.taps
        return hop_call(
            functools.partial(next_hop_kernel, cut),
            [self.taps + 1] * 2,
            [up, down, in_hbm(terms), in_hbm(terms), top],
            [
                whole_spec(up),
                whole_spec(down),
                chunk_spec(terms, left - 1),
                chunk_spec(terms, self.count - left + 1),
                whole_spec(top),
            ],
            "next_hop",
        )

    def last(self, messages, terms, top):
        up, down = messages
        return hop_call(
            last_hop_kernel,
            [self.taps + 1],
            [up, down, top, in_hbm(terms)],
            [whole_spec(up), whole_spec(down), whole_spec(top), chunk_spec(terms, 0)],
            "last_hop",
        )[0]


class Chain:
    def __init__(self, order, count, places, terms, top):
        self.ring = Ring(count, terms.shape[1])
        self.order, self.places = order, places
        self.terms, self.top, self.left = terms, top, self.ring.half
        self.out = order(self.ring.first, terms, top)
        self.codes = []

    def arrive(self):
        self.out = self.order.pin(*self.ring.send(self.out))

    def hop(self):
        run = functools.partial(self.ring.next, self.left)
        self.out = self.order(run, self.out, self.terms, self.top)
        self.left -= 1

    def last(self):
        own = self.order(self.ring.last, self.out, self.terms, self.top)
        self.out = (own, own)
        self.keep(own)

    def keep(self, code):
        self.codes.append(code)

    def take(self):
        codes, self.codes = self.codes, []
        places, blocks = self.places, self.ring.taps // TAPS
        self.places += 3 * len(codes) * blocks
        return places, blocks, codes

    def move(self):
        ring, (up, down) = self.ring, self.out
        if self.left < ring.half:
            self.out = self.order.pin(*ring.send((up, down)))
            self.keep(self.out[0])
            self.keep(self.out[1])
        else:
            cut = ring.cut
            parts = self.order.pin(*ring.send((up[:cut], down[cut:])))
            self.keep(jnp.concatenate(parts, axis=0))
        self.left += 1


PARTS = (((0, 0), (1, 0)), ((0, 1), (1, 1), (2, 1), (2, 0)))


def chunk_order(count):
    aheads = [0]
    for step in range(1, count // 2):
        aheads += [count - step, step]
    return aheads + [count // 2]


def make_table(lon, ch, count):
    place_x, place_core = ch // 2, ch % 2
    spot = ring_position(lon, count)
    entries = [
        (branch, ahead, side)
        for part in PARTS
        for ahead in chunk_order(count)
        for branch, side in part
    ]
    branches, aheads, sides = (np.array(column, np.int32) for column in zip(*entries))
    owners = (spot + aheads) % count
    side = jnp.where(sides == 0, place_x, 1 - place_x) * (count // GROUP)
    places = jnp.stack([jnp.asarray(branches), owners % GROUP, owners // GROUP + side], axis=1)
    head = jnp.stack([spot, place_core, 3 - ch, ch ^ 2, ch ^ 1, ch])
    return jnp.concatenate([head, places.reshape(-1)]).astype(jnp.int32)


def local(features, cotangent, weights):
    block, _, cols, rows = features.shape
    chans = cotangent.shape[1]
    total = weights.shape[4]
    count = lax.axis_size("lon")
    half = count // 2
    cells = cols * count * rows

    feat = jnp.transpose(features.reshape(block, cols, rows), (1, 0, 2))
    cot = jnp.transpose(cotangent.reshape(3, chans, cols, rows), (0, 2, 1, 3))
    order = Order()
    to_core = [(i, i ^ 1) for i in range(4)]
    to_x = [(i, i ^ 2) for i in range(4)]
    to_right = [(i, (i + 1) % count) for i in range(count)]
    to_left = [((i + 1) % count, i) for i in range(count)]

    rims = order(edges, cot)
    halos = [
        (lax.ppermute(rims[2 * k], "lon", to_right), lax.ppermute(rims[2 * k + 1], "lon", to_left))
        for k in range(3)
    ]
    far = lax.ppermute(feat, "ch", to_x)

    norm = 1.0 / (REACH * cells**0.5)
    table = order(
        functools.partial(make_table, count=count), lax.axis_index("lon"), lax.axis_index("ch")
    )
    near = lax.ppermute(order.gate(feat)[0], "ch", to_core)
    weight_rows = order(jnp.transpose, weights.reshape(-1, total))
    flat_near = order(flatten, table, feat, near)

    def terms_of(which, span, *added):
        run = functools.partial(
            input_terms, BLOCKS_AT + which, block=block, span=span, rows=rows
        )
        return order(run, table, weight_rows, grid, *added)

    spans = [(cols * at // 3, cols // 3) for at in range(3)]
    whole = (0, cols)
    shape = (3 * TAPS, chans, total)
    written = []
    places = [BLOCKS_AT + 4, BLOCKS_AT + 4 + 3 * count * len(PARTS[0])]

    def write(chain):
        start, blocks, codes = chain.take()
        run = functools.partial(unfold, start, norm, blocks, shape)
        written[:] = [order(run, table, codes, *written)]

    grid = order(functools.partial(spread, 0), cot, *order.pin(*halos[0]))
    grid = order(functools.partial(spread, 1), cot, *order.pin(*halos[1]), grid)
    terms = order(functools.partial(kernel_terms, count, (2,)), table, grid, flat_near)
    a = Chain(order, count, places[0], *terms)
    far = order.pin(far)[0]
    far_near = lax.ppermute(far, "ch", to_core)
    a.arrive()
    a.hop()
    grid = order(functools.partial(spread, 2), cot, *order.pin(*halos[2]), grid)
    away = terms_of(0, whole)
    flat_far = order(flatten, table, far, far_near)
    away = lax.ppermute(away, "ch", to_core)
    terms = order(functools.partial(kernel_terms, count, (3, 1)), table, grid, flat_far, flat_near)
    b = Chain(order, count, places[1], *terms)
    a.arrive()
    a.hop()
    across = [terms_of(1, span, away) for span in spans]
    b.arrive()
    b.hop()
    across[0] = lax.ppermute(order.gate(across[0])[0], "ch", to_x)
    a.arrive()
    a.hop()
    for _ in range(half - 4):
        b.arrive()
        b.hop()
        a.arrive()
        a.hop()
    beside = terms_of(2, whole)
    b.arrive()
    b.hop()
    across[1:] = [lax.ppermute(part, "ch", to_x) for part in order.gate(*across[1:])]
    a.arrive()
    a.last()
    mine = terms_of(3, whole)
    across[0] = order.pin(across[0])[0]
    b.arrive()
    b.hop()
    a.move()
    beside = lax.ppermute(order.gate(beside)[0], "ch", to_core)
    a.move()
    write(a)
    b.arrive()
    b.last()
    across[1] = order.pin(across[1])[0]
    a.move()
    for _ in range(half - 4):
        a.move()
    write(a)
    a.move()
    b.move()
    write(a)
    b.move()
    write(b)
    for _ in range(half - 4):
        b.move()
    b.move()
    write(b)
    across = jnp.concatenate(across, axis=0)
    input_grad = order(lambda *parts: sum(parts).astype(jnp.bfloat16), mine, beside, across)
    b.move()
    write(b)
    kernel_grad = written[0]

    input_grad = jnp.transpose(input_grad, (1, 0, 2)).reshape(block, 1, cols, rows)
    return (input_grad, kernel_grad.reshape(3, 3, 3, chans, total))


def solution(mesh):
    return jax.shard_map(
        local,
        mesh=mesh,
        in_specs=(
            P("ch", None, "lon", None),
            P(None, "ch", None, "lon", None),
            P(None, None, None, "ch", None),
        ),
        out_specs=(P("ch", None, "lon", None), P(None, None, None, "ch", None)),
        check_vma=False,
    )
```

```python
import functools

import jax
import jax.numpy as jnp
from jax import lax
from jax.experimental import pallas as pl
from jax.experimental.pallas import tpu as pltpu
from jax.sharding import PartitionSpec as P

DILATIONS = (6, 12, 18)
TAPS = 9
GROUP = 8
REACH = 2.0**15.5
TINY = 1e-30
LEAST = 2.0**-125
MIB = 1024 * 1024
GRANT = 16 * MIB
PACE = 3e8
BLOCKS_AT = 2
ROWS_AT = 6


def cost(micros):
    return pl.CostEstimate(flops=int(micros * PACE), bytes_accessed=0, transcendentals=0)


def in_hbm(value):
    return pltpu.with_memory_space_constraint(value, pltpu.HBM)


def ring_order(count):
    return list(range(0, count, 2)) + list(range(count - 1, 0, -2))


def ring_position(index, count):
    return jnp.where(index % 2 == 0, index // 2, count - 1 - index // 2)


def bound_code(bound):
    return (bound * 1.01).astype(jnp.bfloat16)


def encode(value, bound):
    power = value * (REACH / bound.astype(jnp.float32))
    power = power * power
    power = power * power
    power = power * power
    return jnp.where(value < 0, -power, power).astype(jnp.bfloat16)


def decode(code, bound, norm):
    wide = code.astype(jnp.float32)
    fourth = lax.rsqrt(lax.rsqrt(jnp.maximum(jnp.abs(wide), LEAST)))
    root = fourth * lax.rsqrt(fourth) * (bound.astype(jnp.float32) * norm)
    return jnp.where(wide < 0, -root, root)


def direct(kernel, out_shapes, operands, name, table=None, micros=2):
    vmem = pl.BlockSpec(memory_space=pltpu.VMEM)
    smem = pl.BlockSpec(memory_space=pltpu.SMEM)
    return pl.pallas_call(
        kernel,
        in_specs=([] if table is None else [smem]) + [vmem] * len(operands),
        out_specs=[vmem] * len(out_shapes),
        out_shape=out_shapes,
        compiler_params=pltpu.CompilerParams(vmem_limit_bytes=GRANT),
        cost_estimate=cost(micros),
        name=name,
    )(*([] if table is None else [table]), *operands)


def edge_kernel(cot_ref, tail_ref, head_ref):
    cols = cot_ref.shape[1]
    start = 0
    for branch in range(3):
        dilation = DILATIONS[branch]
        tail_ref[start : start + dilation] = cot_ref[branch, cols - dilation :]
        head_ref[start : start + dilation] = cot_ref[branch, :dilation]
        start += dilation


def edges(cot):
    shape = (sum(DILATIONS),) + cot.shape[2:]
    return pl.pallas_call(
        edge_kernel,
        grid=(1,),
        in_specs=[pl.BlockSpec(cot.shape, lambda i: (0, 0, 0, 0))],
        out_specs=[pl.BlockSpec(shape, lambda i: (0, 0, 0))] * 2,
        out_shape=[jax.ShapeDtypeStruct(shape, cot.dtype)] * 2,
        compiler_params=pltpu.CompilerParams(vmem_limit_bytes=GRANT),
        cost_estimate=cost(1),
        name="edges",
    )(in_hbm(cot))


def spread_kernel(cot_ref, left_ref, right_ref, out_ref):
    cols, chans, rows = cot_ref.shape[1:]
    lane = lax.broadcasted_iota(jnp.int32, (chans, rows), 1)
    start = 0
    for branch in range(3):
        dilation = DILATIONS[branch]
        for place in range(-dilation, cols + dilation):
            if place < 0:
                column = left_ref[start + place + dilation]
            elif place >= cols:
                column = right_ref[start + place - cols]
            else:
                column = cot_ref[branch, place]
            wide = column.astype(jnp.float32)
            for lat_tap in range(3):
                shift = dilation * (lat_tap - 1)
                if shift == 0:
                    moved = column
                else:
                    keep = lane >= shift if shift > 0 else lane < rows + shift
                    moved = jnp.where(keep, pltpu.roll(wide, shift % rows, 1), 0.0)
                    moved = moved.astype(jnp.bfloat16)
                for lon_tap in range(3):
                    target = place + dilation * (lon_tap - 1)
                    if 0 <= target < cols:
                        low = (TAPS * branch + 3 * lat_tap + lon_tap) * chans
                        out_ref[low : low + chans, target * rows : (target + 1) * rows] = moved
        start += dilation


def spread(cot, left, right):
    branches, cols, chans, rows = cot.shape
    shape = jax.ShapeDtypeStruct((branches * TAPS * chans, cols * rows), jnp.bfloat16)
    return direct(spread_kernel, [shape], [cot, left, right], "spread")[0]


def flatten_kernel(place_ref, first_ref, second_ref, out_ref):
    cols, block, rows = first_ref.shape
    for ref, core in ((first_ref, place_ref[1]), (second_ref, 1 - place_ref[1])):
        at = pl.ds(pl.multiple_of(core * block, block), block)
        for col in range(cols):
            out_ref[col * rows : (col + 1) * rows, at] = jnp.transpose(ref[col])


def flatten(table, first, second):
    cols, block, rows = first.shape
    shape = jax.ShapeDtypeStruct((cols * rows, 2 * block), jnp.bfloat16)
    return direct(flatten_kernel, [shape], [first, second], "flatten", table)[0]


def kernel_terms_kernel(count, table_ref, grid_ref, feat_ref, out_ref, top_ref):
    chans = grid_ref.shape[0] // (3 * TAPS)
    parts = count // GROUP
    height = chans // GROUP
    width = feat_ref.shape[1] // parts
    deep = TAPS * chans
    top_ref[...] = jnp.full(top_ref.shape, TINY, jnp.float32)

    @pl.loop(0, 3)
    def _(branch):
        lines = grid_ref[pl.ds(pl.multiple_of(branch * deep, deep), deep)]
        sums = jnp.dot(lines, feat_ref[...], preferred_element_type=jnp.float32)
        top_ref[...] = jnp.maximum(top_ref[...], jnp.max(jnp.abs(sums)))
        for owner in range(count):
            at = lax.rem(owner - table_ref[0] + count, count)
            top = (owner % GROUP) * height
            side = (owner // GROUP) * width
            for tap in range(TAPS):
                low = tap * chans + top
                out_ref[at, branch * TAPS + tap] = sums[low : low + height, side : side + width]


def kernel_terms(table, grid, feat, count):
    wide = feat.shape[1]
    taps = 3 * TAPS
    tail = (grid.shape[0] // taps // GROUP, wide // (count // GROUP))
    shapes = [
        jax.ShapeDtypeStruct((count, taps) + tail, jnp.float32),
        jax.ShapeDtypeStruct((1,) + tail, jnp.float32),
    ]
    kernel = functools.partial(kernel_terms_kernel, count)
    return direct(kernel, shapes, [grid, feat], "kernel_terms", table, 6)


def input_terms_kernel(at, first, table_ref, weight_ref, grid_ref, *refs):
    out_ref = refs[-1]
    cols, block, rows = out_ref.shape
    each = 6 if cols % 6 == 0 else 3
    lines = pl.ds(pl.multiple_of(table_ref[at] * block, block), block)

    @pl.loop(0, cols // each)
    def _(step):
        wide = each * rows
        here = pl.ds(pl.multiple_of(step * wide + first * rows, rows), wide)
        sums = jnp.dot(weight_ref[lines], grid_ref[:, here], preferred_element_type=jnp.float32)
        for col in range(each):
            part = sums[:, col * rows : (col + 1) * rows]
            if len(refs) == 2:
                part = part + refs[0][first + step * each + col]
            out_ref[step * each + col] = part


def input_terms(at, table, weight_rows, grid, added=None, *, block, span, rows):
    first, cols = span
    shape = jax.ShapeDtypeStruct((cols, block, rows), jnp.float32)
    operands = [weight_rows, grid] + ([] if added is None else [added])
    kernel = functools.partial(input_terms_kernel, at, first)
    return direct(kernel, [shape], operands, "input_terms", table, 3.5)[0]


def unfold_kernel(norm, held, table_ref, *refs):
    out_ref = refs[-1]
    taps = out_ref.shape[0]
    for at in range(held):

        @pl.when(pl.program_id(0) == at)
        def _(code_ref=refs[at]):
            out_ref[...] = decode(code_ref[:taps], code_ref[taps:], norm)


def unfold(places, norm, shape, table, codes, before=None):
    held = len(codes)
    taps = shape[0]
    height, width = codes[0].shape[1:]
    operands = codes + ([] if before is None else [before])

    def pick(j, values):
        chosen = values[0]
        for k in range(1, held):
            chosen = jnp.where(j == k, values[k], chosen)
        return chosen

    def place(j, s):
        row, col = (pick(j, [place[at] for place in places]) for at in range(2))
        return (0, s[row], s[col])

    return pl.pallas_call(
        functools.partial(unfold_kernel, norm, held),
        grid_spec=pltpu.PrefetchScalarGridSpec(
            num_scalar_prefetch=1,
            grid=(held,),
            in_specs=[pl.BlockSpec(codes[0].shape, lambda j, s: (0, 0, 0))] * held
            + ([] if before is None else [pl.BlockSpec(memory_space=pl.ANY)]),
            out_specs=pl.BlockSpec((taps, height, width), place),
        ),
        out_shape=jax.ShapeDtypeStruct(shape, jnp.float32),
        input_output_aliases={} if before is None else {held + 1: 0},
        compiler_params=pltpu.CompilerParams(vmem_limit_bytes=GRANT),
        cost_estimate=cost(3),
        name="unfold",
    )(table, *operands)


def first_hop_kernel(cut, at, terms_ref, top_ref, up_ref, down_ref):
    taps = terms_ref.shape[1]
    bound = bound_code(top_ref[...])
    up_ref[:cut] = encode(terms_ref[at, :cut], bound)
    up_ref[cut:] = bound
    down_ref[: taps - cut] = encode(terms_ref[at, cut:], bound)
    down_ref[taps - cut :] = bound


def next_hop_kernel(cut, to_up, to_down, up_ref, down_ref, terms_ref, top_ref, up_out, down_out):
    taps = terms_ref.shape[1]
    top = top_ref[...]
    for ref, at, out_ref, low, high in (
        (up_ref, to_up, up_out, 0, cut),
        (down_ref, to_down, down_out, cut if cut < taps else 0, taps),
    ):
        arrived = ref[high - low :]
        bound = bound_code(arrived.astype(jnp.float32) + top)
        value = decode(ref[: high - low], arrived, 1.0 / REACH) + terms_ref[at, low:high]
        out_ref[low:high] = encode(value, bound)
        if low > 0:
            out_ref[:low] = encode(terms_ref[at, :low], bound)
        if high < taps:
            out_ref[high:taps] = encode(terms_ref[at, high:], bound)
        out_ref[taps:] = bound


def last_hop_kernel(up_ref, down_ref, own_ref, top_ref, out_ref):
    taps = own_ref.shape[1]
    up_bound, down_bound = up_ref[taps:], down_ref[taps:]
    bound = bound_code(
        up_bound.astype(jnp.float32) + down_bound.astype(jnp.float32) + top_ref[...]
    )
    value = own_ref[0] + decode(up_ref[:taps], up_bound, 1.0 / REACH)
    value = value + decode(down_ref[:taps], down_bound, 1.0 / REACH)
    out_ref[:taps] = encode(value, bound)
    out_ref[taps:] = bound


def hop_call(kernel, out_rows, operands, name):
    tail = operands[-1].shape[-2:]
    shapes = [jax.ShapeDtypeStruct((rows,) + tail, jnp.bfloat16) for rows in out_rows]
    return direct(kernel, shapes, operands, name)


class Order:
    def __init__(self):
        self.last = ()

    def gate(self, *values):
        if not self.last:
            return values
        return lax.optimization_barrier(values + self.last)[: len(values)]

    def pin(self, *values):
        values = self.gate(*values)
        self.last = (values[0],)
        return values

    def __call__(self, kernel, *values):
        result = kernel(*self.gate(*values))
        self.last = (jax.tree.leaves(result)[0],)
        return result


class Ring:
    def __init__(self, count, taps):
        order = ring_order(count)
        self.ahead = [(order[i], order[(i + 1) % count]) for i in range(count)]
        self.behind = [(b, a) for a, b in self.ahead]
        self.count, self.half = count, count // 2
        self.taps, self.cut = taps, (taps + 1) // 2

    def send(self, messages):
        up, down = messages
        return lax.ppermute(up, "lon", self.ahead), lax.ppermute(down, "lon", self.behind)

    def first(self, terms, top):
        kernel = functools.partial(first_hop_kernel, self.cut, self.half)
        rows = [self.cut + 1, self.taps - self.cut + 1]
        return hop_call(kernel, rows, [terms, top], "first_hop")

    def next(self, left, messages, terms, top):
        cut = self.cut if left == self.half else self.taps
        kernel = functools.partial(next_hop_kernel, cut, left - 1, self.count - left + 1)
        return hop_call(kernel, [self.taps + 1] * 2, [*messages, terms, top], "next_hop")

    def last(self, messages, terms, top):
        return hop_call(last_hop_kernel, [self.taps + 1], [*messages, terms, top], "last_hop")[0]


class Chain:
    def __init__(self, ring, order, side, terms, top):
        self.ring, self.order, self.side = ring, order, side
        self.terms, self.top, self.left = terms, top, ring.half
        self.out = order(ring.first, terms, top)
        self.codes = []

    def arrive(self):
        self.out = self.order.pin(*self.ring.send(self.out))

    def hop(self):
        run = functools.partial(self.ring.next, self.left)
        self.out = self.order(run, self.out, self.terms, self.top)
        self.left -= 1

    def last(self):
        own = self.order(self.ring.last, self.out, self.terms, self.top)
        self.out = (own, own)
        self.keep(0, own)

    def keep(self, ahead, code):
        count = self.ring.count
        self.codes.append(
            ((ROWS_AT + ahead, ROWS_AT + count + 2 * ahead + self.side), code)
        )

    def take(self):
        taken, self.codes = self.codes, []
        return taken

    def move(self):
        ring, (up, down) = self.ring, self.out
        if self.left < ring.half:
            self.out = self.order.pin(*ring.send((up, down)))
            self.keep(ring.count - self.left, self.out[0])
            self.keep(self.left, self.out[1])
        else:
            cut = ring.cut
            parts = self.order.pin(*ring.send((up[:cut], down[cut:])))
            self.keep(ring.half, jnp.concatenate(parts, axis=0))
        self.left += 1


def make_table(lon, ch, count):
    place_x, place_core = ch // 2, ch % 2
    spot = ring_position(lon, count)
    owners = (spot + jnp.arange(count, dtype=jnp.int32)) % count
    sides = jnp.stack([place_x, 1 - place_x]) * (count // GROUP)
    return jnp.concatenate(
        [
            jnp.stack([spot, place_core, 3 - ch, ch ^ 2, ch ^ 1, ch]),
            owners % GROUP,
            (owners[:, None] // GROUP + sides[None]).reshape(-1),
        ]
    ).astype(jnp.int32)


def local(features, cotangent, weights):
    block, _, cols, rows = features.shape
    chans = cotangent.shape[1]
    total = weights.shape[4]
    count = lax.axis_size("lon")
    cells = cols * count * rows

    feat = jnp.transpose(features.reshape(block, cols, rows), (1, 0, 2))
    cot = jnp.transpose(cotangent.reshape(3, chans, cols, rows), (0, 2, 1, 3))
    order = Order()

    tails, heads = order(edges, cot)
    left = lax.ppermute(tails, "lon", [(i, (i + 1) % count) for i in range(count)])
    right = lax.ppermute(heads, "lon", [((i + 1) % count, i) for i in range(count)])

    to_core = [(i, i ^ 1) for i in range(4)]
    to_x = [(i, i ^ 2) for i in range(4)]
    far = lax.ppermute(feat, "ch", to_x)

    norm = 1.0 / (REACH * cells**0.5)
    ring = Ring(count, 3 * TAPS)
    weight_rows = order(jnp.transpose, weights.reshape(-1, total))
    near = lax.ppermute(order.gate(feat)[0], "ch", to_core)
    table = order(
        functools.partial(make_table, count=count), lax.axis_index("lon"), lax.axis_index("ch")
    )
    flat_near = order(flatten, table, feat, near)
    left, right, far = order.gate(left, right, far)
    grid = order(spread, cot, left, right)
    far_near = lax.ppermute(far, "ch", to_core)

    def terms_of(which, span, *added):
        run = functools.partial(
            input_terms, BLOCKS_AT + which, block=block, span=span, rows=rows
        )
        return order(run, table, weight_rows, grid, *added)

    def features_with(flat):
        return order(functools.partial(kernel_terms, count=count), table, grid, flat)

    half = ring.half
    spans = [(cols * at // 3, cols // 3) for at in range(3)]
    whole = (0, cols)
    shape = (3 * TAPS, chans, total)
    written = []

    def write(*chains):
        taken = [item for chain in chains for item in chain.take()]
        places, codes = zip(*taken)
        run = functools.partial(unfold, places, norm, shape)
        written[:] = [order(run, table, list(codes), *written)]

    near = Chain(ring, order, 0, *features_with(flat_near))
    flat_far = order(flatten, table, far, far_near)
    away = terms_of(0, whole)
    near.arrive()
    near.hop()
    away = lax.ppermute(order.gate(away)[0], "ch", to_core)
    far = Chain(ring, order, 1, *features_with(flat_far))
    near.arrive()
    near.hop()
    across = [terms_of(1, span, away) for span in spans]
    far.arrive()
    far.hop()
    across[0] = lax.ppermute(order.gate(across[0])[0], "ch", to_x)
    near.arrive()
    near.hop()
    for _ in range(half - 4):
        far.arrive()
        far.hop()
        near.arrive()
        near.hop()
    beside = terms_of(2, whole)
    far.arrive()
    far.hop()
    across[1:] = [lax.ppermute(part, "ch", to_x) for part in order.gate(*across[1:])]
    near.arrive()
    near.last()
    mine = terms_of(3, whole)
    far.arrive()
    across[0] = order.pin(across[0])[0]
    far.hop()
    near.move()
    beside = lax.ppermute(order.gate(beside)[0], "ch", to_core)
    far.arrive()
    far.last()
    near.move()
    write(near)
    far.move()
    across[1] = order.pin(across[1])[0]
    near.move()
    for _ in range(half - 4):
        near.move()
        far.move()
    write(near, far)
    near.move()
    far.move()
    write(near, far)
    far.move()
    write(far)
    across = jnp.concatenate(across, axis=0)
    input_grad = order(lambda *parts: sum(parts).astype(jnp.bfloat16), mine, beside, across)
    far.move()
    write(far)
    kernel_grad = written[0]

    input_grad = jnp.transpose(input_grad, (1, 0, 2)).reshape(block, 1, cols, rows)
    return (input_grad, kernel_grad.reshape(3, 3, 3, chans, total))


def solution(mesh):
    return jax.shard_map(
        local,
        mesh=mesh,
        in_specs=(
            P("ch", None, "lon", None),
            P(None, "ch", None, "lon", None),
            P(None, None, None, "ch", None),
        ),
        out_specs=(P("ch", None, "lon", None), P(None, None, None, "ch", None)),
        check_vma=False,
    )
```

```python
import functools

import jax
import jax.numpy as jnp
from jax import lax
from jax.experimental import pallas as pl
from jax.experimental.pallas import tpu as pltpu
from jax.sharding import PartitionSpec as P

DILATIONS = (6, 12, 18)
TAPS = 9
GROUP = 8
REACH = 2.0**15.5
TINY = 1e-30
LEAST = 2.0**-125
MIB = 1024 * 1024
GRANT = 16 * MIB
PACE = 3e8
BLOCKS_AT = 2
ROWS_AT = 6


def cost(micros):
    return pl.CostEstimate(flops=int(micros * PACE), bytes_accessed=0, transcendentals=0)


def in_hbm(value):
    return pltpu.with_memory_space_constraint(value, pltpu.HBM)


def ring_order(count):
    return list(range(0, count, 2)) + list(range(count - 1, 0, -2))


def ring_position(index, count):
    return jnp.where(index % 2 == 0, index // 2, count - 1 - index // 2)


def bound_code(bound):
    return (bound * 1.01).astype(jnp.bfloat16)


def encode(value, bound):
    power = value * (REACH / bound.astype(jnp.float32))
    power = power * power
    power = power * power
    power = power * power
    return jnp.where(value < 0, -power, power).astype(jnp.bfloat16)


def decode(code, bound, norm):
    wide = code.astype(jnp.float32)
    fourth = lax.rsqrt(lax.rsqrt(jnp.maximum(jnp.abs(wide), LEAST)))
    root = fourth * lax.rsqrt(fourth) * (bound.astype(jnp.float32) * norm)
    return jnp.where(wide < 0, -root, root)


def direct(kernel, out_shapes, operands, name, table=None, micros=2):
    vmem = pl.BlockSpec(memory_space=pltpu.VMEM)
    smem = pl.BlockSpec(memory_space=pltpu.SMEM)
    return pl.pallas_call(
        kernel,
        in_specs=([] if table is None else [smem]) + [vmem] * len(operands),
        out_specs=[vmem] * len(out_shapes),
        out_shape=out_shapes,
        compiler_params=pltpu.CompilerParams(vmem_limit_bytes=GRANT),
        cost_estimate=cost(micros),
        name=name,
    )(*([] if table is None else [table]), *operands)


def edge_kernel(cot_ref, tail_ref, head_ref):
    cols = cot_ref.shape[1]
    start = 0
    for branch in range(3):
        dilation = DILATIONS[branch]
        tail_ref[start : start + dilation] = cot_ref[branch, cols - dilation :]
        head_ref[start : start + dilation] = cot_ref[branch, :dilation]
        start += dilation


def edges(cot):
    shape = (sum(DILATIONS),) + cot.shape[2:]
    return pl.pallas_call(
        edge_kernel,
        grid=(1,),
        in_specs=[pl.BlockSpec(cot.shape, lambda i: (0, 0, 0, 0))],
        out_specs=[pl.BlockSpec(shape, lambda i: (0, 0, 0))] * 2,
        out_shape=[jax.ShapeDtypeStruct(shape, cot.dtype)] * 2,
        compiler_params=pltpu.CompilerParams(vmem_limit_bytes=GRANT),
        cost_estimate=cost(1),
        name="edges",
    )(in_hbm(cot))


def spread_kernel(cot_ref, left_ref, right_ref, out_ref):
    cols, chans, rows = cot_ref.shape[1:]
    lane = lax.broadcasted_iota(jnp.int32, (chans, rows), 1)
    start = 0
    for branch in range(3):
        dilation = DILATIONS[branch]
        for place in range(-dilation, cols + dilation):
            if place < 0:
                column = left_ref[start + place + dilation]
            elif place >= cols:
                column = right_ref[start + place - cols]
            else:
                column = cot_ref[branch, place]
            wide = column.astype(jnp.float32)
            for lat_tap in range(3):
                shift = dilation * (lat_tap - 1)
                if shift == 0:
                    moved = column
                else:
                    keep = lane >= shift if shift > 0 else lane < rows + shift
                    moved = jnp.where(keep, pltpu.roll(wide, shift % rows, 1), 0.0)
                    moved = moved.astype(jnp.bfloat16)
                for lon_tap in range(3):
                    target = place + dilation * (lon_tap - 1)
                    if 0 <= target < cols:
                        low = (TAPS * branch + 3 * lat_tap + lon_tap) * chans
                        out_ref[low : low + chans, target * rows : (target + 1) * rows] = moved
        start += dilation


def spread(cot, left, right):
    branches, cols, chans, rows = cot.shape
    shape = jax.ShapeDtypeStruct((branches * TAPS * chans, cols * rows), jnp.bfloat16)
    return direct(spread_kernel, [shape], [cot, left, right], "spread")[0]


def flatten_kernel(place_ref, first_ref, second_ref, out_ref):
    cols, block, rows = first_ref.shape
    for ref, core in ((first_ref, place_ref[1]), (second_ref, 1 - place_ref[1])):
        at = pl.ds(pl.multiple_of(core * block, block), block)
        for col in range(cols):
            out_ref[col * rows : (col + 1) * rows, at] = jnp.transpose(ref[col])


def flatten(table, first, second):
    cols, block, rows = first.shape
    shape = jax.ShapeDtypeStruct((cols * rows, 2 * block), jnp.bfloat16)
    return direct(flatten_kernel, [shape], [first, second], "flatten", table)[0]


def kernel_terms_kernel(count, table_ref, grid_ref, feat_ref, out_ref, top_ref):
    chans = grid_ref.shape[0] // (3 * TAPS)
    parts = count // GROUP
    height = chans // GROUP
    width = feat_ref.shape[1] // parts
    deep = TAPS * chans
    top_ref[...] = jnp.full(top_ref.shape, TINY, jnp.float32)

    @pl.loop(0, 3)
    def _(branch):
        lines = grid_ref[pl.ds(pl.multiple_of(branch * deep, deep), deep)]
        sums = jnp.dot(lines, feat_ref[...], preferred_element_type=jnp.float32)
        top_ref[...] = jnp.maximum(top_ref[...], jnp.max(jnp.abs(sums)))
        for owner in range(count):
            at = lax.rem(owner - table_ref[0] + count, count)
            top = (owner % GROUP) * height
            side = (owner // GROUP) * width
            for tap in range(TAPS):
                low = tap * chans + top
                out_ref[at, branch * TAPS + tap] = sums[low : low + height, side : side + width]


def kernel_terms(table, grid, feat, count):
    wide = feat.shape[1]
    taps = 3 * TAPS
    tail = (grid.shape[0] // taps // GROUP, wide // (count // GROUP))
    shapes = [
        jax.ShapeDtypeStruct((count, taps) + tail, jnp.float32),
        jax.ShapeDtypeStruct((1,) + tail, jnp.float32),
    ]
    kernel = functools.partial(kernel_terms_kernel, count)
    return direct(kernel, shapes, [grid, feat], "kernel_terms", table, 6)


def input_terms_kernel(at, table_ref, weight_ref, grid_ref, added_ref, *out_refs):
    block, rows = out_refs[0].shape[1:]
    lines = weight_ref[pl.ds(pl.multiple_of(table_ref[at] * block, block), block)]
    done = 0
    for out_ref in out_refs:
        each = max(cols for cols in range(1, 7) if out_ref.shape[0] % cols == 0)
        for start in range(0, out_ref.shape[0], each):
            here = slice((done + start) * rows, (done + start + each) * rows)
            sums = jnp.dot(lines, grid_ref[:, here], preferred_element_type=jnp.float32)
            for col in range(each):
                part = sums[:, col * rows : (col + 1) * rows]
                if added_ref is not None:
                    part = part + added_ref[done + start + col]
                out_ref[start + col] = part
        done += out_ref.shape[0]


def input_terms(at, table, weight_rows, grid, added=None, *, block, spans, rows):
    shapes = [jax.ShapeDtypeStruct((cols, block, rows), jnp.float32) for cols in spans]
    operands = [weight_rows, grid] + ([] if added is None else [added])

    def kernel(table_ref, weight_ref, grid_ref, *refs):
        added_ref, out_refs = (None, refs) if added is None else (refs[0], refs[1:])
        input_terms_kernel(at, table_ref, weight_ref, grid_ref, added_ref, *out_refs)

    return direct(kernel, shapes, operands, "input_terms", table, 3.5)


def unfold_kernel(norm, places, table_ref, *refs):
    held = len(places)
    codes, (out_ref, plain_ref, sems) = refs[:held], refs[-3:]
    taps, height, width = plain_ref.shape[1:]
    copies = []
    for at, (row, col) in enumerate(places):
        plain_ref[at] = decode(codes[at][:taps], codes[at][taps:], norm)
        top = pl.ds(pl.multiple_of(table_ref[row] * height, height), height)
        side = pl.ds(pl.multiple_of(table_ref[col] * width, width), width)
        copies.append(
            pltpu.make_async_copy(plain_ref.at[at], out_ref.at[:, top, side], sems.at[at])
        )
        copies[-1].start()
    for copy in copies:
        copy.wait()


def unfold(places, norm, shape, table, codes, before=None):
    held = len(codes)
    vmem = pl.BlockSpec(memory_space=pltpu.VMEM)
    hbm = pl.BlockSpec(memory_space=pl.ANY)
    operands = codes + ([] if before is None else [before])
    return pl.pallas_call(
        functools.partial(unfold_kernel, norm, places),
        in_specs=[pl.BlockSpec(memory_space=pltpu.SMEM)]
        + [vmem] * held
        + ([] if before is None else [hbm]),
        out_specs=hbm,
        out_shape=pltpu.HBM(shape, jnp.float32),
        input_output_aliases={} if before is None else {held + 1: 0},
        scratch_shapes=[
            pltpu.VMEM((held, shape[0]) + codes[0].shape[1:], jnp.float32),
            pltpu.SemaphoreType.DMA((held,)),
        ],
        compiler_params=pltpu.CompilerParams(vmem_limit_bytes=GRANT),
        cost_estimate=cost(3),
        name="unfold",
    )(table, *operands)


def first_hop_kernel(cut, at, terms_ref, top_ref, up_ref, down_ref):
    taps = terms_ref.shape[1]
    bound = bound_code(top_ref[...])
    up_ref[:cut] = encode(terms_ref[at, :cut], bound)
    up_ref[cut:] = bound
    down_ref[: taps - cut] = encode(terms_ref[at, cut:], bound)
    down_ref[taps - cut :] = bound


def next_hop_kernel(cut, to_up, to_down, up_ref, down_ref, terms_ref, top_ref, up_out, down_out):
    taps = terms_ref.shape[1]
    top = top_ref[...]
    for ref, at, out_ref, low, high in (
        (up_ref, to_up, up_out, 0, cut),
        (down_ref, to_down, down_out, cut if cut < taps else 0, taps),
    ):
        arrived = ref[high - low :]
        bound = bound_code(arrived.astype(jnp.float32) + top)
        value = decode(ref[: high - low], arrived, 1.0 / REACH) + terms_ref[at, low:high]
        out_ref[low:high] = encode(value, bound)
        if low > 0:
            out_ref[:low] = encode(terms_ref[at, :low], bound)
        if high < taps:
            out_ref[high:taps] = encode(terms_ref[at, high:], bound)
        out_ref[taps:] = bound


def last_hop_kernel(up_ref, down_ref, own_ref, top_ref, out_ref):
    taps = own_ref.shape[1]
    up_bound, down_bound = up_ref[taps:], down_ref[taps:]
    bound = bound_code(
        up_bound.astype(jnp.float32) + down_bound.astype(jnp.float32) + top_ref[...]
    )
    value = own_ref[0] + decode(up_ref[:taps], up_bound, 1.0 / REACH)
    value = value + decode(down_ref[:taps], down_bound, 1.0 / REACH)
    out_ref[:taps] = encode(value, bound)
    out_ref[taps:] = bound


def hop_call(kernel, out_rows, operands, name):
    tail = operands[-1].shape[-2:]
    shapes = [jax.ShapeDtypeStruct((rows,) + tail, jnp.bfloat16) for rows in out_rows]
    return direct(kernel, shapes, operands, name)


class Order:
    def __init__(self):
        self.last = ()

    def gate(self, *values):
        if not self.last:
            return values
        return lax.optimization_barrier(values + self.last)[: len(values)]

    def pin(self, *values):
        values = self.gate(*values)
        self.last = (values[0],)
        return values

    def __call__(self, kernel, *values):
        result = kernel(*self.gate(*values))
        self.last = (jax.tree.leaves(result)[0],)
        return result


class Ring:
    def __init__(self, count, taps):
        order = ring_order(count)
        self.ahead = [(order[i], order[(i + 1) % count]) for i in range(count)]
        self.behind = [(b, a) for a, b in self.ahead]
        self.count, self.half = count, count // 2
        self.taps, self.cut = taps, (taps + 1) // 2

    def send(self, messages):
        up, down = messages
        return lax.ppermute(up, "lon", self.ahead), lax.ppermute(down, "lon", self.behind)

    def first(self, terms, top):
        kernel = functools.partial(first_hop_kernel, self.cut, self.half)
        rows = [self.cut + 1, self.taps - self.cut + 1]
        return hop_call(kernel, rows, [terms, top], "first_hop")

    def next(self, left, messages, terms, top):
        cut = self.cut if left == self.half else self.taps
        kernel = functools.partial(next_hop_kernel, cut, left - 1, self.count - left + 1)
        return hop_call(kernel, [self.taps + 1] * 2, [*messages, terms, top], "next_hop")

    def last(self, messages, terms, top):
        return hop_call(last_hop_kernel, [self.taps + 1], [*messages, terms, top], "last_hop")[0]


class Chain:
    def __init__(self, ring, order, side, terms, top):
        self.ring, self.order, self.side = ring, order, side
        self.terms, self.top, self.left = terms, top, ring.half
        self.out = order(ring.first, terms, top)
        self.codes = []

    def arrive(self):
        self.out = self.order.pin(*self.ring.send(self.out))

    def hop(self):
        run = functools.partial(self.ring.next, self.left)
        self.out = self.order(run, self.out, self.terms, self.top)
        self.left -= 1

    def last(self):
        own = self.order(self.ring.last, self.out, self.terms, self.top)
        self.out = (own, own)
        self.keep(0, own)

    def keep(self, ahead, code):
        count = self.ring.count
        self.codes.append(
            ((ROWS_AT + ahead, ROWS_AT + count + 2 * ahead + self.side), code)
        )

    def take(self):
        taken, self.codes = self.codes, []
        return taken

    def move(self):
        ring, (up, down) = self.ring, self.out
        if self.left < ring.half:
            self.out = self.order.pin(*ring.send((up, down)))
            self.keep(ring.count - self.left, self.out[0])
            self.keep(self.left, self.out[1])
        else:
            cut = ring.cut
            parts = self.order.pin(*ring.send((up[:cut], down[cut:])))
            self.keep(ring.half, jnp.concatenate(parts, axis=0))
        self.left += 1


def make_table(lon, ch, count):
    place_x, place_core = ch // 2, ch % 2
    spot = ring_position(lon, count)
    owners = (spot + jnp.arange(count, dtype=jnp.int32)) % count
    sides = jnp.stack([place_x, 1 - place_x]) * (count // GROUP)
    return jnp.concatenate(
        [
            jnp.stack([spot, place_core, 3 - ch, ch ^ 2, ch ^ 1, ch]),
            owners % GROUP,
            (owners[:, None] // GROUP + sides[None]).reshape(-1),
        ]
    ).astype(jnp.int32)


def local(features, cotangent, weights):
    block, _, cols, rows = features.shape
    chans = cotangent.shape[1]
    total = weights.shape[4]
    count = lax.axis_size("lon")
    cells = cols * count * rows

    feat = jnp.transpose(features.reshape(block, cols, rows), (1, 0, 2))
    cot = jnp.transpose(cotangent.reshape(3, chans, cols, rows), (0, 2, 1, 3))
    order = Order()

    tails, heads = order(edges, cot)
    left = lax.ppermute(tails, "lon", [(i, (i + 1) % count) for i in range(count)])
    right = lax.ppermute(heads, "lon", [((i + 1) % count, i) for i in range(count)])

    to_core = [(i, i ^ 1) for i in range(4)]
    to_x = [(i, i ^ 2) for i in range(4)]
    far = lax.ppermute(feat, "ch", to_x)
    near = lax.ppermute(feat, "ch", to_core)

    norm = 1.0 / (REACH * cells**0.5)
    ring = Ring(count, 3 * TAPS)
    table = order(
        functools.partial(make_table, count=count), lax.axis_index("lon"), lax.axis_index("ch")
    )
    weight_rows = order(jnp.transpose, weights.reshape(-1, total))
    flat_near = order(flatten, table, feat, near)
    left, right, far = order.gate(left, right, far)
    grid = order(spread, cot, left, right)
    far_near = lax.ppermute(far, "ch", to_core)

    def terms_of(which, spans, *added):
        run = functools.partial(
            input_terms, BLOCKS_AT + which, block=block, spans=spans, rows=rows
        )
        return order(run, table, weight_rows, grid, *added)

    def features_with(flat):
        return order(functools.partial(kernel_terms, count=count), table, grid, flat)

    half = ring.half
    most, whole = (cols * 5 // 6, cols // 6), (cols,)
    shape = (3 * TAPS, chans, total)
    written = []

    def write(*chains):
        taken = [item for chain in chains for item in chain.take()]
        places, codes = zip(*taken)
        run = functools.partial(unfold, places, norm, shape)
        written[:] = [order(run, table, list(codes), *written)]

    near = Chain(ring, order, 0, *features_with(flat_near))
    flat_far = order(flatten, table, far, far_near)
    (away,) = terms_of(0, whole)
    near.arrive()
    near.hop()
    away = lax.ppermute(order.gate(away)[0], "ch", to_core)
    far = Chain(ring, order, 1, *features_with(flat_far))
    across = list(terms_of(1, most, away))
    near.arrive()
    near.hop()
    far.arrive()
    far.hop()
    across[0] = lax.ppermute(order.gate(across[0])[0], "ch", to_x)
    (beside,) = terms_of(2, whole)
    for _ in range(half - 4):
        near.arrive()
        near.hop()
        far.arrive()
        far.hop()
    near.arrive()
    near.hop()
    far.arrive()
    far.hop()
    (mine,) = terms_of(3, whole)
    near.arrive()
    near.last()
    far.arrive()
    far.hop()
    near.move()
    far.arrive()
    far.last()
    write(near)
    near.move()
    far.move()
    for _ in range(half - 4):
        near.move()
        far.move()
    write(near, far)
    near.move()
    far.move()
    across[0] = order.pin(across[0])[0]
    across[1] = lax.ppermute(order.gate(across[1])[0], "ch", to_x)
    write(near, far)
    near.move()
    beside = lax.ppermute(order.gate(beside)[0], "ch", to_core)
    far.move()
    write(near, far)
    across = jnp.concatenate(across, axis=0)
    input_grad = order(lambda *parts: sum(parts).astype(jnp.bfloat16), mine, beside, across)
    far.move()
    write(far)
    kernel_grad = written[0]

    input_grad = jnp.transpose(input_grad, (1, 0, 2)).reshape(block, 1, cols, rows)
    return (input_grad, kernel_grad.reshape(3, 3, 3, chans, total))


def solution(mesh):
    return jax.shard_map(
        local,
        mesh=mesh,
        in_specs=(
            P("ch", None, "lon", None),
            P(None, "ch", None, "lon", None),
            P(None, None, None, "ch", None),
        ),
        out_specs=(P("ch", None, "lon", None), P(None, None, None, "ch", None)),
        check_vma=False,
    )
```

```python
import functools

import jax
import jax.numpy as jnp
from jax import lax
from jax.experimental import pallas as pl
from jax.experimental.pallas import tpu as pltpu
from jax.sharding import PartitionSpec as P

DILATIONS = (6, 12, 18)
TAPS = 9
GROUP = 8
REACH = 2.0**15.5
TINY = 1e-30
LEAST = 2.0**-125
MIB = 1024 * 1024
GRANT = 16 * MIB
PACE = 3e8
BLOCKS_AT = 2
ROWS_AT = 6


def cost(micros):
    return pl.CostEstimate(flops=int(micros * PACE), bytes_accessed=0, transcendentals=0)


def in_hbm(value):
    return pltpu.with_memory_space_constraint(value, pltpu.HBM)


def ring_order(count):
    return list(range(0, count, 2)) + list(range(count - 1, 0, -2))


def ring_position(index, count):
    return jnp.where(index % 2 == 0, index // 2, count - 1 - index // 2)


def bound_code(bound):
    return (bound * 1.01).astype(jnp.bfloat16)


def encode(value, bound):
    power = value * (REACH / bound.astype(jnp.float32))
    power = power * power
    power = power * power
    power = power * power
    return jnp.where(value < 0, -power, power).astype(jnp.bfloat16)


def decode(code, bound, norm):
    wide = code.astype(jnp.float32)
    fourth = lax.rsqrt(lax.rsqrt(jnp.maximum(jnp.abs(wide), LEAST)))
    root = fourth * lax.rsqrt(fourth) * (bound.astype(jnp.float32) * norm)
    return jnp.where(wide < 0, -root, root)


def direct(kernel, out_shapes, operands, name, table=None, micros=2):
    vmem = pl.BlockSpec(memory_space=pltpu.VMEM)
    smem = pl.BlockSpec(memory_space=pltpu.SMEM)
    return pl.pallas_call(
        kernel,
        in_specs=([] if table is None else [smem]) + [vmem] * len(operands),
        out_specs=[vmem] * len(out_shapes),
        out_shape=out_shapes,
        compiler_params=pltpu.CompilerParams(vmem_limit_bytes=GRANT),
        cost_estimate=cost(micros),
        name=name,
    )(*([] if table is None else [table]), *operands)


def edge_kernel(cot_ref, tail_ref, head_ref):
    cols = cot_ref.shape[1]
    start = 0
    for branch in range(3):
        dilation = DILATIONS[branch]
        tail_ref[start : start + dilation] = cot_ref[branch, cols - dilation :]
        head_ref[start : start + dilation] = cot_ref[branch, :dilation]
        start += dilation


def edges(cot):
    shape = (sum(DILATIONS),) + cot.shape[2:]
    return pl.pallas_call(
        edge_kernel,
        grid=(1,),
        in_specs=[pl.BlockSpec(cot.shape, lambda i: (0, 0, 0, 0))],
        out_specs=[pl.BlockSpec(shape, lambda i: (0, 0, 0))] * 2,
        out_shape=[jax.ShapeDtypeStruct(shape, cot.dtype)] * 2,
        compiler_params=pltpu.CompilerParams(vmem_limit_bytes=GRANT),
        cost_estimate=cost(1),
        name="edges",
    )(in_hbm(cot))


def spread_kernel(cot_ref, left_ref, right_ref, out_ref):
    cols, chans, rows = cot_ref.shape[1:]
    lane = lax.broadcasted_iota(jnp.int32, (chans, rows), 1)
    start = 0
    for branch in range(3):
        dilation = DILATIONS[branch]
        for place in range(-dilation, cols + dilation):
            if place < 0:
                column = left_ref[start + place + dilation]
            elif place >= cols:
                column = right_ref[start + place - cols]
            else:
                column = cot_ref[branch, place]
            wide = column.astype(jnp.float32)
            for lat_tap in range(3):
                shift = dilation * (lat_tap - 1)
                if shift == 0:
                    moved = column
                else:
                    keep = lane >= shift if shift > 0 else lane < rows + shift
                    moved = jnp.where(keep, pltpu.roll(wide, shift % rows, 1), 0.0)
                    moved = moved.astype(jnp.bfloat16)
                for lon_tap in range(3):
                    target = place + dilation * (lon_tap - 1)
                    if 0 <= target < cols:
                        low = (TAPS * branch + 3 * lat_tap + lon_tap) * chans
                        out_ref[low : low + chans, target * rows : (target + 1) * rows] = moved
        start += dilation


def spread(cot, left, right):
    branches, cols, chans, rows = cot.shape
    shape = jax.ShapeDtypeStruct((branches * TAPS * chans, cols * rows), jnp.bfloat16)
    return direct(spread_kernel, [shape], [cot, left, right], "spread")[0]


def flatten_kernel(place_ref, first_ref, second_ref, out_ref):
    cols, block, rows = first_ref.shape
    for ref, core in ((first_ref, place_ref[1]), (second_ref, 1 - place_ref[1])):
        at = pl.ds(pl.multiple_of(core * block, block), block)
        for col in range(cols):
            out_ref[col * rows : (col + 1) * rows, at] = jnp.transpose(ref[col])


def flatten(table, first, second):
    cols, block, rows = first.shape
    shape = jax.ShapeDtypeStruct((cols * rows, 2 * block), jnp.bfloat16)
    return direct(flatten_kernel, [shape], [first, second], "flatten", table)[0]


def kernel_terms_kernel(count, table_ref, grid_ref, feat_ref, out_ref, top_ref):
    chans = grid_ref.shape[0] // (3 * TAPS)
    parts = count // GROUP
    height = chans // GROUP
    width = feat_ref.shape[1] // parts
    deep = TAPS * chans
    top_ref[...] = jnp.full(top_ref.shape, TINY, jnp.float32)

    @pl.loop(0, 3)
    def _(branch):
        lines = grid_ref[pl.ds(pl.multiple_of(branch * deep, deep), deep)]
        sums = jnp.dot(lines, feat_ref[...], preferred_element_type=jnp.float32)
        top_ref[...] = jnp.maximum(top_ref[...], jnp.max(jnp.abs(sums)))
        for owner in range(count):
            at = lax.rem(owner - table_ref[0] + count, count)
            top = (owner % GROUP) * height
            side = (owner // GROUP) * width
            for tap in range(TAPS):
                low = tap * chans + top
                out_ref[at, branch * TAPS + tap] = sums[low : low + height, side : side + width]


def kernel_terms(table, grid, feat, count):
    wide = feat.shape[1]
    taps = 3 * TAPS
    tail = (grid.shape[0] // taps // GROUP, wide // (count // GROUP))
    shapes = [
        jax.ShapeDtypeStruct((count, taps) + tail, jnp.float32),
        jax.ShapeDtypeStruct((1,) + tail, jnp.float32),
    ]
    kernel = functools.partial(kernel_terms_kernel, count)
    return direct(kernel, shapes, [grid, feat], "kernel_terms", table, 6)


def input_terms_kernel(at, table_ref, weight_ref, grid_ref, added_ref, *out_refs):
    block, rows = out_refs[0].shape[1:]
    lines = weight_ref[pl.ds(pl.multiple_of(table_ref[at] * block, block), block)]
    done = 0
    for out_ref in out_refs:
        each = max(cols for cols in range(1, 7) if out_ref.shape[0] % cols == 0)
        for start in range(0, out_ref.shape[0], each):
            here = slice((done + start) * rows, (done + start + each) * rows)
            sums = jnp.dot(lines, grid_ref[:, here], preferred_element_type=jnp.float32)
            for col in range(each):
                part = sums[:, col * rows : (col + 1) * rows]
                if added_ref is not None:
                    part = part + added_ref[done + start + col]
                out_ref[start + col] = part
        done += out_ref.shape[0]


def input_terms(at, table, weight_rows, grid, added=None, *, block, spans, rows):
    shapes = [jax.ShapeDtypeStruct((cols, block, rows), jnp.float32) for cols in spans]
    operands = [weight_rows, grid] + ([] if added is None else [added])

    def kernel(table_ref, weight_ref, grid_ref, *refs):
        added_ref, out_refs = (None, refs) if added is None else (refs[0], refs[1:])
        input_terms_kernel(at, table_ref, weight_ref, grid_ref, added_ref, *out_refs)

    return direct(kernel, shapes, operands, "input_terms", table, 3.5)


def unfold_kernel(norm, places, table_ref, *refs):
    held = len(places)
    codes, (out_ref, plain_ref, sems) = refs[:held], refs[-3:]
    taps, height, width = plain_ref.shape[1:]
    copies = []
    for at, (row, col) in enumerate(places):
        plain_ref[at] = decode(codes[at][:taps], codes[at][taps:], norm)
        top = pl.ds(pl.multiple_of(table_ref[row] * height, height), height)
        side = pl.ds(pl.multiple_of(table_ref[col] * width, width), width)
        copies.append(
            pltpu.make_async_copy(plain_ref.at[at], out_ref.at[:, top, side], sems.at[at])
        )
        copies[-1].start()
    for copy in copies:
        copy.wait()


def unfold(places, norm, shape, table, codes, before=None):
    held = len(codes)
    vmem = pl.BlockSpec(memory_space=pltpu.VMEM)
    hbm = pl.BlockSpec(memory_space=pl.ANY)
    operands = codes + ([] if before is None else [before])
    return pl.pallas_call(
        functools.partial(unfold_kernel, norm, places),
        in_specs=[pl.BlockSpec(memory_space=pltpu.SMEM)]
        + [vmem] * held
        + ([] if before is None else [hbm]),
        out_specs=hbm,
        out_shape=pltpu.HBM(shape, jnp.float32),
        input_output_aliases={} if before is None else {held + 1: 0},
        scratch_shapes=[
            pltpu.VMEM((held, shape[0]) + codes[0].shape[1:], jnp.float32),
            pltpu.SemaphoreType.DMA((held,)),
        ],
        compiler_params=pltpu.CompilerParams(vmem_limit_bytes=GRANT),
        cost_estimate=cost(3),
        name="unfold",
    )(table, *operands)


def first_hop_kernel(cut, at, terms_ref, top_ref, up_ref, down_ref):
    taps = terms_ref.shape[1]
    bound = bound_code(top_ref[...])
    up_ref[:cut] = encode(terms_ref[at, :cut], bound)
    up_ref[cut:] = bound
    down_ref[: taps - cut] = encode(terms_ref[at, cut:], bound)
    down_ref[taps - cut :] = bound


def next_hop_kernel(cut, to_up, to_down, up_ref, down_ref, terms_ref, top_ref, up_out, down_out):
    taps = terms_ref.shape[1]
    top = top_ref[...]
    for ref, at, out_ref, low, high in (
        (up_ref, to_up, up_out, 0, cut),
        (down_ref, to_down, down_out, cut if cut < taps else 0, taps),
    ):
        arrived = ref[high - low :]
        bound = bound_code(arrived.astype(jnp.float32) + top)
        value = decode(ref[: high - low], arrived, 1.0 / REACH) + terms_ref[at, low:high]
        out_ref[low:high] = encode(value, bound)
        if low > 0:
            out_ref[:low] = encode(terms_ref[at, :low], bound)
        if high < taps:
            out_ref[high:taps] = encode(terms_ref[at, high:], bound)
        out_ref[taps:] = bound


def last_hop_kernel(up_ref, down_ref, own_ref, top_ref, out_ref):
    taps = own_ref.shape[1]
    up_bound, down_bound = up_ref[taps:], down_ref[taps:]
    bound = bound_code(
        up_bound.astype(jnp.float32) + down_bound.astype(jnp.float32) + top_ref[...]
    )
    value = own_ref[0] + decode(up_ref[:taps], up_bound, 1.0 / REACH)
    value = value + decode(down_ref[:taps], down_bound, 1.0 / REACH)
    out_ref[:taps] = encode(value, bound)
    out_ref[taps:] = bound


def hop_call(kernel, out_rows, operands, name):
    tail = operands[-1].shape[-2:]
    shapes = [jax.ShapeDtypeStruct((rows,) + tail, jnp.bfloat16) for rows in out_rows]
    return direct(kernel, shapes, operands, name)


class Order:
    def __init__(self):
        self.last = ()

    def gate(self, *values):
        if not self.last:
            return values
        return lax.optimization_barrier(values + self.last)[: len(values)]

    def pin(self, *values):
        values = self.gate(*values)
        self.last = (values[0],)
        return values

    def __call__(self, kernel, *values):
        result = kernel(*self.gate(*values))
        self.last = (jax.tree.leaves(result)[0],)
        return result


class Ring:
    def __init__(self, count, taps):
        order = ring_order(count)
        self.ahead = [(order[i], order[(i + 1) % count]) for i in range(count)]
        self.behind = [(b, a) for a, b in self.ahead]
        self.count, self.half = count, count // 2
        self.taps, self.cut = taps, (taps + 1) // 2

    def send(self, messages):
        up, down = messages
        return lax.ppermute(up, "lon", self.ahead), lax.ppermute(down, "lon", self.behind)

    def first(self, terms, top):
        kernel = functools.partial(first_hop_kernel, self.cut, self.half)
        rows = [self.cut + 1, self.taps - self.cut + 1]
        return hop_call(kernel, rows, [terms, top], "first_hop")

    def next(self, left, messages, terms, top):
        cut = self.cut if left == self.half else self.taps
        kernel = functools.partial(next_hop_kernel, cut, left - 1, self.count - left + 1)
        return hop_call(kernel, [self.taps + 1] * 2, [*messages, terms, top], "next_hop")

    def last(self, messages, terms, top):
        return hop_call(last_hop_kernel, [self.taps + 1], [*messages, terms, top], "last_hop")[0]


class Chain:
    def __init__(self, ring, order, side, terms, top):
        self.ring, self.order, self.side = ring, order, side
        self.terms, self.top, self.left = terms, top, ring.half
        self.out = order(ring.first, terms, top)
        self.codes = []

    def arrive(self):
        self.out = self.order.pin(*self.ring.send(self.out))

    def hop(self):
        run = functools.partial(self.ring.next, self.left)
        self.out = self.order(run, self.out, self.terms, self.top)
        self.left -= 1

    def last(self):
        own = self.order(self.ring.last, self.out, self.terms, self.top)
        self.out = (own, own)
        self.keep(0, own)

    def keep(self, ahead, code):
        count = self.ring.count
        self.codes.append(
            ((ROWS_AT + ahead, ROWS_AT + count + 2 * ahead + self.side), code)
        )

    def take(self):
        taken, self.codes = self.codes, []
        return taken

    def move(self):
        ring, (up, down) = self.ring, self.out
        if self.left < ring.half:
            self.out = self.order.pin(*ring.send((up, down)))
            self.keep(ring.count - self.left, self.out[0])
            self.keep(self.left, self.out[1])
        else:
            cut = ring.cut
            parts = self.order.pin(*ring.send((up[:cut], down[cut:])))
            self.keep(ring.half, jnp.concatenate(parts, axis=0))
        self.left += 1


def make_table(lon, ch, count):
    place_x, place_core = ch // 2, ch % 2
    spot = ring_position(lon, count)
    owners = (spot + jnp.arange(count, dtype=jnp.int32)) % count
    sides = jnp.stack([place_x, 1 - place_x]) * (count // GROUP)
    return jnp.concatenate(
        [
            jnp.stack([spot, place_core, 3 - ch, ch ^ 2, ch ^ 1, ch]),
            owners % GROUP,
            (owners[:, None] // GROUP + sides[None]).reshape(-1),
        ]
    ).astype(jnp.int32)


def local(features, cotangent, weights):
    block, _, cols, rows = features.shape
    chans = cotangent.shape[1]
    total = weights.shape[4]
    count = lax.axis_size("lon")
    cells = cols * count * rows

    feat = jnp.transpose(features.reshape(block, cols, rows), (1, 0, 2))
    cot = jnp.transpose(cotangent.reshape(3, chans, cols, rows), (0, 2, 1, 3))
    order = Order()

    tails, heads = order(edges, cot)
    left = lax.ppermute(tails, "lon", [(i, (i + 1) % count) for i in range(count)])
    right = lax.ppermute(heads, "lon", [((i + 1) % count, i) for i in range(count)])

    to_core = [(i, i ^ 1) for i in range(4)]
    to_x = [(i, i ^ 2) for i in range(4)]
    far = lax.ppermute(feat, "ch", to_x)
    near = lax.ppermute(feat, "ch", to_core)

    norm = 1.0 / (REACH * cells**0.5)
    ring = Ring(count, 3 * TAPS)
    table = order(
        functools.partial(make_table, count=count), lax.axis_index("lon"), lax.axis_index("ch")
    )
    weight_rows = order(jnp.transpose, weights.reshape(-1, total))
    flat_near = order(flatten, table, feat, near)
    left, right, far = order.gate(left, right, far)
    grid = order(spread, cot, left, right)
    far_near = lax.ppermute(far, "ch", to_core)

    def terms_of(which, spans, *added):
        run = functools.partial(
            input_terms, BLOCKS_AT + which, block=block, spans=spans, rows=rows
        )
        return order(run, table, weight_rows, grid, *added)

    def features_with(flat):
        return order(functools.partial(kernel_terms, count=count), table, grid, flat)

    half = ring.half
    most, whole = (cols * 5 // 6, cols // 6), (cols,)
    shape = (3 * TAPS, chans, total)
    written = []

    def write(*chains):
        taken = [item for chain in chains for item in chain.take()]
        places, codes = zip(*taken)
        run = functools.partial(unfold, places, norm, shape)
        written[:] = [order(run, table, list(codes), *written)]

    near = Chain(ring, order, 0, *features_with(flat_near))
    flat_far = order(flatten, table, far, far_near)
    (away,) = terms_of(0, whole)
    near.arrive()
    near.hop()
    away = lax.ppermute(order.gate(away)[0], "ch", to_core)
    far = Chain(ring, order, 1, *features_with(flat_far))
    across = list(terms_of(1, most, away))
    near.arrive()
    near.hop()
    far.arrive()
    far.hop()
    across[0] = lax.ppermute(order.gate(across[0])[0], "ch", to_x)
    (beside,) = terms_of(2, whole)
    for _ in range(half - 4):
        near.arrive()
        near.hop()
        far.arrive()
        far.hop()
    near.arrive()
    near.hop()
    far.arrive()
    far.hop()
    (mine,) = terms_of(3, whole)
    near.arrive()
    near.last()
    far.arrive()
    far.hop()
    near.move()
    far.arrive()
    far.last()
    write(near)
    near.move()
    far.move()
    for _ in range(half - 4):
        near.move()
        far.move()
    write(near, far)
    near.move()
    far.move()
    across[0] = order.pin(across[0])[0]
    across[1] = lax.ppermute(order.gate(across[1])[0], "ch", to_x)
    write(near, far)
    far.move()
    near.move()
    beside = lax.ppermute(order.gate(beside)[0], "ch", to_core)
    write(near, far)
    across = jnp.concatenate(across, axis=0)
    input_grad = order(lambda *parts: sum(parts).astype(jnp.bfloat16), mine, beside, across)
    far.move()
    write(far)
    kernel_grad = written[0]

    input_grad = jnp.transpose(input_grad, (1, 0, 2)).reshape(block, 1, cols, rows)
    return (input_grad, kernel_grad.reshape(3, 3, 3, chans, total))


def solution(mesh):
    return jax.shard_map(
        local,
        mesh=mesh,
        in_specs=(
            P("ch", None, "lon", None),
            P(None, "ch", None, "lon", None),
            P(None, None, None, "ch", None),
        ),
        out_specs=(P("ch", None, "lon", None), P(None, None, None, "ch", None)),
        check_vma=False,
    )
```

```python
import functools

import jax
import jax.numpy as jnp
from jax import lax
from jax.experimental import pallas as pl
from jax.experimental.pallas import tpu as pltpu
from jax.sharding import PartitionSpec as P

DILATIONS = (6, 12, 18)
TAPS = 9
GROUP = 8
REACH = 2.0**15.5
TINY = 1e-30
LEAST = 2.0**-125
MIB = 1024 * 1024
GRANT = 16 * MIB
PACE = 3e8
BLOCKS_AT = 2
ROWS_AT = 6


def cost(micros):
    return pl.CostEstimate(flops=int(micros * PACE), bytes_accessed=0, transcendentals=0)


def in_hbm(value):
    return pltpu.with_memory_space_constraint(value, pltpu.HBM)


def ring_order(count):
    return list(range(0, count, 2)) + list(range(count - 1, 0, -2))


def ring_position(index, count):
    return jnp.where(index % 2 == 0, index // 2, count - 1 - index // 2)


def bound_code(bound):
    return (bound * 1.01).astype(jnp.bfloat16)


def encode(value, bound):
    power = value * (REACH / bound.astype(jnp.float32))
    power = power * power
    power = power * power
    power = power * power
    return jnp.where(value < 0, -power, power).astype(jnp.bfloat16)


def decode(code, bound, norm):
    wide = code.astype(jnp.float32)
    fourth = lax.rsqrt(lax.rsqrt(jnp.maximum(jnp.abs(wide), LEAST)))
    root = fourth * lax.rsqrt(fourth) * (bound.astype(jnp.float32) * norm)
    return jnp.where(wide < 0, -root, root)


def direct(kernel, out_shapes, operands, name, table=None, micros=2):
    vmem = pl.BlockSpec(memory_space=pltpu.VMEM)
    smem = pl.BlockSpec(memory_space=pltpu.SMEM)
    return pl.pallas_call(
        kernel,
        in_specs=([] if table is None else [smem]) + [vmem] * len(operands),
        out_specs=[vmem] * len(out_shapes),
        out_shape=out_shapes,
        compiler_params=pltpu.CompilerParams(vmem_limit_bytes=GRANT),
        cost_estimate=cost(micros),
        name=name,
    )(*([] if table is None else [table]), *operands)


def edge_kernel(cot_ref, tail_ref, head_ref):
    cols = cot_ref.shape[1]
    start = 0
    for branch in range(3):
        dilation = DILATIONS[branch]
        tail_ref[start : start + dilation] = cot_ref[branch, cols - dilation :]
        head_ref[start : start + dilation] = cot_ref[branch, :dilation]
        start += dilation


def edges(cot):
    shape = (sum(DILATIONS),) + cot.shape[2:]
    return pl.pallas_call(
        edge_kernel,
        grid=(1,),
        in_specs=[pl.BlockSpec(cot.shape, lambda i: (0, 0, 0, 0))],
        out_specs=[pl.BlockSpec(shape, lambda i: (0, 0, 0))] * 2,
        out_shape=[jax.ShapeDtypeStruct(shape, cot.dtype)] * 2,
        compiler_params=pltpu.CompilerParams(vmem_limit_bytes=GRANT),
        cost_estimate=cost(1),
        name="edges",
    )(in_hbm(cot))


def spread_kernel(cot_ref, left_ref, right_ref, out_ref):
    cols, chans, rows = cot_ref.shape[1:]
    lane = lax.broadcasted_iota(jnp.int32, (chans, rows), 1)
    start = 0
    for branch in range(3):
        dilation = DILATIONS[branch]
        for place in range(-dilation, cols + dilation):
            if place < 0:
                column = left_ref[start + place + dilation]
            elif place >= cols:
                column = right_ref[start + place - cols]
            else:
                column = cot_ref[branch, place]
            wide = column.astype(jnp.float32)
            for lat_tap in range(3):
                shift = dilation * (lat_tap - 1)
                if shift == 0:
                    moved = column
                else:
                    keep = lane >= shift if shift > 0 else lane < rows + shift
                    moved = jnp.where(keep, pltpu.roll(wide, shift % rows, 1), 0.0)
                    moved = moved.astype(jnp.bfloat16)
                for lon_tap in range(3):
                    target = place + dilation * (lon_tap - 1)
                    if 0 <= target < cols:
                        low = (TAPS * branch + 3 * lat_tap + lon_tap) * chans
                        out_ref[low : low + chans, target * rows : (target + 1) * rows] = moved
        start += dilation


def spread(cot, left, right):
    branches, cols, chans, rows = cot.shape
    shape = jax.ShapeDtypeStruct((branches * TAPS * chans, cols * rows), jnp.bfloat16)
    return direct(spread_kernel, [shape], [cot, left, right], "spread")[0]


def flatten_kernel(place_ref, first_ref, second_ref, out_ref):
    cols, block, rows = first_ref.shape
    for ref, core in ((first_ref, place_ref[1]), (second_ref, 1 - place_ref[1])):
        at = pl.ds(pl.multiple_of(core * block, block), block)
        for col in range(cols):
            out_ref[col * rows : (col + 1) * rows, at] = jnp.transpose(ref[col])


def flatten(table, first, second):
    cols, block, rows = first.shape
    shape = jax.ShapeDtypeStruct((cols * rows, 2 * block), jnp.bfloat16)
    return direct(flatten_kernel, [shape], [first, second], "flatten", table)[0]


def kernel_terms_kernel(count, table_ref, grid_ref, feat_ref, out_ref, top_ref):
    chans = grid_ref.shape[0] // (3 * TAPS)
    parts = count // GROUP
    height = chans // GROUP
    width = feat_ref.shape[1] // parts
    deep = TAPS * chans
    top_ref[...] = jnp.full(top_ref.shape, TINY, jnp.float32)

    @pl.loop(0, 3)
    def _(branch):
        lines = grid_ref[pl.ds(pl.multiple_of(branch * deep, deep), deep)]
        sums = jnp.dot(lines, feat_ref[...], preferred_element_type=jnp.float32)
        top_ref[...] = jnp.maximum(top_ref[...], jnp.max(jnp.abs(sums)))
        for owner in range(count):
            at = lax.rem(owner - table_ref[0] + count, count)
            top = (owner % GROUP) * height
            side = (owner // GROUP) * width
            for tap in range(TAPS):
                low = tap * chans + top
                out_ref[at, branch * TAPS + tap] = sums[low : low + height, side : side + width]


def kernel_terms(table, grid, feat, count):
    wide = feat.shape[1]
    taps = 3 * TAPS
    tail = (grid.shape[0] // taps // GROUP, wide // (count // GROUP))
    shapes = [
        jax.ShapeDtypeStruct((count, taps) + tail, jnp.float32),
        jax.ShapeDtypeStruct((1,) + tail, jnp.float32),
    ]
    kernel = functools.partial(kernel_terms_kernel, count)
    return direct(kernel, shapes, [grid, feat], "kernel_terms", table, 6)


def input_terms_kernel(at, table_ref, weight_ref, grid_ref, added_ref, *out_refs):
    block, rows = out_refs[0].shape[1:]
    lines = weight_ref[pl.ds(pl.multiple_of(table_ref[at] * block, block), block)]
    done = 0
    for out_ref in out_refs:
        each = max(cols for cols in range(1, 7) if out_ref.shape[0] % cols == 0)
        for start in range(0, out_ref.shape[0], each):
            here = slice((done + start) * rows, (done + start + each) * rows)
            sums = jnp.dot(lines, grid_ref[:, here], preferred_element_type=jnp.float32)
            for col in range(each):
                part = sums[:, col * rows : (col + 1) * rows]
                if added_ref is not None:
                    part = part + added_ref[done + start + col]
                out_ref[start + col] = part
        done += out_ref.shape[0]


def input_terms(at, table, weight_rows, grid, added=None, *, block, spans, rows):
    shapes = [jax.ShapeDtypeStruct((cols, block, rows), jnp.float32) for cols in spans]
    operands = [weight_rows, grid] + ([] if added is None else [added])

    def kernel(table_ref, weight_ref, grid_ref, *refs):
        added_ref, out_refs = (None, refs) if added is None else (refs[0], refs[1:])
        input_terms_kernel(at, table_ref, weight_ref, grid_ref, added_ref, *out_refs)

    return direct(kernel, shapes, operands, "input_terms", table, 3.5)


def unfold_kernel(norm, places, table_ref, *refs):
    held = len(places)
    codes, (out_ref, plain_ref, sems) = refs[:held], refs[-3:]
    taps, height, width = plain_ref.shape[1:]
    copies = []
    for at, (row, col) in enumerate(places):
        plain_ref[at] = decode(codes[at][:taps], codes[at][taps:], norm)
        top = pl.ds(pl.multiple_of(table_ref[row] * height, height), height)
        side = pl.ds(pl.multiple_of(table_ref[col] * width, width), width)
        copies.append(
            pltpu.make_async_copy(plain_ref.at[at], out_ref.at[:, top, side], sems.at[at])
        )
        copies[-1].start()
    for copy in copies:
        copy.wait()


def unfold(places, norm, shape, table, codes, before=None):
    held = len(codes)
    vmem = pl.BlockSpec(memory_space=pltpu.VMEM)
    hbm = pl.BlockSpec(memory_space=pl.ANY)
    operands = codes + ([] if before is None else [before])
    return pl.pallas_call(
        functools.partial(unfold_kernel, norm, places),
        in_specs=[pl.BlockSpec(memory_space=pltpu.SMEM)]
        + [vmem] * held
        + ([] if before is None else [hbm]),
        out_specs=hbm,
        out_shape=pltpu.HBM(shape, jnp.float32),
        input_output_aliases={} if before is None else {held + 1: 0},
        scratch_shapes=[
            pltpu.VMEM((held, shape[0]) + codes[0].shape[1:], jnp.float32),
            pltpu.SemaphoreType.DMA((held,)),
        ],
        compiler_params=pltpu.CompilerParams(vmem_limit_bytes=GRANT),
        cost_estimate=cost(3),
        name="unfold",
    )(table, *operands)


def first_hop_kernel(cut, at, terms_ref, top_ref, up_ref, down_ref):
    taps = terms_ref.shape[1]
    bound = bound_code(top_ref[...])
    up_ref[:cut] = encode(terms_ref[at, :cut], bound)
    up_ref[cut:] = bound
    down_ref[: taps - cut] = encode(terms_ref[at, cut:], bound)
    down_ref[taps - cut :] = bound


def next_hop_kernel(cut, to_up, to_down, up_ref, down_ref, terms_ref, top_ref, up_out, down_out):
    taps = terms_ref.shape[1]
    top = top_ref[...]
    for ref, at, out_ref, low, high in (
        (up_ref, to_up, up_out, 0, cut),
        (down_ref, to_down, down_out, cut if cut < taps else 0, taps),
    ):
        arrived = ref[high - low :]
        bound = bound_code(arrived.astype(jnp.float32) + top)
        value = decode(ref[: high - low], arrived, 1.0 / REACH) + terms_ref[at, low:high]
        out_ref[low:high] = encode(value, bound)
        if low > 0:
            out_ref[:low] = encode(terms_ref[at, :low], bound)
        if high < taps:
            out_ref[high:taps] = encode(terms_ref[at, high:], bound)
        out_ref[taps:] = bound


def last_hop_kernel(up_ref, down_ref, own_ref, top_ref, out_ref):
    taps = own_ref.shape[1]
    up_bound, down_bound = up_ref[taps:], down_ref[taps:]
    bound = bound_code(
        up_bound.astype(jnp.float32) + down_bound.astype(jnp.float32) + top_ref[...]
    )
    value = own_ref[0] + decode(up_ref[:taps], up_bound, 1.0 / REACH)
    value = value + decode(down_ref[:taps], down_bound, 1.0 / REACH)
    out_ref[:taps] = encode(value, bound)
    out_ref[taps:] = bound


def hop_call(kernel, out_rows, operands, name):
    tail = operands[-1].shape[-2:]
    shapes = [jax.ShapeDtypeStruct((rows,) + tail, jnp.bfloat16) for rows in out_rows]
    return direct(kernel, shapes, operands, name)


class Order:
    def __init__(self):
        self.last = ()

    def gate(self, *values):
        if not self.last:
            return values
        return lax.optimization_barrier(values + self.last)[: len(values)]

    def pin(self, *values):
        values = self.gate(*values)
        self.last = (values[0],)
        return values

    def __call__(self, kernel, *values):
        result = kernel(*self.gate(*values))
        self.last = (jax.tree.leaves(result)[0],)
        return result


class Ring:
    def __init__(self, count, taps):
        order = ring_order(count)
        self.ahead = [(order[i], order[(i + 1) % count]) for i in range(count)]
        self.behind = [(b, a) for a, b in self.ahead]
        self.count, self.half = count, count // 2
        self.taps, self.cut = taps, (taps + 1) // 2

    def send(self, messages):
        up, down = messages
        return lax.ppermute(up, "lon", self.ahead), lax.ppermute(down, "lon", self.behind)

    def first(self, terms, top):
        kernel = functools.partial(first_hop_kernel, self.cut, self.half)
        rows = [self.cut + 1, self.taps - self.cut + 1]
        return hop_call(kernel, rows, [terms, top], "first_hop")

    def next(self, left, messages, terms, top):
        cut = self.cut if left == self.half else self.taps
        kernel = functools.partial(next_hop_kernel, cut, left - 1, self.count - left + 1)
        return hop_call(kernel, [self.taps + 1] * 2, [*messages, terms, top], "next_hop")

    def last(self, messages, terms, top):
        return hop_call(last_hop_kernel, [self.taps + 1], [*messages, terms, top], "last_hop")[0]


class Chain:
    def __init__(self, ring, order, side, terms, top):
        self.ring, self.order, self.side = ring, order, side
        self.terms, self.top, self.left = terms, top, ring.half
        self.out = order(ring.first, terms, top)
        self.codes = []

    def arrive(self):
        self.out = self.order.pin(*self.ring.send(self.out))

    def hop(self):
        run = functools.partial(self.ring.next, self.left)
        self.out = self.order(run, self.out, self.terms, self.top)
        self.left -= 1

    def last(self):
        own = self.order(self.ring.last, self.out, self.terms, self.top)
        self.out = (own, own)
        self.keep(0, own)

    def keep(self, ahead, code):
        count = self.ring.count
        self.codes.append(
            ((ROWS_AT + ahead, ROWS_AT + count + 2 * ahead + self.side), code)
        )

    def take(self):
        taken, self.codes = self.codes, []
        return taken

    def move(self):
        ring, (up, down) = self.ring, self.out
        if self.left < ring.half:
            self.out = self.order.pin(*ring.send((up, down)))
            self.keep(ring.count - self.left, self.out[0])
            self.keep(self.left, self.out[1])
        else:
            cut = ring.cut
            parts = self.order.pin(*ring.send((up[:cut], down[cut:])))
            self.keep(ring.half, jnp.concatenate(parts, axis=0))
        self.left += 1


def make_table(lon, ch, count):
    place_x, place_core = ch // 2, ch % 2
    spot = ring_position(lon, count)
    owners = (spot + jnp.arange(count, dtype=jnp.int32)) % count
    sides = jnp.stack([place_x, 1 - place_x]) * (count // GROUP)
    return jnp.concatenate(
        [
            jnp.stack([spot, place_core, 3 - ch, ch ^ 2, ch ^ 1, ch]),
            owners % GROUP,
            (owners[:, None] // GROUP + sides[None]).reshape(-1),
        ]
    ).astype(jnp.int32)


def local(features, cotangent, weights):
    block, _, cols, rows = features.shape
    chans = cotangent.shape[1]
    total = weights.shape[4]
    count = lax.axis_size("lon")
    cells = cols * count * rows

    feat = jnp.transpose(features.reshape(block, cols, rows), (1, 0, 2))
    cot = jnp.transpose(cotangent.reshape(3, chans, cols, rows), (0, 2, 1, 3))
    order = Order()

    tails, heads = order(edges, cot)
    left = lax.ppermute(tails, "lon", [(i, (i + 1) % count) for i in range(count)])
    right = lax.ppermute(heads, "lon", [((i + 1) % count, i) for i in range(count)])

    to_core = [(i, i ^ 1) for i in range(4)]
    to_x = [(i, i ^ 2) for i in range(4)]
    far = lax.ppermute(feat, "ch", to_x)
    near = lax.ppermute(feat, "ch", to_core)

    norm = 1.0 / (REACH * cells**0.5)
    ring = Ring(count, 3 * TAPS)
    table = order(
        functools.partial(make_table, count=count), lax.axis_index("lon"), lax.axis_index("ch")
    )
    weight_rows = order(jnp.transpose, weights.reshape(-1, total))
    flat_near = order(flatten, table, feat, near)
    left, right, far = order.gate(left, right, far)
    grid = order(spread, cot, left, right)
    far_near = lax.ppermute(far, "ch", to_core)

    def terms_of(which, spans, *added):
        run = functools.partial(
            input_terms, BLOCKS_AT + which, block=block, spans=spans, rows=rows
        )
        return order(run, table, weight_rows, grid, *added)

    def features_with(flat):
        return order(functools.partial(kernel_terms, count=count), table, grid, flat)

    half = ring.half
    most, whole = (cols * 5 // 6, cols // 6), (cols,)
    shape = (3 * TAPS, chans, total)
    written = []

    def write(*chains):
        taken = [item for chain in chains for item in chain.take()]
        places, codes = zip(*taken)
        run = functools.partial(unfold, places, norm, shape)
        written[:] = [order(run, table, list(codes), *written)]

    near = Chain(ring, order, 0, *features_with(flat_near))
    flat_far = order(flatten, table, far, far_near)
    (away,) = terms_of(0, whole)
    near.arrive()
    near.hop()
    away = lax.ppermute(order.gate(away)[0], "ch", to_core)
    far = Chain(ring, order, 1, *features_with(flat_far))
    across = list(terms_of(1, most, away))
    far.arrive()
    far.hop()
    near.arrive()
    near.hop()
    across[0] = lax.ppermute(order.gate(across[0])[0], "ch", to_x)
    (beside,) = terms_of(2, whole)
    for _ in range(half - 4):
        far.arrive()
        far.hop()
        near.arrive()
        near.hop()
    far.arrive()
    far.hop()
    near.arrive()
    near.hop()
    far.arrive()
    far.hop()
    (mine,) = terms_of(3, whole)
    near.arrive()
    near.last()
    near.move()
    far.arrive()
    far.last()
    write(near)
    near.move()
    far.move()
    for _ in range(half - 4):
        near.move()
        far.move()
    write(near, far)
    near.move()
    far.move()
    across[0] = order.pin(across[0])[0]
    across[1] = lax.ppermute(order.gate(across[1])[0], "ch", to_x)
    write(near, far)
    near.move()
    beside = lax.ppermute(order.gate(beside)[0], "ch", to_core)
    far.move()
    write(near, far)
    across = jnp.concatenate(across, axis=0)
    input_grad = order(lambda *parts: sum(parts).astype(jnp.bfloat16), mine, beside, across)
    far.move()
    write(far)
    kernel_grad = written[0]

    input_grad = jnp.transpose(input_grad, (1, 0, 2)).reshape(block, 1, cols, rows)
    return (input_grad, kernel_grad.reshape(3, 3, 3, chans, total))


def solution(mesh):
    return jax.shard_map(
        local,
        mesh=mesh,
        in_specs=(
            P("ch", None, "lon", None),
            P(None, "ch", None, "lon", None),
            P(None, None, None, "ch", None),
        ),
        out_specs=(P("ch", None, "lon", None), P(None, None, None, "ch", None)),
        check_vma=False,
    )
```

```python
import functools

import jax
import jax.numpy as jnp
from jax import lax
from jax.experimental import pallas as pl
from jax.experimental.pallas import tpu as pltpu
from jax.sharding import PartitionSpec as P

DILATIONS = (6, 12, 18)
TAPS = 9
GROUP = 8
REACH = 2.0**15.5
TINY = 1e-30
LEAST = 2.0**-125
MIB = 1024 * 1024
GRANT = 16 * MIB
PACE = 3e8
BLOCKS_AT = 2
ROWS_AT = 6


def cost(micros):
    return pl.CostEstimate(flops=int(micros * PACE), bytes_accessed=0, transcendentals=0)


def in_hbm(value):
    return pltpu.with_memory_space_constraint(value, pltpu.HBM)


def ring_order(count):
    return list(range(0, count, 2)) + list(range(count - 1, 0, -2))


def ring_position(index, count):
    return jnp.where(index % 2 == 0, index // 2, count - 1 - index // 2)


def bound_code(bound):
    return (bound * 1.01).astype(jnp.bfloat16)


def encode(value, bound):
    power = value * (REACH / bound.astype(jnp.float32))
    power = power * power
    power = power * power
    power = power * power
    return jnp.where(value < 0, -power, power).astype(jnp.bfloat16)


def decode(code, bound, norm):
    wide = code.astype(jnp.float32)
    fourth = lax.rsqrt(lax.rsqrt(jnp.maximum(jnp.abs(wide), LEAST)))
    root = fourth * lax.rsqrt(fourth) * (bound.astype(jnp.float32) * norm)
    return jnp.where(wide < 0, -root, root)


def direct(kernel, out_shapes, operands, name, table=None, micros=2):
    vmem = pl.BlockSpec(memory_space=pltpu.VMEM)
    smem = pl.BlockSpec(memory_space=pltpu.SMEM)
    return pl.pallas_call(
        kernel,
        in_specs=([] if table is None else [smem]) + [vmem] * len(operands),
        out_specs=[vmem] * len(out_shapes),
        out_shape=out_shapes,
        compiler_params=pltpu.CompilerParams(vmem_limit_bytes=GRANT),
        cost_estimate=cost(micros),
        name=name,
    )(*([] if table is None else [table]), *operands)


def edge_kernel(cot_ref, tail_ref, head_ref):
    cols = cot_ref.shape[1]
    start = 0
    for branch in range(3):
        dilation = DILATIONS[branch]
        tail_ref[start : start + dilation] = cot_ref[branch, cols - dilation :]
        head_ref[start : start + dilation] = cot_ref[branch, :dilation]
        start += dilation


def edges(cot):
    shape = (sum(DILATIONS),) + cot.shape[2:]
    return pl.pallas_call(
        edge_kernel,
        grid=(1,),
        in_specs=[pl.BlockSpec(cot.shape, lambda i: (0, 0, 0, 0))],
        out_specs=[pl.BlockSpec(shape, lambda i: (0, 0, 0))] * 2,
        out_shape=[jax.ShapeDtypeStruct(shape, cot.dtype)] * 2,
        compiler_params=pltpu.CompilerParams(vmem_limit_bytes=GRANT),
        cost_estimate=cost(1),
        name="edges",
    )(in_hbm(cot))


def spread_kernel(cot_ref, left_ref, right_ref, out_ref):
    cols, chans, rows = cot_ref.shape[1:]
    lane = lax.broadcasted_iota(jnp.int32, (chans, rows), 1)
    start = 0
    for branch in range(3):
        dilation = DILATIONS[branch]
        for place in range(-dilation, cols + dilation):
            if place < 0:
                column = left_ref[start + place + dilation]
            elif place >= cols:
                column = right_ref[start + place - cols]
            else:
                column = cot_ref[branch, place]
            wide = column.astype(jnp.float32)
            for lat_tap in range(3):
                shift = dilation * (lat_tap - 1)
                if shift == 0:
                    moved = column
                else:
                    keep = lane >= shift if shift > 0 else lane < rows + shift
                    moved = jnp.where(keep, pltpu.roll(wide, shift % rows, 1), 0.0)
                    moved = moved.astype(jnp.bfloat16)
                for lon_tap in range(3):
                    target = place + dilation * (lon_tap - 1)
                    if 0 <= target < cols:
                        low = (TAPS * branch + 3 * lat_tap + lon_tap) * chans
                        out_ref[low : low + chans, target * rows : (target + 1) * rows] = moved
        start += dilation


def spread(cot, left, right):
    branches, cols, chans, rows = cot.shape
    shape = jax.ShapeDtypeStruct((branches * TAPS * chans, cols * rows), jnp.bfloat16)
    return direct(spread_kernel, [shape], [cot, left, right], "spread")[0]


def flatten_kernel(place_ref, first_ref, second_ref, out_ref):
    cols, block, rows = first_ref.shape
    for ref, core in ((first_ref, place_ref[1]), (second_ref, 1 - place_ref[1])):
        at = pl.ds(pl.multiple_of(core * block, block), block)
        for col in range(cols):
            out_ref[col * rows : (col + 1) * rows, at] = jnp.transpose(ref[col])


def flatten(table, first, second):
    cols, block, rows = first.shape
    shape = jax.ShapeDtypeStruct((cols * rows, 2 * block), jnp.bfloat16)
    return direct(flatten_kernel, [shape], [first, second], "flatten", table)[0]


def kernel_terms_kernel(count, table_ref, grid_ref, feat_ref, out_ref, top_ref):
    chans = grid_ref.shape[0] // (3 * TAPS)
    parts = count // GROUP
    height = chans // GROUP
    width = feat_ref.shape[1] // parts
    deep = TAPS * chans
    top_ref[...] = jnp.full(top_ref.shape, TINY, jnp.float32)

    @pl.loop(0, 3)
    def _(branch):
        lines = grid_ref[pl.ds(pl.multiple_of(branch * deep, deep), deep)]
        sums = jnp.dot(lines, feat_ref[...], preferred_element_type=jnp.float32)
        top_ref[...] = jnp.maximum(top_ref[...], jnp.max(jnp.abs(sums)))
        for owner in range(count):
            at = lax.rem(owner - table_ref[0] + count, count)
            top = (owner % GROUP) * height
            side = (owner // GROUP) * width
            for tap in range(TAPS):
                low = tap * chans + top
                out_ref[at, branch * TAPS + tap] = sums[low : low + height, side : side + width]


def kernel_terms(table, grid, feat, count):
    wide = feat.shape[1]
    taps = 3 * TAPS
    tail = (grid.shape[0] // taps // GROUP, wide // (count // GROUP))
    shapes = [
        jax.ShapeDtypeStruct((count, taps) + tail, jnp.float32),
        jax.ShapeDtypeStruct((1,) + tail, jnp.float32),
    ]
    kernel = functools.partial(kernel_terms_kernel, count)
    return direct(kernel, shapes, [grid, feat], "kernel_terms", table, 6)


def input_terms_kernel(at, table_ref, weight_ref, grid_ref, added_ref, *out_refs):
    block, rows = out_refs[0].shape[1:]
    lines = weight_ref[pl.ds(pl.multiple_of(table_ref[at] * block, block), block)]
    done = 0
    for out_ref in out_refs:
        each = max(cols for cols in range(1, 7) if out_ref.shape[0] % cols == 0)
        for start in range(0, out_ref.shape[0], each):
            here = slice((done + start) * rows, (done + start + each) * rows)
            sums = jnp.dot(lines, grid_ref[:, here], preferred_element_type=jnp.float32)
            for col in range(each):
                part = sums[:, col * rows : (col + 1) * rows]
                if added_ref is not None:
                    part = part + added_ref[done + start + col]
                out_ref[start + col] = part
        done += out_ref.shape[0]


def input_terms(at, table, weight_rows, grid, added=None, *, block, spans, rows):
    shapes = [jax.ShapeDtypeStruct((cols, block, rows), jnp.float32) for cols in spans]
    operands = [weight_rows, grid] + ([] if added is None else [added])

    def kernel(table_ref, weight_ref, grid_ref, *refs):
        added_ref, out_refs = (None, refs) if added is None else (refs[0], refs[1:])
        input_terms_kernel(at, table_ref, weight_ref, grid_ref, added_ref, *out_refs)

    return direct(kernel, shapes, operands, "input_terms", table, 3.5)


def unfold_kernel(norm, places, table_ref, *refs):
    held = len(places)
    codes, (out_ref, plain_ref, sems) = refs[:held], refs[-3:]
    taps, height, width = plain_ref.shape[1:]
    copies = []
    for at, (row, col) in enumerate(places):
        plain_ref[at] = decode(codes[at][:taps], codes[at][taps:], norm)
        top = pl.ds(pl.multiple_of(table_ref[row] * height, height), height)
        side = pl.ds(pl.multiple_of(table_ref[col] * width, width), width)
        copies.append(
            pltpu.make_async_copy(plain_ref.at[at], out_ref.at[:, top, side], sems.at[at])
        )
        copies[-1].start()
    for copy in copies:
        copy.wait()


def unfold(places, norm, shape, table, codes, before=None):
    held = len(codes)
    vmem = pl.BlockSpec(memory_space=pltpu.VMEM)
    hbm = pl.BlockSpec(memory_space=pl.ANY)
    operands = codes + ([] if before is None else [before])
    return pl.pallas_call(
        functools.partial(unfold_kernel, norm, places),
        in_specs=[pl.BlockSpec(memory_space=pltpu.SMEM)]
        + [vmem] * held
        + ([] if before is None else [hbm]),
        out_specs=hbm,
        out_shape=pltpu.HBM(shape, jnp.float32),
        input_output_aliases={} if before is None else {held + 1: 0},
        scratch_shapes=[
            pltpu.VMEM((held, shape[0]) + codes[0].shape[1:], jnp.float32),
            pltpu.SemaphoreType.DMA((held,)),
        ],
        compiler_params=pltpu.CompilerParams(vmem_limit_bytes=GRANT),
        cost_estimate=cost(3),
        name="unfold",
    )(table, *operands)


def first_hop_kernel(cut, at, terms_ref, top_ref, up_ref, down_ref):
    taps = terms_ref.shape[1]
    bound = bound_code(top_ref[...])
    up_ref[:cut] = encode(terms_ref[at, :cut], bound)
    up_ref[cut:] = bound
    down_ref[: taps - cut] = encode(terms_ref[at, cut:], bound)
    down_ref[taps - cut :] = bound


def next_hop_kernel(cut, to_up, to_down, up_ref, down_ref, terms_ref, top_ref, up_out, down_out):
    taps = terms_ref.shape[1]
    top = top_ref[...]
    for ref, at, out_ref, low, high in (
        (up_ref, to_up, up_out, 0, cut),
        (down_ref, to_down, down_out, cut if cut < taps else 0, taps),
    ):
        arrived = ref[high - low :]
        bound = bound_code(arrived.astype(jnp.float32) + top)
        value = decode(ref[: high - low], arrived, 1.0 / REACH) + terms_ref[at, low:high]
        out_ref[low:high] = encode(value, bound)
        if low > 0:
            out_ref[:low] = encode(terms_ref[at, :low], bound)
        if high < taps:
            out_ref[high:taps] = encode(terms_ref[at, high:], bound)
        out_ref[taps:] = bound


def last_hop_kernel(up_ref, down_ref, own_ref, top_ref, out_ref):
    taps = own_ref.shape[1]
    up_bound, down_bound = up_ref[taps:], down_ref[taps:]
    bound = bound_code(
        up_bound.astype(jnp.float32) + down_bound.astype(jnp.float32) + top_ref[...]
    )
    value = own_ref[0] + decode(up_ref[:taps], up_bound, 1.0 / REACH)
    value = value + decode(down_ref[:taps], down_bound, 1.0 / REACH)
    out_ref[:taps] = encode(value, bound)
    out_ref[taps:] = bound


def hop_call(kernel, out_rows, operands, name):
    tail = operands[-1].shape[-2:]
    shapes = [jax.ShapeDtypeStruct((rows,) + tail, jnp.bfloat16) for rows in out_rows]
    return direct(kernel, shapes, operands, name)


class Order:
    def __init__(self):
        self.last = ()

    def gate(self, *values):
        if not self.last:
            return values
        return lax.optimization_barrier(values + self.last)[: len(values)]

    def pin(self, *values):
        values = self.gate(*values)
        self.last = (values[0],)
        return values

    def __call__(self, kernel, *values):
        result = kernel(*self.gate(*values))
        self.last = (jax.tree.leaves(result)[0],)
        return result


class Ring:
    def __init__(self, count, taps):
        order = ring_order(count)
        self.ahead = [(order[i], order[(i + 1) % count]) for i in range(count)]
        self.behind = [(b, a) for a, b in self.ahead]
        self.count, self.half = count, count // 2
        self.taps, self.cut = taps, (taps + 1) // 2

    def send(self, messages):
        up, down = messages
        return lax.ppermute(up, "lon", self.ahead), lax.ppermute(down, "lon", self.behind)

    def first(self, terms, top):
        kernel = functools.partial(first_hop_kernel, self.cut, self.half)
        rows = [self.cut + 1, self.taps - self.cut + 1]
        return hop_call(kernel, rows, [terms, top], "first_hop")

    def next(self, left, messages, terms, top):
        cut = self.cut if left == self.half else self.taps
        kernel = functools.partial(next_hop_kernel, cut, left - 1, self.count - left + 1)
        return hop_call(kernel, [self.taps + 1] * 2, [*messages, terms, top], "next_hop")

    def last(self, messages, terms, top):
        return hop_call(last_hop_kernel, [self.taps + 1], [*messages, terms, top], "last_hop")[0]


class Chain:
    def __init__(self, ring, order, side, terms, top):
        self.ring, self.order, self.side = ring, order, side
        self.terms, self.top, self.left = terms, top, ring.half
        self.out = order(ring.first, terms, top)
        self.codes = []

    def arrive(self):
        self.out = self.order.pin(*self.ring.send(self.out))

    def hop(self):
        run = functools.partial(self.ring.next, self.left)
        self.out = self.order(run, self.out, self.terms, self.top)
        self.left -= 1

    def last(self):
        own = self.order(self.ring.last, self.out, self.terms, self.top)
        self.out = (own, own)
        self.keep(0, own)

    def keep(self, ahead, code):
        count = self.ring.count
        self.codes.append(
            ((ROWS_AT + ahead, ROWS_AT + count + 2 * ahead + self.side), code)
        )

    def take(self):
        taken, self.codes = self.codes, []
        return taken

    def move(self):
        ring, (up, down) = self.ring, self.out
        if self.left < ring.half:
            self.out = self.order.pin(*ring.send((up, down)))
            self.keep(ring.count - self.left, self.out[0])
            self.keep(self.left, self.out[1])
        else:
            cut = ring.cut
            parts = self.order.pin(*ring.send((up[:cut], down[cut:])))
            self.keep(ring.half, jnp.concatenate(parts, axis=0))
        self.left += 1


def make_table(lon, ch, count):
    place_x, place_core = ch // 2, ch % 2
    spot = ring_position(lon, count)
    owners = (spot + jnp.arange(count, dtype=jnp.int32)) % count
    sides = jnp.stack([place_x, 1 - place_x]) * (count // GROUP)
    return jnp.concatenate(
        [
            jnp.stack([spot, place_core, 3 - ch, ch ^ 2, ch ^ 1, ch]),
            owners % GROUP,
            (owners[:, None] // GROUP + sides[None]).reshape(-1),
        ]
    ).astype(jnp.int32)


def local(features, cotangent, weights):
    block, _, cols, rows = features.shape
    chans = cotangent.shape[1]
    total = weights.shape[4]
    count = lax.axis_size("lon")
    cells = cols * count * rows

    feat = jnp.transpose(features.reshape(block, cols, rows), (1, 0, 2))
    cot = jnp.transpose(cotangent.reshape(3, chans, cols, rows), (0, 2, 1, 3))
    order = Order()

    tails, heads = order(edges, cot)
    left = lax.ppermute(tails, "lon", [(i, (i + 1) % count) for i in range(count)])
    right = lax.ppermute(heads, "lon", [((i + 1) % count, i) for i in range(count)])

    to_core = [(i, i ^ 1) for i in range(4)]
    to_x = [(i, i ^ 2) for i in range(4)]
    far = lax.ppermute(feat, "ch", to_x)
    near = lax.ppermute(feat, "ch", to_core)

    norm = 1.0 / (REACH * cells**0.5)
    ring = Ring(count, 3 * TAPS)
    table = order(
        functools.partial(make_table, count=count), lax.axis_index("lon"), lax.axis_index("ch")
    )
    weight_rows = order(jnp.transpose, weights.reshape(-1, total))
    flat_near = order(flatten, table, feat, near)
    left, right, far = order.gate(left, right, far)
    grid = order(spread, cot, left, right)
    far_near = lax.ppermute(far, "ch", to_core)

    def terms_of(which, spans, *added):
        run = functools.partial(
            input_terms, BLOCKS_AT + which, block=block, spans=spans, rows=rows
        )
        return order(run, table, weight_rows, grid, *added)

    def features_with(flat):
        return order(functools.partial(kernel_terms, count=count), table, grid, flat)

    half = ring.half
    whole = (cols,)
    shape = (3 * TAPS, chans, total)
    written = []

    def write(*chains):
        taken = [item for chain in chains for item in chain.take()]
        places, codes = zip(*taken)
        run = functools.partial(unfold, places, norm, shape)
        written[:] = [order(run, table, list(codes), *written)]

    near = Chain(ring, order, 0, *features_with(flat_near))
    flat_far = order(flatten, table, far, far_near)
    (away,) = terms_of(0, whole)
    near.arrive()
    near.hop()
    away = lax.ppermute(order.gate(away)[0], "ch", to_core)
    far = Chain(ring, order, 1, *features_with(flat_far))
    (across,) = terms_of(1, whole, away)
    far.arrive()
    far.hop()
    near.arrive()
    near.hop()
    across = lax.ppermute(order.gate(across)[0], "ch", to_x)
    (beside,) = terms_of(2, whole)
    for _ in range(half - 4):
        far.arrive()
        far.hop()
        near.arrive()
        near.hop()
    far.arrive()
    far.hop()
    near.arrive()
    near.hop()
    far.arrive()
    far.hop()
    (mine,) = terms_of(3, whole)
    near.arrive()
    near.last()
    far.arrive()
    far.last()
    near.move()
    write(near)
    far.move()
    write(far)
    near.move()
    for _ in range(half - 4):
        far.move()
        near.move()
    far.move()
    write(near, far)
    near.move()
    across = order.pin(across)[0]
    far.move()
    beside = lax.ppermute(order.gate(beside)[0], "ch", to_core)
    write(near, far)
    input_grad = order(lambda *parts: sum(parts).astype(jnp.bfloat16), mine, beside, across)
    far.move()
    near.move()
    write(near, far)
    kernel_grad = written[0]

    input_grad = jnp.transpose(input_grad, (1, 0, 2)).reshape(block, 1, cols, rows)
    return (input_grad, kernel_grad.reshape(3, 3, 3, chans, total))


def solution(mesh):
    return jax.shard_map(
        local,
        mesh=mesh,
        in_specs=(
            P("ch", None, "lon", None),
            P(None, "ch", None, "lon", None),
            P(None, None, None, "ch", None),
        ),
        out_specs=(P("ch", None, "lon", None), P(None, None, None, "ch", None)),
        check_vma=False,
    )
```

```python
import functools

import jax
import jax.numpy as jnp
from jax import lax
from jax.experimental import pallas as pl
from jax.experimental.pallas import tpu as pltpu
from jax.sharding import PartitionSpec as P

DILATIONS = (6, 12, 18)
TAPS = 9
GROUP = 8
REACH = 2.0**15.5
TINY = 1e-30
LEAST = 2.0**-125
MIB = 1024 * 1024
GRANT = 16 * MIB
PACE = 3e8
BLOCKS_AT = 2
ROWS_AT = 6


def cost(micros):
    return pl.CostEstimate(flops=int(micros * PACE), bytes_accessed=0, transcendentals=0)


def in_hbm(value):
    return pltpu.with_memory_space_constraint(value, pltpu.HBM)


def ring_order(count):
    return list(range(0, count, 2)) + list(range(count - 1, 0, -2))


def ring_position(index, count):
    return jnp.where(index % 2 == 0, index // 2, count - 1 - index // 2)


def bound_code(bound):
    return (bound * 1.01).astype(jnp.bfloat16)


def encode(value, bound):
    power = value * (REACH / bound.astype(jnp.float32))
    power = power * power
    power = power * power
    power = power * power
    return jnp.where(value < 0, -power, power).astype(jnp.bfloat16)


def decode(code, bound, norm):
    wide = code.astype(jnp.float32)
    fourth = lax.rsqrt(lax.rsqrt(jnp.maximum(jnp.abs(wide), LEAST)))
    root = fourth * lax.rsqrt(fourth) * (bound.astype(jnp.float32) * norm)
    return jnp.where(wide < 0, -root, root)


def direct(kernel, out_shapes, operands, name, table=None, micros=2):
    vmem = pl.BlockSpec(memory_space=pltpu.VMEM)
    smem = pl.BlockSpec(memory_space=pltpu.SMEM)
    return pl.pallas_call(
        kernel,
        in_specs=([] if table is None else [smem]) + [vmem] * len(operands),
        out_specs=[vmem] * len(out_shapes),
        out_shape=out_shapes,
        compiler_params=pltpu.CompilerParams(vmem_limit_bytes=GRANT),
        cost_estimate=cost(micros),
        name=name,
    )(*([] if table is None else [table]), *operands)


def edge_kernel(cot_ref, tail_ref, head_ref):
    cols = cot_ref.shape[1]
    start = 0
    for branch in range(3):
        dilation = DILATIONS[branch]
        tail_ref[start : start + dilation] = cot_ref[branch, cols - dilation :]
        head_ref[start : start + dilation] = cot_ref[branch, :dilation]
        start += dilation


def edges(cot):
    shape = (sum(DILATIONS),) + cot.shape[2:]
    return pl.pallas_call(
        edge_kernel,
        grid=(1,),
        in_specs=[pl.BlockSpec(cot.shape, lambda i: (0, 0, 0, 0))],
        out_specs=[pl.BlockSpec(shape, lambda i: (0, 0, 0))] * 2,
        out_shape=[jax.ShapeDtypeStruct(shape, cot.dtype)] * 2,
        compiler_params=pltpu.CompilerParams(vmem_limit_bytes=GRANT),
        cost_estimate=cost(1),
        name="edges",
    )(in_hbm(cot))


def spread_kernel(cot_ref, left_ref, right_ref, weight_ref, out_ref):
    del weight_ref
    cols, chans, rows = cot_ref.shape[1:]
    lane = lax.broadcasted_iota(jnp.int32, (chans, rows), 1)
    start = 0
    for branch in range(3):
        dilation = DILATIONS[branch]
        for place in range(-dilation, cols + dilation):
            if place < 0:
                column = left_ref[start + place + dilation]
            elif place >= cols:
                column = right_ref[start + place - cols]
            else:
                column = cot_ref[branch, place]
            wide = column.astype(jnp.float32)
            for lat_tap in range(3):
                shift = dilation * (lat_tap - 1)
                if shift == 0:
                    moved = column
                else:
                    keep = lane >= shift if shift > 0 else lane < rows + shift
                    moved = jnp.where(keep, pltpu.roll(wide, shift % rows, 1), 0.0)
                    moved = moved.astype(jnp.bfloat16)
                for lon_tap in range(3):
                    target = place + dilation * (lon_tap - 1)
                    if 0 <= target < cols:
                        low = (TAPS * branch + 3 * lat_tap + lon_tap) * chans
                        out_ref[low : low + chans, target * rows : (target + 1) * rows] = moved
        start += dilation


def spread(cot, left, right, weight_rows):
    branches, cols, chans, rows = cot.shape
    shape = jax.ShapeDtypeStruct((branches * TAPS * chans, cols * rows), jnp.bfloat16)
    return direct(spread_kernel, [shape], [cot, left, right, weight_rows], "spread")[0]


def flatten_kernel(place_ref, first_ref, second_ref, out_ref):
    cols, block, rows = first_ref.shape
    for ref, core in ((first_ref, place_ref[1]), (second_ref, 1 - place_ref[1])):
        at = pl.ds(pl.multiple_of(core * block, block), block)
        for col in range(cols):
            out_ref[col * rows : (col + 1) * rows, at] = jnp.transpose(ref[col])


def flatten(table, first, second):
    cols, block, rows = first.shape
    shape = jax.ShapeDtypeStruct((cols * rows, 2 * block), jnp.bfloat16)
    return direct(flatten_kernel, [shape], [first, second], "flatten", table)[0]


def kernel_terms_kernel(count, table_ref, grid_ref, feat_ref, out_ref, top_ref):
    chans = grid_ref.shape[0] // (3 * TAPS)
    parts = count // GROUP
    height = chans // GROUP
    width = feat_ref.shape[1] // parts
    deep = TAPS * chans
    top_ref[...] = jnp.full(top_ref.shape, TINY, jnp.float32)

    @pl.loop(0, 3)
    def _(branch):
        lines = grid_ref[pl.ds(pl.multiple_of(branch * deep, deep), deep)]
        sums = jnp.dot(lines, feat_ref[...], preferred_element_type=jnp.float32)
        top_ref[...] = jnp.maximum(top_ref[...], jnp.max(jnp.abs(sums)))
        for owner in range(count):
            at = lax.rem(owner - table_ref[0] + count, count)
            top = (owner % GROUP) * height
            side = (owner // GROUP) * width
            for tap in range(TAPS):
                low = tap * chans + top
                out_ref[at, branch * TAPS + tap] = sums[low : low + height, side : side + width]


def kernel_terms(table, grid, feat, count):
    wide = feat.shape[1]
    taps = 3 * TAPS
    tail = (grid.shape[0] // taps // GROUP, wide // (count // GROUP))
    shapes = [
        jax.ShapeDtypeStruct((count, taps) + tail, jnp.float32),
        jax.ShapeDtypeStruct((1,) + tail, jnp.float32),
    ]
    kernel = functools.partial(kernel_terms_kernel, count)
    return direct(kernel, shapes, [grid, feat], "kernel_terms", table, 6)


def input_terms_kernel(at, table_ref, weight_ref, grid_ref, added_ref, *out_refs):
    block, rows = out_refs[0].shape[1:]
    lines = weight_ref[pl.ds(pl.multiple_of(table_ref[at] * block, block), block)]
    done = 0
    for out_ref in out_refs:
        each = max(cols for cols in range(1, 7) if out_ref.shape[0] % cols == 0)
        for start in range(0, out_ref.shape[0], each):
            here = slice((done + start) * rows, (done + start + each) * rows)
            sums = jnp.dot(lines, grid_ref[:, here], preferred_element_type=jnp.float32)
            for col in range(each):
                part = sums[:, col * rows : (col + 1) * rows]
                if added_ref is not None:
                    part = part + added_ref[done + start + col]
                out_ref[start + col] = part
        done += out_ref.shape[0]


def input_terms(at, table, weight_rows, grid, added=None, *, block, spans, rows):
    shapes = [jax.ShapeDtypeStruct((cols, block, rows), jnp.float32) for cols in spans]
    operands = [weight_rows, grid] + ([] if added is None else [added])

    def kernel(table_ref, weight_ref, grid_ref, *refs):
        added_ref, out_refs = (None, refs) if added is None else (refs[0], refs[1:])
        input_terms_kernel(at, table_ref, weight_ref, grid_ref, added_ref, *out_refs)

    return direct(kernel, shapes, operands, "input_terms", table, 3.5)


def unfold_kernel(norm, places, table_ref, *refs):
    held = len(places)
    codes, (out_ref, plain_ref, sems) = refs[:held], refs[-3:]
    taps, height, width = plain_ref.shape[1:]
    copies = []
    for at, (row, col) in enumerate(places):
        plain_ref[at] = decode(codes[at][:taps], codes[at][taps:], norm)
        top = pl.ds(pl.multiple_of(table_ref[row] * height, height), height)
        side = pl.ds(pl.multiple_of(table_ref[col] * width, width), width)
        copies.append(
            pltpu.make_async_copy(plain_ref.at[at], out_ref.at[:, top, side], sems.at[at])
        )
        copies[-1].start()
    for copy in copies:
        copy.wait()


def unfold(places, norm, shape, table, codes, before=None):
    held = len(codes)
    vmem = pl.BlockSpec(memory_space=pltpu.VMEM)
    hbm = pl.BlockSpec(memory_space=pl.ANY)
    operands = codes + ([] if before is None else [before])
    return pl.pallas_call(
        functools.partial(unfold_kernel, norm, places),
        in_specs=[pl.BlockSpec(memory_space=pltpu.SMEM)]
        + [vmem] * held
        + ([] if before is None else [hbm]),
        out_specs=hbm,
        out_shape=pltpu.HBM(shape, jnp.float32),
        input_output_aliases={} if before is None else {held + 1: 0},
        scratch_shapes=[
            pltpu.VMEM((held, shape[0]) + codes[0].shape[1:], jnp.float32),
            pltpu.SemaphoreType.DMA((held,)),
        ],
        compiler_params=pltpu.CompilerParams(vmem_limit_bytes=GRANT),
        cost_estimate=cost(3),
        name="unfold",
    )(table, *operands)


def first_hop_kernel(cut, at, terms_ref, top_ref, up_ref, down_ref):
    taps = terms_ref.shape[1]
    bound = bound_code(top_ref[...])
    up_ref[:cut] = encode(terms_ref[at, :cut], bound)
    up_ref[cut:] = bound
    down_ref[: taps - cut] = encode(terms_ref[at, cut:], bound)
    down_ref[taps - cut :] = bound


def next_hop_kernel(cut, to_up, to_down, up_ref, down_ref, terms_ref, top_ref, up_out, down_out):
    taps = terms_ref.shape[1]
    top = top_ref[...]
    for ref, at, out_ref, low, high in (
        (up_ref, to_up, up_out, 0, cut),
        (down_ref, to_down, down_out, cut if cut < taps else 0, taps),
    ):
        arrived = ref[high - low :]
        bound = bound_code(arrived.astype(jnp.float32) + top)
        value = decode(ref[: high - low], arrived, 1.0 / REACH) + terms_ref[at, low:high]
        out_ref[low:high] = encode(value, bound)
        if low > 0:
            out_ref[:low] = encode(terms_ref[at, :low], bound)
        if high < taps:
            out_ref[high:taps] = encode(terms_ref[at, high:], bound)
        out_ref[taps:] = bound


def last_hop_kernel(up_ref, down_ref, own_ref, top_ref, out_ref):
    taps = own_ref.shape[1]
    up_bound, down_bound = up_ref[taps:], down_ref[taps:]
    bound = bound_code(
        up_bound.astype(jnp.float32) + down_bound.astype(jnp.float32) + top_ref[...]
    )
    value = own_ref[0] + decode(up_ref[:taps], up_bound, 1.0 / REACH)
    value = value + decode(down_ref[:taps], down_bound, 1.0 / REACH)
    out_ref[:taps] = encode(value, bound)
    out_ref[taps:] = bound


def hop_call(kernel, out_rows, operands, name):
    tail = operands[-1].shape[-2:]
    shapes = [jax.ShapeDtypeStruct((rows,) + tail, jnp.bfloat16) for rows in out_rows]
    return direct(kernel, shapes, operands, name)


class Order:
    def __init__(self):
        self.last = ()

    def gate(self, *values):
        if not self.last:
            return values
        return lax.optimization_barrier(values + self.last)[: len(values)]

    def pin(self, *values):
        values = self.gate(*values)
        self.last = (values[0],)
        return values

    def __call__(self, kernel, *values):
        result = kernel(*self.gate(*values))
        self.last = (jax.tree.leaves(result)[0],)
        return result


class Ring:
    def __init__(self, count, taps):
        order = ring_order(count)
        self.ahead = [(order[i], order[(i + 1) % count]) for i in range(count)]
        self.behind = [(b, a) for a, b in self.ahead]
        self.count, self.half = count, count // 2
        self.taps, self.cut = taps, (taps + 1) // 2

    def send(self, messages):
        up, down = messages
        return lax.ppermute(up, "lon", self.ahead), lax.ppermute(down, "lon", self.behind)

    def first(self, terms, top):
        kernel = functools.partial(first_hop_kernel, self.cut, self.half)
        rows = [self.cut + 1, self.taps - self.cut + 1]
        return hop_call(kernel, rows, [terms, top], "first_hop")

    def next(self, left, messages, terms, top):
        cut = self.cut if left == self.half else self.taps
        kernel = functools.partial(next_hop_kernel, cut, left - 1, self.count - left + 1)
        return hop_call(kernel, [self.taps + 1] * 2, [*messages, terms, top], "next_hop")

    def last(self, messages, terms, top):
        return hop_call(last_hop_kernel, [self.taps + 1], [*messages, terms, top], "last_hop")[0]


class Chain:
    def __init__(self, ring, order, side, terms, top):
        self.ring, self.order, self.side = ring, order, side
        self.terms, self.top, self.left = terms, top, ring.half
        self.out = order(ring.first, terms, top)
        self.codes = []

    def arrive(self):
        self.out = self.order.pin(*self.ring.send(self.out))

    def hop(self):
        run = functools.partial(self.ring.next, self.left)
        self.out = self.order(run, self.out, self.terms, self.top)
        self.left -= 1

    def last(self):
        own = self.order(self.ring.last, self.out, self.terms, self.top)
        self.out = (own, own)
        self.keep(0, own)

    def keep(self, ahead, code):
        count = self.ring.count
        self.codes.append(
            ((ROWS_AT + ahead, ROWS_AT + count + 2 * ahead + self.side), code)
        )

    def take(self):
        taken, self.codes = self.codes, []
        return taken

    def move(self):
        ring, (up, down) = self.ring, self.out
        if self.left < ring.half:
            self.out = self.order.pin(*ring.send((up, down)))
            self.keep(ring.count - self.left, self.out[0])
            self.keep(self.left, self.out[1])
        else:
            cut = ring.cut
            parts = self.order.pin(*ring.send((up[:cut], down[cut:])))
            self.keep(ring.half, jnp.concatenate(parts, axis=0))
        self.left += 1


def make_table(lon, ch, count):
    place_x, place_core = ch // 2, ch % 2
    spot = ring_position(lon, count)
    owners = (spot + jnp.arange(count, dtype=jnp.int32)) % count
    sides = jnp.stack([place_x, 1 - place_x]) * (count // GROUP)
    return jnp.concatenate(
        [
            jnp.stack([spot, place_core, 3 - ch, ch ^ 2, ch ^ 1, ch]),
            owners % GROUP,
            (owners[:, None] // GROUP + sides[None]).reshape(-1),
        ]
    ).astype(jnp.int32)


def local(features, cotangent, weights):
    block, _, cols, rows = features.shape
    chans = cotangent.shape[1]
    total = weights.shape[4]
    count = lax.axis_size("lon")
    cells = cols * count * rows

    feat = jnp.transpose(features.reshape(block, cols, rows), (1, 0, 2))
    cot = jnp.transpose(cotangent.reshape(3, chans, cols, rows), (0, 2, 1, 3))
    order = Order()

    tails, heads = order(edges, cot)
    left = lax.ppermute(tails, "lon", [(i, (i + 1) % count) for i in range(count)])
    right = lax.ppermute(heads, "lon", [((i + 1) % count, i) for i in range(count)])

    to_core = [(i, i ^ 1) for i in range(4)]
    to_x = [(i, i ^ 2) for i in range(4)]
    feat = order.gate(feat)[0]
    far = lax.ppermute(feat, "ch", to_x)
    near = lax.ppermute(feat, "ch", to_core)

    norm = 1.0 / (REACH * cells**0.5)
    ring = Ring(count, 3 * TAPS)
    table = order(
        functools.partial(make_table, count=count), lax.axis_index("lon"), lax.axis_index("ch")
    )
    weight_rows = order(jnp.transpose, weights.reshape(-1, total))
    flat_near = order(flatten, table, feat, near)
    left, right, far = order.gate(left, right, far)
    grid = order(spread, cot, left, right, weight_rows)
    far_near = lax.ppermute(far, "ch", to_core)

    def terms_of(which, spans, *added):
        run = functools.partial(
            input_terms, BLOCKS_AT + which, block=block, spans=spans, rows=rows
        )
        return order(run, table, weight_rows, grid, *added)

    def features_with(flat):
        return order(functools.partial(kernel_terms, count=count), table, grid, flat)

    half = ring.half
    whole = (cols,)
    shape = (3 * TAPS, chans, total)
    written = []

    def write(*chains):
        taken = [item for chain in chains for item in chain.take()]
        places, codes = zip(*taken)
        run = functools.partial(unfold, places, norm, shape)
        written[:] = [order(run, table, list(codes), *written)]

    near = Chain(ring, order, 0, *features_with(flat_near))
    flat_far = order(flatten, table, far, far_near)
    (away,) = terms_of(0, whole)
    near.arrive()
    near.hop()
    away = lax.ppermute(order.gate(away)[0], "ch", to_core)
    far = Chain(ring, order, 1, *features_with(flat_far))
    (across,) = terms_of(1, whole, away)
    far.arrive()
    far.hop()
    near.arrive()
    near.hop()
    across = lax.ppermute(order.gate(across)[0], "ch", to_x)
    (beside,) = terms_of(2, whole)
    for _ in range(half - 4):
        far.arrive()
        far.hop()
        near.arrive()
        near.hop()
    far.arrive()
    far.hop()
    near.arrive()
    near.hop()
    far.arrive()
    far.hop()
    (mine,) = terms_of(3, whole)
    near.arrive()
    near.last()
    far.arrive()
    far.last()
    near.move()
    write(near)
    far.move()
    write(far)
    near.move()
    for _ in range(half - 4):
        far.move()
        near.move()
    far.move()
    write(near, far)
    near.move()
    across = order.pin(across)[0]
    far.move()
    beside = lax.ppermute(order.gate(beside)[0], "ch", to_core)
    write(near, far)
    input_grad = order(lambda *parts: sum(parts).astype(jnp.bfloat16), mine, beside, across)
    far.move()
    near.move()
    write(near, far)
    kernel_grad = written[0]

    input_grad = jnp.transpose(input_grad, (1, 0, 2)).reshape(block, 1, cols, rows)
    return (input_grad, kernel_grad.reshape(3, 3, 3, chans, total))


def solution(mesh):
    return jax.shard_map(
        local,
        mesh=mesh,
        in_specs=(
            P("ch", None, "lon", None),
            P(None, "ch", None, "lon", None),
            P(None, None, None, "ch", None),
        ),
        out_specs=(P("ch", None, "lon", None), P(None, None, None, "ch", None)),
        check_vma=False,
    )
```
